32 devices in a mesh: ctx: 8 (over y, x, core), fsdp: 4 (over z).
Axes of the slice: x: 2, y: 2, z: 4, core: 2. Of those that a mesh axis runs over, the one named last changes fastest.
Arguments:
- inputs: bfloat16 [4, 512, 2048], P('fsdp', 'ctx'), may hold values from -6 to 6
- cotangent: bfloat16 [4, 512, 2048], P('fsdp', 'ctx'), may hold values from -6 to 6
- doc_lengths: int32 [4, 3], replicated, may hold values from 1 to 480, as said below
- att_routes: int32 [512, 4, 2], P('ctx'), may hold values from 0 to 7, all different within a row; in each aligned block of 256 rows (0 to 255, 256 to 511, ..., all dimensions but the last counted through in order) at most 80 rows name the same one
- ffn_routes: int32 [512, 4, 2], P('ctx'), may hold values from 0 to 7, all different within a row; in each aligned block of 256 rows (0 to 255, 256 to 511, ..., all dimensions but the last counted through in order) at most 80 rows name the same one
- kv_weight: float32 [2048, 2, 2048], P('ctx', None, 'fsdp'), may hold values from -0.125 to 0.125
- query_weight: float32 [2048, 8, 2048], P('ctx', None, 'fsdp'), may hold values from -0.125 to 0.125
- output_weight: float32 [2048, 8, 2048], P('ctx', None, 'fsdp'), may hold values from -0.75 to 0.75
- att_router: float32 [2048, 8], P('ctx'), may hold values from -0.09375 to 0.09375
- att_gain: float32 [2048], P('ctx'), may hold values from 0.5 to 1.5
- gate_up_weight: float32 [2048, 8, 2, 5632], P('ctx', None, None, 'fsdp'), may hold values from -0.125 to 0.125
- down_weight: float32 [2048, 8, 5632], P('ctx', None, 'fsdp'), may hold values from -0.078125 to 0.078125
- ffn_router: float32 [2048, 8], P('ctx'), may hold values from -0.09375 to 0.09375
- ffn_gain: float32 [2048], P('ctx'), may hold values from 0.5 to 1.5
Outputs:
- outputs: bfloat16 [4, 512, 2048], P('fsdp', 'ctx')
- input_grad: bfloat16 [4, 512, 2048], P('fsdp', 'ctx')
- kv_grad: float32 [2048, 2, 2048], P('ctx', None, 'fsdp')
- query_grad: float32 [2048, 8, 2048], P('ctx', None, 'fsdp')
- output_grad: float32 [2048, 8, 2048], P('ctx', None, 'fsdp')
- att_router_grad: float32 [2048, 8], P('ctx')
- att_gain_grad: float32 [2048], P('ctx')
- gate_up_grad: float32 [2048, 8, 2, 5632], P('ctx', None, None, 'fsdp')
- down_grad: float32 [2048, 8, 5632], P('ctx', None, 'fsdp')
- ffn_router_grad: float32 [2048, 8], P('ctx')
- ffn_gain_grad: float32 [2048], P('ctx')
The draws below stay inside these ranges and needn't reach their ends.
Inputs may be any that keep to these rules, and one draw needn't show every extreme that they name: `doc_lengths`: each stream holds its 3 documents from position 0 on, in order, and the rest of its 512 positions is padding; every stream has at least one padding position; in every stream one document has exactly 480 positions. `att_routes`: the two experts of a position differ; within the rows of one device (aligned blocks of 256 rows, positions slowest) no expert is named by more than 80 rows. `ffn_routes`: the two experts of a position differ; within the rows of one device (aligned blocks of 256 rows, positions slowest) no expert is named by more than 80 rows.
All inputs are finite; a program needn't handle non-finite values.
Results may differ from the reference program's by a relative error of at most 0.025.
Values may be sent and summed in bfloat16 or wider, within the bound.
No kernel may reach another device: no remote copies, remote signals or barrier semaphores. Data moves between devices by JAX's collectives and lax.ppermute only.
A program may use at most 576 MiB of HBM per device.

```python
import math
import jax
import jax.numpy as jnp
import numpy as np
from jax import lax

D = 2048
HEADS = 16
HD = 128
E_A = 8
E_F = 8
FF = 5632
DOCS = 3
TOK_DEV = 64
STREAMS = 4
SEQ = 512
CAP_A = 80
CAP_F = 80
N_CTX = 8


def draw_doc_lengths(key, part):
    key = jax.random.fold_in(key, 11)
    short_key, place_key = jax.random.split(key, 2)
    short_top = max(2, TOK_DEV // 4)
    shorter = jax.random.randint(short_key, (STREAMS, 2), 1, short_top)
    longest = jnp.full((STREAMS, 1), SEQ - TOK_DEV // 2, jnp.int32)
    long_slot = jax.random.randint(place_key, (STREAMS, 1), 0, DOCS)
    columns = jnp.arange(DOCS, dtype=jnp.int32)[None, :]
    short_rank = jnp.clip(columns - (columns > long_slot).astype(jnp.int32), 0, 1)
    short_pick = jnp.where(short_rank == 0, shorter[:, 0:1], shorter[:, 1:2])
    return jnp.where(columns == long_slot, longest, short_pick).astype(jnp.int32)


def steps_of(rng, extent, cuts, smallest, high):
    def one(position, blocks):
        heights = jax.random.uniform(jax.random.fold_in(jax.random.fold_in(rng, 6), position), (blocks,), jnp.float32, smallest / len(cuts), high / len(cuts))
        return jnp.repeat(jnp.exp(heights), extent[position] // blocks).reshape((-1,) + (1,) * (len(extent) - position - 1))

    level = one(*cuts[0])
    for cut in cuts[1:]:
        level = level * one(*cut)
    return level


def assign_block(stream_key, own, number, rows, number_of, top, bound, lean):
    sequence = jax.random.permutation(stream_key, number_of)
    heavy_load, common = portions_of(number_of, rows * top, bound, lean, True), portions_of(number_of, rows * top, bound, lean, False)
    places = jnp.arange(number_of)

    def named(lengths, turn):
        used = int((lengths > 0).sum())
        fixed = max(1, used // 4)
        moved = fixed + (places - fixed + turn * (used - fixed)) % max(1, number_of - fixed)
        return jnp.zeros((number_of,), jnp.int32).at[sequence[jnp.where(places < fixed, places, moved)]].set(jnp.asarray(lengths, jnp.int32))

    lengths = jnp.where(number % 4 == 0, named(heavy_load, number // 4), named(common, number - number // 4 - 1))
    mixed = jax.random.permutation(jax.random.fold_in(own, 3), number_of)
    giver, sink = mixed[0:number_of // 2 * 2:2], mixed[1:number_of // 2 * 2:2]
    slack = jnp.minimum(lengths[giver] - 1, bound - lengths[sink]) // 2
    slack = jnp.where((giver == sequence[0]) | (sink == sequence[0]) | (lengths[sink] == 0), 0, jnp.maximum(slack, 0))
    moved = jax.random.randint(jax.random.fold_in(own, 4), (number_of // 2,), 0, 1 << 20) % (slack + 1)
    lengths = lengths.at[giver].add(-moved).at[sink].add(moved)
    items = jnp.searchsorted(jnp.cumsum(lengths), jnp.arange(rows * top), side="right").astype(jnp.int32)
    grid = items.reshape(top, rows).T
    grid = grid[jax.random.permutation(jax.random.fold_in(own, 1), rows)]
    turn = jax.random.randint(jax.random.fold_in(own, 2), (rows, 1), 0, top)
    return jnp.take_along_axis(grid, (jnp.arange(top)[None, :] + turn) % top, axis=1)


def portions_of(amount, total, limit, skew, full):
    loads = [(1 << 20) // math.isqrt(grade ** skew) + 1 for grade in range(1, amount + 1)]
    largest = limit if full else min(limit, max(-(-total // amount), total * loads[0] // sum(loads)))
    least = 1 if total - largest >= amount - 1 else 0
    holding, surplus = [largest] + [least] * (amount - 1), total - largest - least * (amount - 1)
    while surplus > 0:
        free = [i for i in range(1, amount) if holding[i] < largest] or [i for i in range(1, amount) if holding[i] < limit]
        mass, budget = sum([loads[i] for i in free]), surplus
        for i in free:
            more = min(limit - holding[i], max(1, budget * loads[i] // mass), surplus)
            holding[i] = holding[i] + more
            surplus = surplus - more
    return np.array(holding)


def gaussian(stream_key, shape, scale, reach, cuts=(), kind=jnp.bfloat16):
    array = scale * jax.random.normal(stream_key, shape, jnp.float32)
    if cuts:
        array = array * steps_of(stream_key, shape, cuts, -0.22, 0.18)
    return jnp.clip(array, -reach, reach).astype(kind)


def setup_inputs(seed: int = 0) -> dict:
    key_list = jax.random.split(jax.random.key(seed), 15)
    inputs = gaussian(key_list[0], (STREAMS, SEQ, D), 1.0, 6.0, ((0, 4), (1, 8)))
    cotangent = gaussian(key_list[1], (STREAMS, SEQ, D), 1.0, 6.0, ((0, 4), (1, 8)))
    doc_lengths = draw_doc_lengths(jax.random.fold_in(key_list[14], 71), 0)
    att_routes_keys = jax.random.split(jax.random.fold_in(key_list[3], 1), SEQ * STREAMS // (TOK_DEV * STREAMS))
    att_routes_turns = jax.random.permutation(jax.random.fold_in(key_list[3], 3), SEQ * STREAMS // (TOK_DEV * STREAMS))
    att_routes = jax.vmap(lambda own, number: assign_block(jax.random.fold_in(key_list[3], 2), own, number, TOK_DEV * STREAMS, E_A, 2, CAP_A, 1))(att_routes_keys, att_routes_turns).reshape((SEQ, STREAMS, 2))
    ffn_routes_keys = jax.random.split(jax.random.fold_in(key_list[4], 1), SEQ * STREAMS // (TOK_DEV * STREAMS))
    ffn_routes_turns = jax.random.permutation(jax.random.fold_in(key_list[4], 3), SEQ * STREAMS // (TOK_DEV * STREAMS))
    ffn_routes = jax.vmap(lambda own, number: assign_block(jax.random.fold_in(key_list[4], 2), own, number, TOK_DEV * STREAMS, E_F, 2, CAP_F, 1))(ffn_routes_keys, ffn_routes_turns).reshape((SEQ, STREAMS, 2))
    kv_weight = gaussian(key_list[5], (D, 2, HEADS * HD), D ** -0.5, 0.125, ((0, 8), (2, 4)), jnp.float32)
    query_weight = gaussian(key_list[6], (D, E_A, HEADS * HD), D ** -0.5, 0.125, ((0, 8), (2, 4)), jnp.float32)
    output_weight = gaussian(key_list[7], (D, E_A, HEADS * HD), (HEADS * HD // 32) ** -0.5, 0.75, ((0, 8), (2, 4)), jnp.float32)
    att_router = gaussian(key_list[8], (D, E_A), (2 * D) ** -0.5, 0.09375, ((0, 8),), jnp.float32)
    att_gain = jnp.clip(1.0 + 0.1 * jax.random.normal(key_list[9], (D,), jnp.float32), 0.5, 1.5)
    gate_up_weight = gaussian(key_list[10], (D, E_F, 2, FF), D ** -0.5, 0.125, ((0, 8), (3, 4)), jnp.float32)
    down_weight = gaussian(key_list[11], (D, E_F, FF), FF ** -0.5, 0.078125, ((0, 8), (2, 4)), jnp.float32)
    ffn_router = gaussian(key_list[12], (D, E_F), (2 * D) ** -0.5, 0.09375, ((0, 8),), jnp.float32)
    ffn_gain = jnp.clip(1.0 + 0.1 * jax.random.normal(key_list[13], (D,), jnp.float32), 0.5, 1.5)
    return {"inputs": inputs, "cotangent": cotangent, "doc_lengths": doc_lengths, "att_routes": att_routes, "ffn_routes": ffn_routes, "kv_weight": kv_weight, "query_weight": query_weight, "output_weight": output_weight, "att_router": att_router, "att_gain": att_gain, "gate_up_weight": gate_up_weight, "down_weight": down_weight, "ffn_router": ffn_router, "ffn_gain": ffn_gain}


@jax.custom_vjp
def low(v):
    return lax.optimization_barrier(v.astype(jnp.bfloat16)).astype(jnp.float32)

@jax.custom_vjp
def low_back(v):
    return v

def low_keep(v):
    return (low(v), None)

def low_pass(kept, grad):
    return (grad,)

def back_keep(v):
    return (v, None)

def back_low(kept, grad):
    return (low(grad),)
low.defvjp(low_keep, low_pass)
low_back.defvjp(back_keep, back_low)
norm_eps = 1e-06
rope_base = 10000.0
masked_score = -1e+30
HIGHEST = lax.Precision.HIGHEST

def doc_layout(doc_lengths, seq_len):
    doc_ends = jnp.cumsum(doc_lengths, axis=1)
    starts = doc_ends - doc_lengths
    positions = jnp.arange(seq_len, dtype=jnp.int32)
    doc_index = lax.optimization_barrier(jnp.sum((positions[None, :, None] >= doc_ends[:, None, :]).astype(jnp.int32), axis=2))
    labels = jnp.arange(doc_lengths.shape[1], dtype=jnp.int32)
    doc_start = lax.optimization_barrier(jnp.sum(jnp.where(doc_index[:, :, None] == labels[None, None, :], starts[:, None, :], 0), axis=2))
    return (doc_index, positions[None, :] - doc_start)

def rope_tables(doc_place, head_dim):
    halves = jnp.arange(head_dim // 2, dtype=jnp.float32)
    inverse_freq = rope_base ** (-2.0 * halves / head_dim)
    angles = doc_place.astype(jnp.float32)[..., None] * inverse_freq
    return (jnp.cos(angles), jnp.sin(angles))

def rotate(values, cos_part, sin_part):
    half_dim = values.shape[-1] // 2
    first_half = values[..., :half_dim]
    second_half = values[..., half_dim:]
    return jnp.concatenate((first_half * cos_part - second_half * sin_part, second_half * cos_part + first_half * sin_part), axis=-1)

def expert_table(route_rows, experts, capacity):
    row_count = route_rows.shape[0]
    flat_routes = route_rows.reshape(-1)
    labels = jnp.arange(experts, dtype=jnp.int32)
    onehot = (flat_routes[:, None] == labels[None, :]).astype(jnp.int32)
    slot_of = lax.optimization_barrier(jnp.sum((jnp.cumsum(onehot, axis=0) - 1) * onehot, axis=1))
    slot_table = jnp.full((experts, capacity), 2 * row_count, jnp.int32)
    return slot_table.at[flat_routes, slot_of].set(jnp.arange(2 * row_count, dtype=jnp.int32))

def put_slots(values, slot_table, slot_total):
    feature = values.shape[-1]
    holder = jnp.zeros((slot_total + 1, feature), values.dtype)
    return holder.at[slot_table.reshape(-1)].set(values.reshape(-1, feature))[:slot_total]

def rms_scale(values, gain_row):
    return values * lax.rsqrt(lax.optimization_barrier(jnp.mean(values * values, axis=-1, keepdims=True)) + norm_eps) * gain_row

def attend_stream(stream_args):
    query_all, key_all, value_all, doc_row = stream_args
    block_rows = math.gcd(SEQ, 512)
    positions = jnp.arange(SEQ, dtype=jnp.int32)
    score_scale = HD ** (-0.5)

    def one_block(block_id):
        query_part = lax.dynamic_slice_in_dim(query_all, block_id * block_rows, block_rows, 0)
        doc_part = lax.dynamic_slice_in_dim(doc_row, block_id * block_rows, block_rows, 0)
        pos_part = block_id * block_rows + jnp.arange(block_rows, dtype=jnp.int32)
        scores = low_back(score_scale * jnp.einsum('tshd,uhd->htsu', query_part, key_all, precision=HIGHEST))
        allowed = (doc_part[:, None] == doc_row[None, :]) & (positions[None, :] <= pos_part[:, None]) & (doc_part[:, None] < DOCS)
        allowed = allowed[None, :, None, :]
        masked = jnp.where(allowed, scores, masked_score)
        row_max = lax.optimization_barrier(jnp.max(masked, axis=3, keepdims=True))
        probs = jnp.where(allowed, jnp.exp(masked - row_max), 0.0)
        row_sum = lax.optimization_barrier(jnp.sum(probs, axis=3))
        weighted = jnp.einsum('htsu,uhd->tshd', low(probs), value_all, precision=HIGHEST)
        row_norm = jnp.where(row_sum > 0, row_sum, 1.0)
        keep_part = (doc_part < DOCS).astype(jnp.float32)
        return weighted / jnp.transpose(row_norm, (1, 2, 0))[..., None] * keep_part[:, None, None, None]
    blocks_out = lax.map(jax.checkpoint(one_block), jnp.arange(SEQ // block_rows, dtype=jnp.int32))
    return blocks_out.reshape(SEQ, 2, HEADS, HD)

def reference(inputs, cotangent, doc_lengths, att_routes, ffn_routes, kv_weight, query_weight, output_weight, att_router, att_gain, gate_up_weight, down_weight, ffn_router, ffn_gain):
    row_count = STREAMS * SEQ
    doc_index, doc_place = doc_layout(doc_lengths, SEQ)
    keep_rows = (doc_index < DOCS).astype(jnp.float32).reshape(row_count, 1)
    cos_part, sin_part = rope_tables(doc_place.reshape(row_count), HD)
    att_rows = jnp.transpose(att_routes, (1, 0, 2)).reshape(row_count, 2)
    ffn_rows = jnp.transpose(ffn_routes, (1, 0, 2)).reshape(row_count, 2)
    att_table = expert_table(att_rows, E_A, CAP_A * N_CTX)
    ffn_table = expert_table(ffn_rows, E_F, CAP_F * N_CTX)
    att_hot = (att_rows[:, :, None] == jnp.arange(E_A, dtype=jnp.int32)[None, None, :]).astype(jnp.float32)
    ffn_hot = (ffn_rows[:, :, None] == jnp.arange(E_F, dtype=jnp.int32)[None, None, :]).astype(jnp.float32)

    def forward(x_rows, kv_master, query_master, output_master, att_router_master, att_gain_master, gate_up_master, down_master, ffn_router_master, ffn_gain_master):
        att_hidden = low(rms_scale(x_rows, low(att_gain_master)))
        att_logits = low_back(jnp.dot(att_hidden, low(att_router_master), precision=HIGHEST, preferred_element_type=jnp.float32))
        att_gates = jax.nn.softmax(lax.optimization_barrier(jnp.sum(att_hot * att_logits[:, None, :], axis=2)), axis=1)
        kv_proj = jnp.einsum('rd,dkf->rkf', att_hidden, low(kv_master), precision=HIGHEST)
        key_pre = low_back(kv_proj[:, 0].reshape(row_count, HEADS, HD))
        key_low = low(low_back(rotate(key_pre, cos_part[:, None], sin_part[:, None])))
        value_low = low(low_back(kv_proj[:, 1].reshape(row_count, HEADS, HD)))
        att_padded = jnp.concatenate((att_hidden, jnp.zeros((1, D), jnp.float32)), axis=0)
        query_in = att_padded[att_table // 2]
        query_expert = jnp.einsum('ecd,def->ecf', query_in, low(query_master), precision=HIGHEST)
        query_pre = low_back(put_slots(query_expert, att_table, 2 * row_count).reshape(row_count, 2, HEADS, HD))
        query_low = low(low_back(rotate(query_pre, cos_part[:, None, None], sin_part[:, None, None])))
        att_core = lax.map(jax.checkpoint(attend_stream), (query_low.reshape(STREAMS, SEQ, 2, HEADS, HD), key_low.reshape(STREAMS, SEQ, HEADS, HD), value_low.reshape(STREAMS, SEQ, HEADS, HD), doc_index))
        att_flat = low(low_back(att_core.reshape(2 * row_count, HEADS * HD)))
        out_in = jnp.concatenate((att_flat, jnp.zeros((1, HEADS * HD), jnp.float32)), axis=0)[att_table]
        out_expert = low_back(jnp.einsum('ecf,def->ecd', out_in, low(output_master), precision=HIGHEST))
        out_slots = put_slots(out_expert, att_table, 2 * row_count).reshape(row_count, 2, D)
        residual = x_rows + lax.optimization_barrier(jnp.sum(att_gates[:, :, None] * out_slots, axis=1))
        ffn_hidden = low(rms_scale(residual, low(ffn_gain_master)))
        ffn_logits = low_back(jnp.dot(ffn_hidden, low(ffn_router_master), precision=HIGHEST, preferred_element_type=jnp.float32))
        ffn_gates = jax.nn.softmax(lax.optimization_barrier(jnp.sum(ffn_hot * ffn_logits[:, None, :], axis=2)), axis=1)
        ffn_padded = jnp.concatenate((ffn_hidden, jnp.zeros((1, D), jnp.float32)), axis=0)

        def one_expert(expert_args):
            table_row, gate_up_part, down_part = expert_args
            expert_in = ffn_padded[table_row // 2]
            gate_up = low_back(jnp.einsum('cd,djf->cjf', expert_in, gate_up_part, precision=HIGHEST))
            activated = low(jax.nn.silu(gate_up[:, 0]) * gate_up[:, 1])
            return low_back(jnp.einsum('cf,df->cd', activated, down_part, precision=HIGHEST))
        ffn_expert = lax.map(jax.checkpoint(one_expert), (ffn_table, jnp.transpose(low(gate_up_master), (1, 0, 2, 3)), jnp.transpose(low(down_master), (1, 0, 2))))
        ffn_slots = put_slots(ffn_expert, ffn_table, 2 * row_count).reshape(row_count, 2, D)
        final_rows = residual + lax.optimization_barrier(jnp.sum(ffn_gates[:, :, None] * ffn_slots, axis=1))
        return final_rows.reshape(STREAMS, SEQ, D)
    x_rows = inputs.astype(jnp.float32).reshape(row_count, D)
    final, pullback = jax.vjp(forward, x_rows, kv_weight, query_weight, output_weight, att_router, att_gain, gate_up_weight, down_weight, ffn_router, ffn_gain)
    grads = pullback(cotangent.astype(jnp.float32) * keep_rows.reshape(STREAMS, SEQ, 1))
    return (final.astype(jnp.bfloat16), grads[0].reshape(STREAMS, SEQ, D).astype(jnp.bfloat16), grads[1], grads[2], grads[3], grads[4], grads[5], grads[6], grads[7], grads[8], grads[9])
```

```python
import functools

import jax
import jax.numpy as jnp
from jax import lax
from jax.experimental import pallas as pl
from jax.experimental.pallas import tpu as pltpu
from jax.sharding import PartitionSpec as P

D = 2048
HEADS = 16
HD = 128
E_A = 8
E_F = 8
FF = 5632
DOCS = 3

norm_eps = 1e-06
rope_base = 10000.0
masked_score = -1e30

BF = jnp.bfloat16
F32 = jnp.float32
VMEM_CAP = 60 * 1024 * 1024


def dot(a, b):
    return lax.dot_general(a, b, (((1,), (0,)), ((), ())), preferred_element_type=F32)


def dot_nt(a, b):
    return lax.dot_general(a, b, (((1,), (1,)), ((), ())), preferred_element_type=F32)


def dot_tn(a, b):
    return lax.dot_general(a, b, (((0,), (0,)), ((), ())), preferred_element_type=F32)


def spec(shape, index=None):
    if index is not None:
        return pl.BlockSpec(shape, index)
    zeros = (0,) * len(shape)
    return pl.BlockSpec(shape, lambda *_: zeros, pipeline_mode=pl.Buffered(1))


def call(body, sc, grid, in_specs, out_specs, out_shape, scratch=(), aliases=None, flops=0, size=0):
    return functools.partial(
        pl.pallas_call(
            body,
            out_shape=out_shape,
            grid_spec=pltpu.PrefetchScalarGridSpec(
                num_scalar_prefetch=1,
                grid=grid,
                in_specs=in_specs,
                out_specs=jax.tree.map(
                    lambda s: pl.BlockSpec(s.block_shape, s.index_map), out_specs
                ),
                scratch_shapes=list(scratch),
            ),
            input_output_aliases=aliases or {},
            compiler_params=pltpu.CompilerParams(
                dimension_semantics=("arbitrary",) * len(grid), vmem_limit_bytes=VMEM_CAP
            ),
            cost_estimate=pl.CostEstimate(flops=flops, bytes_accessed=size, transcendentals=0),
        ),
        sc,
    )


def proj_body(n_extra, width, sc, route, xo, xt, *refs):
    wm, wt = refs[0], refs[1]
    out = refs[-1]
    a, b = xo[...], xt[...]
    r0, r1 = route[:, 0:1], route[:, 1:2]
    acc0 = jnp.zeros((a.shape[0], width), F32)
    acc1 = acc0
    for e in range(E_A):
        r = dot(a, wm[e]) + dot(b, wt[e])
        acc0 = jnp.where(r0 == e, r, acc0)
        acc1 = jnp.where(r1 == e, r, acc1)
    out[:, 0:width] = acc0.astype(BF)
    out[:, width : 2 * width] = acc1.astype(BF)
    if n_extra:
        km, kt = refs[2], refs[3]
        for i in range(n_extra):
            out[:, (2 + i) * width : (3 + i) * width] = (dot(a, km[i]) + dot(b, kt[i])).astype(BF)


def rotate(u, cosf, sinf):
    return u * cosf + pltpu.roll(u, HD // 2, 1) * sinf


def unrotate(u, cosf, sinf):
    return u * cosf - pltpu.roll(u, HD // 2, 1) * sinf


def add_halves(refs):
    a0, a1, b0, b1 = refs
    top = a0[...].astype(F32) + a1[...].astype(F32)
    low = b0[...].astype(F32) + b1[...].astype(F32)
    return jnp.concatenate((top, low), axis=0)


def allowed_pairs(doc_col, doc_row):
    n = doc_col.shape[0]
    t = lax.broadcasted_iota(jnp.int32, (n, n), 0)
    u = lax.broadcasted_iota(jnp.int32, (n, n), 1)
    return (doc_col[...] == doc_row[...]) & (u <= t) & (doc_col[...] < DOCS)


def attend_body(hc, sc, a0, a1, b0, b1, doc_col, doc_row, cosr, sinr, qkv, out, lse):
    width = hc * HD
    u = add_halves((a0, a1, b0, b1))
    cosf, sinf = cosr[...], sinr[...]
    ok = allowed_pairs(doc_col, doc_row)
    for h in range(hc):
        at = 2 * width + h * HD
        k = rotate(u[:, at : at + HD], cosf, sinf).astype(BF)
        v = u[:, at + width : at + width + HD].astype(BF)
        qkv[:, at : at + HD] = k
        qkv[:, at + width : at + width + HD] = v
        for j in range(2):
            lo = j * width + h * HD
            q = rotate(u[:, lo : lo + HD], cosf, sinf).astype(BF)
            qkv[:, lo : lo + HD] = q
            s = jnp.where(ok, dot_nt(q, k) * (HD**-0.5), masked_score)
            m = jnp.max(s, axis=1, keepdims=True)
            p = jnp.where(ok, jnp.exp(s - m), 0.0)
            total = jnp.sum(p, axis=1, keepdims=True)
            total = jnp.where(total > 0, total, 1.0)
            out[:, lo : lo + HD] = (dot(p.astype(BF), v) / total).astype(BF)
            lse[:, 2 * h + j : 2 * h + j + 1] = m + jnp.log(total)


def attend_back_body(hc, sc, a0, a1, b0, b1, qkv, att, lse, gates, doc_col, doc_row, cosr, sinr, grads, dgate):
    width = hc * HD
    u = add_halves((a0, a1, b0, b1))
    cosf, sinf = cosr[...], sinr[...]
    ok = allowed_pairs(doc_col, doc_row)
    keep = (doc_col[...] < DOCS).astype(F32)
    dg = [jnp.zeros((u.shape[0], 1), F32) for _ in range(2)]
    for h in range(hc):
        at = 2 * width + h * HD
        k = qkv[:, at : at + HD]
        v = qkv[:, at + width : at + width + HD]
        dk = jnp.zeros((u.shape[0], HD), F32)
        dv = dk
        for j in range(2):
            lo = j * width + h * HD
            q = qkv[:, lo : lo + HD]
            o = att[:, lo : lo + HD].astype(F32)
            raw = u[:, lo : lo + HD]
            dg[j] = dg[j] + jnp.sum(raw * o, axis=1, keepdims=True)
            do = (raw * (gates[:, j : j + 1] * keep)).astype(BF)
            delta = jnp.sum(do.astype(F32) * o, axis=1, keepdims=True)
            s = dot_nt(q, k) * (HD**-0.5)
            p = jnp.where(ok, jnp.exp(s - lse[:, 2 * h + j : 2 * h + j + 1]), 0.0)
            ds = (p * (dot_nt(do, v) - delta)).astype(BF)
            dq = dot(ds, k) * (HD**-0.5)
            grads[:, lo : lo + HD] = unrotate(dq, cosf, sinf).astype(BF)
            dk = dk + dot_tn(ds, q)
            dv = dv + dot_tn(p.astype(BF), do)
        grads[:, at : at + HD] = unrotate(dk * (HD**-0.5), cosf, sinf).astype(BF)
        grads[:, at + width : at + width + HD] = dv.astype(BF)
    dgate[...] = jnp.zeros_like(dgate)
    dgate[:, 0:1] = dg[0]
    dgate[:, 1:2] = dg[1]


def chosen(route, vals, lo, width, e, scale=None):
    a = vals[:, lo : lo + width].astype(F32)
    b = vals[:, lo + width : lo + 2 * width].astype(F32)
    s0 = scale[:, 0:1] if scale is not None else 1.0
    s1 = scale[:, 1:2] if scale is not None else 1.0
    w0 = jnp.where(route[:, 0:1] == e, s0, 0.0)
    w1 = jnp.where(route[:, 1:2] == e, s1, 0.0)
    return (a * w0 + b * w1).astype(BF)


def att_out_body(width, sc, route, gates, om, ot, wm, wt, prev, out):
    acc = jnp.zeros(out.shape[1:], F32)
    for e in range(E_A):
        acc += dot_nt(chosen(route, om, 0, width, e, gates), wm[e])
        acc += dot_nt(chosen(route, ot, 0, width, e, gates), wt[e])
    out[0] = acc.astype(BF)


def att_in_back_body(width, sc, route, gm, gt, wm, wt, km, kt, prev, out):
    acc = jnp.zeros(out.shape[1:], F32)
    for e in range(E_A):
        acc += dot_nt(chosen(route, gm, 0, width, e), wm[e])
        acc += dot_nt(chosen(route, gt, 0, width, e), wt[e])
    for i in range(2):
        lo = (2 + i) * width
        acc += dot_nt(gm[:, lo : lo + width], km[i]) + dot_nt(gt[:, lo : lo + width], kt[i])
    out[0] = acc.astype(BF)


def att_weight_body(width, n, gated, extra, sc, *refs):
    xt, route, gates = refs[0], refs[1], refs[2]
    pieces = refs[3 : 3 + 2 * n]
    out = refs[3 + 2 * n]
    out2 = refs[4 + 2 * n] if extra else None
    half = pl.program_id(0)
    e = pl.program_id(1)
    for side in range(2):

        @pl.when(half == side)
        def _():
            acc = jnp.zeros((xt.shape[1], width), F32)
            for k in range(n):
                s = sc[k]
                sel = chosen(route[s], pieces[2 * k + side], 0, width, e, gates[s] if gated else None)
                acc += dot(xt[s], sel)
            out[0] = acc
            if extra:

                @pl.when(e < 2)
                def _():
                    acc = jnp.zeros((xt.shape[1], width), F32)
                    for k in range(n):
                        vals = pieces[2 * k + side]
                        both = [vals[:, (2 + i) * width : (3 + i) * width] for i in range(2)]
                        acc += dot(xt[sc[k]], jnp.where(e == 0, both[0].astype(F32), both[1].astype(F32)).astype(BF))
                    out2[0] = acc


def row_chunks(rows):
    step = min(rows, 1024)
    return [(i, step) for i in range(0, rows, step)]


def group_proj_body(sc, pos, xo, xt, wm, wt, out, xs):
    i = pl.program_id(0)
    ts = out.shape[0]
    dc = xo.shape[1]
    p0, first, last = sc[0], sc[1], sc[2]

    @pl.when(i == 0)
    def _():
        a = jnp.zeros((ts, dc), F32)
        b = a
        for lo, n in row_chunks(xo.shape[0]):
            ids = p0 + lax.broadcasted_iota(jnp.int32, (ts, n), 0)
            hot = (pos[0:1, lo : lo + n] == ids) | (pos[1:2, lo : lo + n] == ids)
            hot = jnp.where(hot, 1.0, 0.0).astype(BF)
            a = a + dot(hot, xo[lo : lo + n, :])
            b = b + dot(hot, xt[lo : lo + n, :])
        xs[:, 0:dc] = a.astype(BF)
        xs[:, dc : 2 * dc] = b.astype(BF)
        out[...] = (dot(xs[:, 0:dc], wm[0]) + dot(xs[:, dc : 2 * dc], wt[0])).astype(BF)

    e = jnp.minimum(first + i, last)

    @pl.when((i > 0) & (first + i <= last))
    def _():
        rows = p0 + lax.broadcasted_iota(jnp.int32, (ts, 1), 0)
        r = dot(xs[:, 0:dc], wm[0]) + dot(xs[:, dc : 2 * dc], wt[0])
        out[...] = jnp.where(rows >= sc[3 + e], r, out[...].astype(F32)).astype(BF)


def middle_body(fl, sc, pos, rowv, g0, g1, d0, d1, dgu, act, tok):
    ts = g0.shape[0]
    rows = pos.shape[1]
    p0 = sc[0]
    inv = jnp.zeros((ts, 1), F32)
    gate = inv
    for lo, n in row_chunks(rows):
        ids = p0 + lax.broadcasted_iota(jnp.int32, (ts, n), 0)
        is0 = jnp.where(pos[0:1, lo : lo + n] == ids, 1.0, 0.0)
        is1 = jnp.where(pos[1:2, lo : lo + n] == ids, 1.0, 0.0)
        inv += jnp.sum((is0 + is1) * rowv[0:1, lo : lo + n], axis=1, keepdims=True)
        gate += jnp.sum(is0 * rowv[1:2, lo : lo + n] + is1 * rowv[2:3, lo : lo + n], axis=1, keepdims=True)
    dpf = jnp.zeros((ts, 1), F32)
    dn = dpf
    step = 128
    for lo in range(0, fl, step):
        gt = (g0[:, lo : lo + step].astype(F32) + g1[:, lo : lo + step].astype(F32)) * inv
        up = (g0[:, fl + lo : fl + lo + step].astype(F32) + g1[:, fl + lo : fl + lo + step].astype(F32)) * inv
        raw = d0[:, lo : lo + step].astype(F32) + d1[:, lo : lo + step].astype(F32)
        sg = 1.0 / (1.0 + jnp.exp(-gt))
        silu = gt * sg
        a = (silu * up).astype(BF)
        act[:, lo : lo + step] = a
        da = raw * gate
        dgt = da * up * (sg * (1.0 + gt * (1.0 - sg)))
        dup = da * silu
        dgu[:, lo : lo + step] = dgt.astype(BF)
        dgu[:, fl + lo : fl + lo + step] = dup.astype(BF)
        dpf += jnp.sum(raw * a.astype(F32), axis=1, keepdims=True)
        dn += jnp.sum(dgt * gt + dup * up, axis=1, keepdims=True)
    for lo, n in row_chunks(rows):
        ids = p0 + lax.broadcasted_iota(jnp.int32, (ts, n), 0)
        is0 = jnp.where(pos[0:1, lo : lo + n] == ids, 1.0, 0.0)
        is1 = jnp.where(pos[1:2, lo : lo + n] == ids, 1.0, 0.0)
        t0 = jnp.sum(is0 * dpf, axis=0, keepdims=True)
        t1 = jnp.sum(is1 * dpf, axis=0, keepdims=True)
        t2 = jnp.sum((is0 + is1) * dn, axis=0, keepdims=True)
        tok[:, lo : lo + n] = jnp.concatenate((t0, t1, t2, jnp.zeros((5, n), F32)), axis=0)


def group_back_body(sc, posc, wcol, d, w, prev, out, dh):
    i = pl.program_id(0)
    ts = d.shape[0]
    p0, first, last = sc[0], sc[1], sc[2]
    e = jnp.minimum(first + i, last)

    @pl.when(i == 0)
    def _():
        dh[...] = dot_nt(d[...], w[0])

    @pl.when((i > 0) & (first + i <= last))
    def _():
        rows = p0 + lax.broadcasted_iota(jnp.int32, (ts, 1), 0)
        dh[...] = jnp.where(rows >= sc[3 + e], dot_nt(d[...], w[0]), dh[...])

    @pl.when(i == pl.num_programs(0) - 1)
    def _():
        vals = dh[...].astype(BF)
        for lo, n in row_chunks(out.shape[0]):
            ids = p0 + lax.broadcasted_iota(jnp.int32, (n, ts), 1)
            hot = jnp.where(posc[lo : lo + n, 0:1] == ids, wcol[lo : lo + n, 0:1], 0.0)
            hot = hot + jnp.where(posc[lo : lo + n, 1:2] == ids, wcol[lo : lo + n, 1:2], 0.0)
            out[lo : lo + n, :] = prev[lo : lo + n, :] + dot(hot.astype(BF), vals)


def sort_t_body(sc, posc, wcol, xt, out):
    p0 = sc[pl.program_id(0)]
    ts = out.shape[1]
    acc = jnp.zeros(out.shape, F32)
    for lo, n in row_chunks(xt.shape[1]):
        ids = p0 + lax.broadcasted_iota(jnp.int32, (n, ts), 1)
        hot = jnp.where(posc[lo : lo + n, 0:1] == ids, wcol[lo : lo + n, 0:1], 0.0)
        hot = hot + jnp.where(posc[lo : lo + n, 1:2] == ids, wcol[lo : lo + n, 1:2], 0.0)
        acc += dot(xt[:, lo : lo + n], hot.astype(BF))
    out[...] = acc.astype(BF)


def group_weight_body(n, sc, xs, *refs):
    pieces, out = refs[:n], refs[n]
    ts = pieces[0].shape[0]
    e = pl.program_id(1)
    lo, hi = sc[n + e], sc[n + e + 1]
    out[...] = jnp.zeros_like(out)
    for i in range(n):
        p0 = sc[i]

        @pl.when((p0 < hi) & (p0 + ts > lo))
        def _():
            ids = p0 + lax.broadcasted_iota(jnp.int32, (1, ts), 1)
            ok = jnp.where((ids >= lo) & (ids < hi), 1.0, 0.0).astype(BF)
            out[0] += dot(xs[:, i * ts : (i + 1) * ts] * ok, pieces[i][...])


def per_device(
    inputs,
    cotangent,
    doc_lengths,
    att_routes,
    ffn_routes,
    kv_weight,
    query_weight,
    output_weight,
    att_router,
    att_gain,
    gate_up_weight,
    down_weight,
    ffn_router,
    ffn_gain,
):
    n_ctx = lax.axis_size("ctx")
    n_z = lax.axis_size("fsdp")
    c = lax.axis_index("ctx")
    f = lax.axis_index("fsdp")
    n_chip = n_ctx // 2
    chip, core = c // 2, c % 2
    tok = inputs.shape[1]
    seq = tok * n_ctx
    dc = D // n_ctx
    rows = n_z * seq
    hc = HEADS // n_z // 2
    width = hc * HD
    half = seq // 2
    fl_real = FF // n_z
    fl = -(-fl_real // 128) * 128
    ts = 2 * rows // n_ctx // 2
    assert n_chip == n_z

    def swap(x, axis, k, n):
        return lax.ppermute(x, axis, [(i, i ^ k) for i in range(n)])

    def core_swap(x):
        return swap(x, "ctx", 1, n_ctx)

    def chip_swap(x, k):
        return swap(x, "ctx", 2 * k, n_ctx)

    def z_swap(x, k):
        return swap(x, "fsdp", k, n_z)

    chip_bits = [1 << i for i in range(n_chip.bit_length() - 1)]
    z_bits = [1 << i for i in range(n_z.bit_length() - 1)]

    def z_gather(x):
        return [x] + [z_swap(x, k) for k in range(1, n_z)]

    def z_reduce(pieces):
        total = pieces[0].astype(F32)
        for k in range(1, n_z):
            total = total + z_swap(pieces[k], k).astype(F32)
        return total

    def small_sum(x, over_ctx, over_z):
        if over_ctx:
            for k in [1] + [2 * b for b in chip_bits]:
                x = x + swap(x, "ctx", k, n_ctx)
        if over_z:
            for k in z_bits:
                x = x + z_swap(x, k)
        return x

    def chip_reduce(pieces):
        result = []
        for h, order in ((0, chip_bits), (1, chip_bits[::-1])):
            cur = dict(pieces[h])
            for step, b in enumerate(order):
                keep = {k: v for k, v in cur.items() if not k & b}
                for k, v in cur.items():
                    if k & b:
                        got = chip_swap(v, b)
                        if step == len(order) - 1:
                            return_pair = (keep[k ^ b], got)
                        else:
                            keep[k ^ b] = (keep[k ^ b].astype(F32) + got.astype(F32)).astype(BF)
                cur = keep
            result.extend(return_pair)
        return result

    def chip_gather(halves):
        result = {k: [None, None] for k in range(n_chip)}
        for h, order in ((0, chip_bits), (1, chip_bits[::-1])):
            cur = {0: halves[h]}
            for b in order:
                for k, v in list(cur.items()):
                    cur[k ^ b] = chip_swap(v, b)
            for k, v in cur.items():
                result[k][h] = v
        return result

    def rel(x):
        return jnp.take(x, f ^ jnp.arange(n_z, dtype=jnp.int32), axis=0)

    x_loc = inputs[0].astype(F32)
    ends = jnp.cumsum(doc_lengths, axis=1)
    starts = ends - doc_lengths
    positions = jnp.arange(seq, dtype=jnp.int32)
    doc_abs = jnp.sum((positions[None, :, None] >= ends[:, None, :]).astype(jnp.int32), axis=2)
    labels = jnp.arange(DOCS, dtype=jnp.int32)
    begin = jnp.sum(jnp.where(doc_abs[:, :, None] == labels, starts[:, None, :], 0), axis=2)
    place_abs = positions[None, :] - begin
    my_pos = c * tok + jnp.arange(tok, dtype=jnp.int32)
    my_ends = lax.dynamic_slice_in_dim(ends, f, 1, 0)
    my_keep = (my_pos < my_ends[0, DOCS - 1]).astype(F32)[:, None]
    inv1_loc = lax.rsqrt(jnp.mean(x_loc * x_loc, axis=1, keepdims=True) + norm_eps)
    n1_loc = x_loc * inv1_loc
    dy_loc = cotangent[0].astype(F32) * my_keep
    payload = jnp.stack((n1_loc.astype(BF), dy_loc.astype(BF), inputs[0]), axis=1)
    payload = payload.reshape(tok, 3, n_ctx, dc).transpose(2, 0, 1, 3).reshape(n_ctx, tok, 3 * dc)
    payload = lax.all_to_all(payload, "ctx", 0, 0, tiled=True).reshape(seq, 3 * dc)
    x_col = payload[:, 2 * dc :].astype(F32)
    nd = z_gather(payload[:, : 2 * dc])
    nd_t = [core_swap(v) for v in nd]
    nd_o = jnp.concatenate(nd, axis=0)
    nd_t = jnp.concatenate(nd_t, axis=0)

    small = jnp.concatenate((att_gain[None], ffn_gain[None]), axis=0).astype(BF)
    small_t = core_swap(small)
    ga, gf = small[0:1].astype(F32), small[1:2].astype(F32)
    ga_t, gf_t = small_t[0:1].astype(F32), small_t[1:2].astype(F32)
    ra, rf = att_router.astype(BF), ffn_router.astype(BF)

    routes = jnp.concatenate((att_routes, ffn_routes), axis=2)
    routes = lax.all_gather(routes, "ctx", axis=0, tiled=True)
    routes = rel(jnp.transpose(routes, (1, 0, 2))).reshape(rows, 4)
    route_row = jnp.transpose(routes)
    att_route3 = routes[:, :2].reshape(n_z, seq, 2)
    experts = jnp.arange(E_F, dtype=jnp.int32)
    hot = (route_row[2:4, None, :] == experts[None, :, None]).astype(F32)
    blocks = rows // 128
    hot_b = hot.reshape(2 * E_F, blocks, 128)
    lane = jnp.arange(128)
    tri = (lane[:, None] < lane[None, :]).astype(BF)
    before = jnp.einsum("anl,lm->anm", hot_b.astype(BF), tri, preferred_element_type=F32)
    totals = jnp.sum(hot_b, axis=2)
    lane_b = jnp.arange(blocks)
    tri_b = (lane_b[:, None] < lane_b[None, :]).astype(BF)
    before_b = jnp.dot(totals.astype(BF), tri_b, preferred_element_type=F32)
    rank = (before + before_b[:, :, None]).reshape(2, E_F, rows)
    counts = jnp.sum(totals, axis=1).reshape(2, E_F)
    per_expert = counts[0] + counts[1]
    off = jnp.sum(jnp.where(experts[:, None] > experts[None, :], per_expert[None, :], 0.0), axis=1)
    base = jnp.stack((off, off + counts[0]))
    pos_row = jnp.sum(hot * (base[:, :, None] + rank), axis=1).astype(jnp.int32)
    pos_col = jnp.transpose(pos_row)
    offsets = jnp.concatenate((off, jnp.sum(per_expert)[None])).astype(jnp.int32)

    def tile_scalars(p0):
        first = jnp.sum((offsets[1:] <= p0).astype(jnp.int32))
        last = jnp.sum((offsets[1:] <= p0 + ts - 1).astype(jnp.int32))
        return jnp.concatenate((jnp.stack((p0, first, last)), offsets))

    def start_of(k, other, h):
        return 2 * ts * (2 * (chip ^ k) + (core ^ other)) + h * ts

    def split_halves(w):
        mine = lax.dynamic_slice_in_dim(w, core * width, width, 2)
        theirs = lax.dynamic_slice_in_dim(w, (1 - core) * width, width, 2)
        return mine, theirs, core_swap(theirs)

    def e_major(w):
        return jnp.transpose(w.astype(BF), (1, 0, 2))

    wq_m, wq_t, wq_x = split_halves(e_major(query_weight))
    wk_m, wk_t, wk_x = split_halves(e_major(kv_weight))
    wo_m, wo_t, wo_x = split_halves(e_major(output_weight))

    def pad_lanes(w):
        return w if fl == fl_real else jnp.pad(w, [(0, 0)] * (w.ndim - 1) + [(0, fl - fl_real)])

    wd = pad_lanes(e_major(down_weight))
    wd_x = core_swap(wd)
    wg = pad_lanes(jnp.transpose(gate_up_weight.astype(BF), (1, 0, 2, 3))).reshape(E_F, dc, 2 * fl)
    wg_x = core_swap(wg)

    h1 = (nd_o[:, :dc].astype(F32) * ga).astype(BF)
    h1_x = (nd_t[:, :dc].astype(F32) * ga_t).astype(BF)
    dy = nd_o[:, dc:]
    dy_x = nd_t[:, dc:]

    la = lax.dot_general(ra, h1, (((0,), (1,)), ((), ())), preferred_element_type=F32)
    la = small_sum(la, True, False)

    def gates_of(logits, route2):
        picked = jnp.sum(jnp.where(route2[:, None, :] == experts[None, :, None], logits[None], 0.0), axis=1)
        return jax.nn.softmax(picked, axis=0)

    pa = gates_of(la, route_row[0:2])
    pa3 = jnp.transpose(pa).reshape(n_z, seq, 2)

    def project(xo, xt, weights, k, h):
        n_extra = 2 if len(weights) == 4 else 0
        cols = (2 + n_extra) * width
        at = lambda i, sc: (sc[0], 0)
        return call(
            functools.partial(proj_body, n_extra, width),
            jnp.reshape(2 * (chip ^ k) + h, (1,)),
            (1,),
            [spec((half, 4), at), spec((half, dc), at), spec((half, dc), at)] + [spec(w.shape) for w in weights],
            spec((half, cols)),
            jax.ShapeDtypeStruct((half, cols), BF),
            flops=2 * half * 2 * dc * (E_A + n_extra) * width,
            size=2 * (half * cols + 2 * half * dc + 2 * dc * (E_A + n_extra) * width),
        )(routes, xo, xt, *weights)

    def project_all(xo, xt, weights):
        return [{k: project(xo, xt, weights, k, h) for k in range(n_chip)[::-1]} for h in range(2)]

    qkv_parts = chip_reduce(project_all(h1, h1_x, (wq_m, wq_x, wk_m, wk_x)))

    s_abs = f ^ chip
    doc_one = lax.dynamic_index_in_dim(doc_abs, s_abs, 0, keepdims=False)
    place_one = lax.dynamic_index_in_dim(place_abs, s_abs, 0, keepdims=False)
    doc_col, doc_row = doc_one[:, None], doc_one[None, :]
    halves = jnp.arange(HD // 2, dtype=F32)
    angles = place_one.astype(F32)[:, None] * (rope_base ** (-2.0 * halves / HD))[None, :]
    cos, sin = jnp.cos(angles), jnp.sin(angles)
    cosf = jnp.concatenate((cos, cos), axis=1)
    sinf = jnp.concatenate((-sin, sin), axis=1)

    one = jnp.zeros((1,), jnp.int32)
    att_flops = 2 * hc * 2 * 2 * seq * seq * HD
    qkv, ao, lse = call(
        functools.partial(attend_body, hc),
        one,
        (1,),
        [spec((half, 4 * width))] * 4 + [spec((seq, 1)), spec((1, seq)), spec((seq, HD)), spec((seq, HD))],
        [spec((seq, 4 * width)), spec((seq, 2 * width)), spec((seq, 128))],
        [
            jax.ShapeDtypeStruct((seq, 4 * width), BF),
            jax.ShapeDtypeStruct((seq, 2 * width), BF),
            jax.ShapeDtypeStruct((seq, 128), F32),
        ],
        flops=att_flops,
        size=seq * width * 20,
    )(*qkv_parts, doc_col, doc_row, cosf, sinf)

    ao_m = [ao] + [chip_swap(ao, k) for k in range(1, n_chip)]
    ao_t = [core_swap(v) for v in ao_m]

    def into_stream(body, k, streams, vals, weights, buf, flops, cols):
        sc = jnp.reshape(chip ^ k, (1,))
        by_stream = [spec((pl.squeezed, seq, 2), lambda i, sc: (sc[0], 0, 0))] * len(streams)
        n_in = len(streams) + 2 + len(weights)
        return call(
            body,
            sc,
            (1,),
            by_stream
            + [spec((seq, cols))] * 2
            + [spec(w.shape) for w in weights]
            + [pl.BlockSpec(memory_space=pl.ANY)],
            spec((1, seq, dc), lambda i, sc: (sc[0], 0, 0)),
            jax.ShapeDtypeStruct((n_z, seq, dc), BF),
            aliases={n_in + 1: 0},
            flops=flops,
            size=2 * (2 * seq * cols + 2 * E_A * dc * width + seq * dc),
        )(*streams, *vals, *weights, buf)

    buf = jnp.zeros((n_z, seq, dc), BF)
    for k in range(n_chip):
        buf = into_stream(
            functools.partial(att_out_body, width),
            k,
            (att_route3, pa3),
            (ao_m[k], ao_t[k]),
            (wo_m, wo_t),
            buf,
            4 * seq * E_A * width * dc,
            2 * width,
        )
    y1 = x_col + z_reduce([buf[k] for k in range(n_z)])

    y1_low = jnp.concatenate(z_gather(y1.astype(BF)), axis=0)
    y1_all = y1_low.astype(F32)
    yg = (y1_all * gf).astype(BF)
    yg_x = (core_swap(y1_low).astype(F32) * gf_t).astype(BF)
    stat = jnp.concatenate(
        (
            lax.dot_general(rf, yg, (((0,), (1,)), ((), ())), preferred_element_type=F32),
            jnp.sum(y1_all * y1_all, axis=1)[None],
            jnp.zeros((7, rows), F32),
        ),
        axis=0,
    )
    stat = small_sum(stat, True, False)
    inv2 = lax.rsqrt(stat[8:9] / D + norm_eps)
    lf = stat[0:E_F] * inv2
    pf = gates_of(lf, route_row[2:4])
    rowv = jnp.concatenate((inv2, pf, jnp.zeros((5, rows), F32)), axis=0)
    pf_col = jnp.transpose(pf)
    ones_col = jnp.ones((rows, 2), F32)
    inv2_col = jnp.transpose(inv2)

    def group_proj(xo, xt, wm, wx, k, h):
        n = wm.shape[2]
        by_expert = spec((1, dc, n), lambda i, sc: (jnp.minimum(sc[1] + i, sc[2]), 0, 0))
        return call(
            group_proj_body,
            tile_scalars(start_of(k, 0, h)),
            (E_F,),
            [spec((2, rows)), spec((rows, dc)), spec((rows, dc)), by_expert, by_expert],
            spec((ts, n)),
            jax.ShapeDtypeStruct((ts, n), BF),
            [pltpu.VMEM((ts, 2 * dc), BF)],
            flops=2 * ts * 2 * dc * (rows + 2 * n),
            size=2 * (2 * rows * dc + 4 * dc * n + ts * n),
        )(pos_row, xo, xt, wm, wx)

    def group_all(xo, xt, wm, wx):
        return [{k: group_proj(xo, xt, wm, wx, k, h) for k in range(n_chip)[::-1]} for h in range(2)]

    da_parts = chip_reduce(group_all(dy, dy_x, wd, wd_x))
    gu_parts = chip_reduce(group_all(yg, yg_x, wg, wg_x))

    dgu_own, act_own, tok_sum = [], [], 0.0
    for h in range(2):
        a, b, t = call(
            functools.partial(middle_body, fl),
            tile_scalars(start_of(0, 0, h)),
            (1,),
            [spec((2, rows)), spec((8, rows))] + [spec((ts, 2 * fl))] * 2 + [spec((ts, fl))] * 2,
            [spec((ts, 2 * fl)), spec((ts, fl)), spec((8, rows))],
            [
                jax.ShapeDtypeStruct((ts, 2 * fl), BF),
                jax.ShapeDtypeStruct((ts, fl), BF),
                jax.ShapeDtypeStruct((8, rows), F32),
            ],
            flops=ts * fl * 30,
            size=ts * fl * 18,
        )(pos_row, rowv, gu_parts[2 * h], gu_parts[2 * h + 1], da_parts[2 * h], da_parts[2 * h + 1])
        dgu_own.append(a)
        act_own.append(b)
        tok_sum = tok_sum + t

    tok_sum = rel(tok_sum.reshape(8, n_z, seq).transpose(1, 0, 2))
    tok_sum = rel(small_sum(tok_sum, True, True)).transpose(1, 0, 2).reshape(8, rows)

    def router_back(dgate, gates, route2):
        dlog = gates * (dgate - jnp.sum(gates * dgate, axis=0, keepdims=True))
        return jnp.sum(jnp.where(route2[:, None, :] == experts[None, :, None], dlog[:, None, :], 0.0), axis=0)

    dlf = router_back(tok_sum[0:2], pf, route_row[2:4])
    m2 = (tok_sum[2:3] + jnp.sum(dlf * lf, axis=0, keepdims=True)) / D
    dlf_low = dlf.astype(BF)

    def gather_pieces(own):
        got = chip_gather(own)
        out = []
        for k in range(n_chip):
            for h in range(2):
                out.append((k, 0, h, got[k][h]))
        for k in range(n_chip):
            for h in range(2):
                out.append((k, 1, h, core_swap(got[k][h])))
        return out

    dgu_pieces = gather_pieces(dgu_own)
    act_pieces = gather_pieces(act_own)

    def group_back(piece, wcol, w, prev):
        k, other, h, vals = piece
        n = w.shape[2]
        return call(
            group_back_body,
            tile_scalars(start_of(k, other, h)),
            (E_F,),
            [
                spec((rows, 2)),
                spec((rows, 2)),
                spec((ts, n)),
                spec((1, dc, n), lambda i, sc: (jnp.minimum(sc[1] + i, sc[2]), 0, 0)),
                spec((rows, dc)),
            ],
            spec((rows, dc)),
            jax.ShapeDtypeStruct((rows, dc), F32),
            [pltpu.VMEM((ts, dc), F32)],
            aliases={5: 0},
            flops=2 * ts * dc * (rows + 2 * n),
            size=2 * (ts * n + 2 * dc * n) + 8 * rows * dc,
        )(pos_col, wcol, vals, w, prev)

    dh2 = jnp.zeros((rows, dc), F32)
    for piece in dgu_pieces:
        dh2 = group_back(piece, ones_col, wg, dh2)
    dh2_own = z_reduce([dh2[k * seq : (k + 1) * seq].astype(BF) for k in range(n_z)])
    dh2_all = jnp.concatenate(z_gather(dh2_own.astype(BF)), axis=0).astype(F32)
    dh2_all = dh2_all + lax.dot_general(dlf_low, rf, (((0,), (1,)), ((), ())), preferred_element_type=F32)
    n2 = y1_all * inv2_col
    dy1 = dy.astype(F32) + inv2_col * (dh2_all * gf - n2 * jnp.transpose(m2))
    dy1_low = dy1.astype(BF)
    dy1_x = core_swap(dy1_low)

    dao_parts = chip_reduce(project_all(dy1_low, dy1_x, (wo_m, wo_x)))
    pa_one = lax.dynamic_index_in_dim(pa3, chip, 0, keepdims=False)
    grads, dgate = call(
        functools.partial(attend_back_body, hc),
        one,
        (1,),
        [spec((half, 2 * width))] * 4
        + [spec((seq, 4 * width)), spec((seq, 2 * width)), spec((seq, 128)), spec((seq, 2))]
        + [spec((seq, 1)), spec((1, seq)), spec((seq, HD)), spec((seq, HD))],
        [spec((seq, 4 * width)), spec((seq, 128))],
        [jax.ShapeDtypeStruct((seq, 4 * width), BF), jax.ShapeDtypeStruct((seq, 128), F32)],
        flops=att_flops * 5 // 2,
        size=seq * width * 30,
    )(*dao_parts, qkv, ao, lse, pa_one, doc_col, doc_row, cosf, sinf)
    g_m = [grads] + [chip_swap(grads, k) for k in range(1, n_chip)]
    g_t = [core_swap(v) for v in g_m]

    dpa = jnp.zeros((n_z, 8, seq), F32)
    dpa = lax.dynamic_update_slice(dpa, jnp.transpose(dgate[:, :8])[None], (s_abs, 0, 0))
    dpa = small_sum(dpa, True, True)
    dpa = lax.dynamic_index_in_dim(dpa, f, 0, keepdims=False)[0:2]

    buf = jnp.zeros((n_z, seq, dc), BF)
    for k in range(n_chip):
        buf = into_stream(
            functools.partial(att_in_back_body, width),
            k,
            (att_route3,),
            (g_m[k], g_t[k]),
            (wq_m, wq_t, wk_m, wk_t),
            buf,
            4 * seq * (E_A + 2) * width * dc,
            4 * width,
        )
    dh1 = z_reduce([buf[k] for k in range(n_z)])
    dla = router_back(dpa, pa[:, :seq], route_row[0:2, :seq]).astype(BF)
    dh1 = dh1 + lax.dot_general(dla, ra, (((0,), (1,)), ((), ())), preferred_element_type=F32)
    back = jnp.concatenate(((dh1 * ga).astype(BF), dy1_low[:seq]), axis=1)

    def to_rows(v):
        n = v.shape[1] // dc
        v = lax.all_to_all(v.reshape(n_ctx, tok, n * dc), "ctx", 0, 0, tiled=True)
        v = v.reshape(n_ctx, tok, n, dc).transpose(2, 1, 0, 3)
        return v.reshape(n, tok, D)

    back = to_rows(back).astype(F32)
    input_grad = back[1] + inv1_loc * (back[0] - n1_loc * jnp.mean(back[0] * n1_loc, axis=1, keepdims=True))
    input_grad = input_grad.astype(BF)[None]

    ffn = jnp.zeros((rows, dc), F32)
    for piece in act_pieces:
        ffn = group_back(piece, pf_col, wd, ffn)
    ffn = z_reduce([ffn[k * seq : (k + 1) * seq].astype(BF) for k in range(n_z)])
    outputs = to_rows((y1 + ffn).astype(BF))

    n_pieces = len(dgu_pieces)
    starts_all = jnp.stack([start_of(k, other, h) for k, other, h, _ in dgu_pieces])

    def sort_t(xt, wcol):
        return call(
            sort_t_body,
            starts_all,
            (n_pieces,),
            [spec((rows, 2)), spec((rows, 2)), spec((dc, rows))],
            spec((dc, ts), lambda i, sc: (0, i)),
            jax.ShapeDtypeStruct((dc, 2 * rows), BF),
            flops=4 * dc * rows * rows,
            size=6 * dc * rows,
        )(pos_col, wcol, xt)

    def group_weight(xs, pieces):
        n = pieces[0][3].shape[1]
        return call(
            functools.partial(group_weight_body, n_pieces),
            jnp.concatenate((starts_all, offsets)),
            (n // fl, E_F),
            [spec((dc, 2 * rows))] + [spec((ts, fl), lambda j, e, sc: (0, j))] * n_pieces,
            spec((1, dc, fl), lambda j, e, sc: (e, 0, j)),
            jax.ShapeDtypeStruct((E_F, dc, n), F32),
            flops=8 * dc * rows * n,
            size=4 * E_F * dc * n + 4 * rows * n,
        )(xs, *[p[3] for p in pieces])

    h2 = (n2 * gf).astype(BF)
    h2_s = sort_t(jnp.transpose(h2), ones_col)
    dfe_s = sort_t(jnp.transpose(dy), pf_col)
    gate_up_grad = group_weight(h2_s, dgu_pieces).reshape(E_F, dc, 2, fl)[..., :fl_real]
    gate_up_grad = jnp.transpose(gate_up_grad, (1, 0, 2, 3))
    down_grad = jnp.transpose(group_weight(dfe_s, act_pieces)[..., :fl_real], (1, 0, 2))

    def att_weight(xt, gated, extra, mine, theirs, cols):
        pieces = [v for pair in zip(mine, theirs) for v in pair]
        sc = jnp.concatenate((chip ^ jnp.arange(n_chip, dtype=jnp.int32), core[None]))
        outs = [(E_A, lambda i, e, sc: (e, 0, sc[n_chip] ^ i))]
        if extra:
            outs.append((2, lambda i, e, sc: (jnp.minimum(e, 1), 0, sc[n_chip] ^ i)))
        return call(
            functools.partial(att_weight_body, width, n_chip, gated, extra),
            sc,
            (2, E_A),
            [spec(xt.shape), spec((n_z, seq, 2)), spec((n_z, seq, 2))] + [spec((seq, cols))] * len(pieces),
            [spec((1, dc, width), at) for _, at in outs],
            [jax.ShapeDtypeStruct((n, dc, 2 * width), F32) for n, _ in outs],
            flops=4 * rows * dc * (E_A + 2) * width,
            size=8 * E_A * dc * width + 4 * rows * cols,
        )(xt, att_route3, pa3, *pieces)

    def stream_t(v):
        return jnp.transpose(v.reshape(n_z, seq, dc), (0, 2, 1))

    (output_grad,) = att_weight(stream_t(dy1_low), True, False, ao_m, ao_t, 2 * width)
    query_grad, kv_grad = att_weight(stream_t(h1), False, True, g_m, g_t, 4 * width)
    output_grad = jnp.transpose(output_grad, (1, 0, 2))
    query_grad = jnp.transpose(query_grad, (1, 0, 2))
    kv_grad = jnp.transpose(kv_grad, (1, 0, 2))

    own = slice(0, seq)
    tail = jnp.concatenate(
        (
            jnp.dot(dla, h1[own], preferred_element_type=F32),
            jnp.dot(dlf_low[:, own], h2[own], preferred_element_type=F32),
            jnp.sum(dh1 * nd_o[own, :dc].astype(F32), axis=0, keepdims=True),
            jnp.sum(dh2_all[own] * n2[own], axis=0, keepdims=True),
            jnp.zeros((6, dc), F32),
        ),
        axis=0,
    )
    tail = small_sum(tail, False, True)
    att_router_grad = jnp.transpose(tail[0:E_A])
    ffn_router_grad = jnp.transpose(tail[E_A : E_A + E_F])
    att_gain_grad = tail[E_A + E_F]
    ffn_gain_grad = tail[E_A + E_F + 1]

    return (
        outputs,
        input_grad,
        kv_grad,
        query_grad,
        output_grad,
        att_router_grad,
        att_gain_grad,
        gate_up_grad,
        down_grad,
        ffn_router_grad,
        ffn_gain_grad,
    )


def solution(mesh):
    in_specs = (
        P("fsdp", "ctx", None),
        P("fsdp", "ctx", None),
        P(),
        P("ctx", None, None),
        P("ctx", None, None),
        P("ctx", None, "fsdp"),
        P("ctx", None, "fsdp"),
        P("ctx", None, "fsdp"),
        P("ctx", None),
        P("ctx"),
        P("ctx", None, None, "fsdp"),
        P("ctx", None, "fsdp"),
        P("ctx", None),
        P("ctx"),
    )
    out_specs = (
        P("fsdp", "ctx", None),
        P("fsdp", "ctx", None),
        P("ctx", None, "fsdp"),
        P("ctx", None, "fsdp"),
        P("ctx", None, "fsdp"),
        P("ctx", None),
        P("ctx"),
        P("ctx", None, None, "fsdp"),
        P("ctx", None, "fsdp"),
        P("ctx", None),
        P("ctx"),
    )
    return jax.shard_map(
        per_device, mesh=mesh, in_specs=in_specs, out_specs=out_specs, check_vma=False
    )
```

```python
import functools

import jax
import jax.numpy as jnp
from jax import lax
from jax.experimental import pallas as pl
from jax.experimental.pallas import tpu as pltpu
from jax.sharding import PartitionSpec as P

D = 2048
HEADS = 16
HD = 128
E_A = 8
E_F = 8
FF = 5632
DOCS = 3

norm_eps = 1e-06
rope_base = 10000.0
masked_score = -1e30

BF = jnp.bfloat16
F32 = jnp.float32
VMEM_CAP = 60 * 1024 * 1024
PER_US = 1.1e9


def dot(a, b):
    return lax.dot_general(a, b, (((1,), (0,)), ((), ())), preferred_element_type=F32)


def dot_nt(a, b):
    return lax.dot_general(a, b, (((1,), (1,)), ((), ())), preferred_element_type=F32)


def dot_tn(a, b):
    return lax.dot_general(a, b, (((0,), (0,)), ((), ())), preferred_element_type=F32)


def spec(shape, index=None):
    if index is not None:
        return pl.BlockSpec(shape, index)
    zeros = (0,) * len(shape)
    return pl.BlockSpec(shape, lambda *_: zeros, pipeline_mode=pl.Buffered(1))


def call(chain, body, sc, grid, in_specs, out_specs, out_shape, scratch=(), aliases=None, us=5):
    single = not isinstance(out_shape, (list, tuple))
    out_specs, out_shape = ([out_specs], [out_shape]) if single else (list(out_specs), list(out_shape))
    out_specs = [pl.BlockSpec(v.block_shape, v.index_map) for v in out_specs]
    anywhere = pl.BlockSpec(memory_space=pl.ANY)

    def go(*operands, carry=()):
        waits = [v for v in chain if not any(v is u for u in operands) and not any(v is u for u in carry)]
        n_in, n_extra, n_out, n_carry = len(operands), len(waits) + len(carry), len(out_shape), len(carry)

        def kernel_body(first, *refs):
            outs = refs[n_in + n_extra :]
            body(first, *refs[:n_in], *outs[:n_out], *outs[n_out + n_carry :])

        alias = dict(aliases or {})
        for i in range(n_carry):
            alias[1 + n_in + len(waits) + i] = n_out + i
        out = pl.pallas_call(
            kernel_body,
            out_shape=out_shape + [jax.ShapeDtypeStruct(v.shape, v.dtype) for v in carry],
            grid_spec=pltpu.PrefetchScalarGridSpec(
                num_scalar_prefetch=1,
                grid=grid,
                in_specs=list(in_specs) + [anywhere] * n_extra,
                out_specs=out_specs + [anywhere] * n_carry,
                scratch_shapes=list(scratch),
            ),
            input_output_aliases=alias,
            compiler_params=pltpu.CompilerParams(
                dimension_semantics=("arbitrary",) * len(grid), vmem_limit_bytes=VMEM_CAP
            ),
            cost_estimate=pl.CostEstimate(flops=int(us * PER_US), bytes_accessed=0, transcendentals=0),
        )(sc, *operands, *waits, *carry)
        chain[:] = out[:1]
        result = out[0] if single else out[:n_out]
        return (result, *out[n_out:]) if carry else result

    return go


def proj_body(n_extra, width, n, sc, route, xo, xt, *refs):
    wm, wt = refs[0], refs[1]
    outs, tile = refs[-3:-1], refs[-1]
    a, b = xo[...], xt[...]
    r0, r1 = route[:, 0:1], route[:, 1:2]
    acc0 = jnp.zeros((a.shape[0], width), F32)
    acc1 = acc0
    for e in range(E_A):
        r = dot(a, wm[e]) + dot(b, wt[e])
        acc0 = jnp.where(r0 == e, r, acc0)
        acc1 = jnp.where(r1 == e, r, acc1)
    tile[:, 0:width] = acc0.astype(BF)
    tile[:, width : 2 * width] = acc1.astype(BF)
    for i in range(n_extra):
        r = dot(a, wm[E_A + i]) + dot(b, wt[E_A + i])
        tile[:, (2 + i) * width : (3 + i) * width] = r.astype(BF)
    for i in range(n):

        @pl.when(pl.program_id(0) == i)
        def _():
            outs[i // (n // 2)][i % (n // 2)] = tile[...]


def rotate(u, cosf, sinf):
    return u * cosf + pltpu.roll(u, HD // 2, 1) * sinf


def unrotate(u, cosf, sinf):
    return u * cosf - pltpu.roll(u, HD // 2, 1) * sinf


def add_halves(refs):
    a0, a1, b0, b1 = refs
    top = a0[...].astype(F32) + a1[...].astype(F32)
    low = b0[...].astype(F32) + b1[...].astype(F32)
    return jnp.concatenate((top, low), axis=0)


def allowed_pairs(doc_col, doc_row):
    n = doc_col.shape[0]
    t = lax.broadcasted_iota(jnp.int32, (n, n), 0)
    u = lax.broadcasted_iota(jnp.int32, (n, n), 1)
    return (doc_col[...] == doc_row[...]) & (u <= t) & (doc_col[...] < DOCS)


def attend_body(hc, sc, a0, a1, b0, b1, doc_col, doc_row, cosr, sinr, qkv, out, lse):
    width = hc * HD
    u = add_halves((a0, a1, b0, b1))
    cosf, sinf = cosr[...], sinr[...]
    ok = allowed_pairs(doc_col, doc_row)
    for h in range(hc):
        at = 2 * width + h * HD
        k = rotate(u[:, at : at + HD], cosf, sinf).astype(BF)
        v = u[:, at + width : at + width + HD].astype(BF)
        qkv[:, at : at + HD] = k
        qkv[:, at + width : at + width + HD] = v
        for j in range(2):
            lo = j * width + h * HD
            q = rotate(u[:, lo : lo + HD], cosf, sinf).astype(BF)
            qkv[:, lo : lo + HD] = q
            s = jnp.where(ok, dot_nt(q, k) * (HD**-0.5), masked_score)
            m = jnp.max(s, axis=1, keepdims=True)
            p = jnp.where(ok, jnp.exp(s - m), 0.0)
            total = jnp.sum(p, axis=1, keepdims=True)
            total = jnp.where(total > 0, total, 1.0)
            out[:, lo : lo + HD] = (dot(p.astype(BF), v) / total).astype(BF)
            lse[:, 2 * h + j : 2 * h + j + 1] = m + jnp.log(total)


def attend_back_body(hc, sc, a0, a1, b0, b1, qkv, att, lse, gates, doc_col, doc_row, cosr, sinr, grads, dgate):
    width = hc * HD
    u = add_halves((a0, a1, b0, b1))
    cosf, sinf = cosr[...], sinr[...]
    ok = allowed_pairs(doc_col, doc_row)
    keep = (doc_col[...] < DOCS).astype(F32)
    dg = [jnp.zeros((u.shape[0], 1), F32) for _ in range(2)]
    for h in range(hc):
        at = 2 * width + h * HD
        k = qkv[:, at : at + HD]
        v = qkv[:, at + width : at + width + HD]
        dk = jnp.zeros((u.shape[0], HD), F32)
        dv = dk
        for j in range(2):
            lo = j * width + h * HD
            q = qkv[:, lo : lo + HD]
            o = att[:, lo : lo + HD].astype(F32)
            raw = u[:, lo : lo + HD]
            dg[j] = dg[j] + jnp.sum(raw * o, axis=1, keepdims=True)
            do = (raw * (gates[:, j : j + 1] * keep)).astype(BF)
            delta = jnp.sum(do.astype(F32) * o, axis=1, keepdims=True)
            s = dot_nt(q, k) * (HD**-0.5)
            p = jnp.where(ok, jnp.exp(s - lse[:, 2 * h + j : 2 * h + j + 1]), 0.0)
            ds = (p * (dot_nt(do, v) - delta)).astype(BF)
            dq = dot(ds, k) * (HD**-0.5)
            grads[:, lo : lo + HD] = unrotate(dq, cosf, sinf).astype(BF)
            dk = dk + dot_tn(ds, q)
            dv = dv + dot_tn(p.astype(BF), do)
        grads[:, at : at + HD] = unrotate(dk * (HD**-0.5), cosf, sinf).astype(BF)
        grads[:, at + width : at + width + HD] = dv.astype(BF)
    dgate[...] = jnp.zeros_like(dgate)
    dgate[:, 0:1] = dg[0]
    dgate[:, 1:2] = dg[1]


def chosen(hot0, hot1, a, b, e):
    return a * hot0[e] + b * hot1[e]


def one_hots(route):
    return [[jnp.where(route[:, j : j + 1] == e, 1.0, 0.0).astype(BF) for e in range(E_A)] for j in range(2)]


def gated(vals, gates, width):
    a = (vals[:, 0:width].astype(F32) * gates[:, 0:1]).astype(BF)
    b = (vals[:, width : 2 * width].astype(F32) * gates[:, 1:2]).astype(BF)
    return a, b


def att_out_body(width, sc, route, gates, om, ot, wm, wt, prev, out):
    acc = jnp.zeros(out.shape[1:], F32)
    hot0, hot1 = one_hots(route)
    am, bm = gated(om, gates, width)
    at, bt = gated(ot, gates, width)
    for e in range(E_A):
        acc += dot_nt(chosen(hot0, hot1, am, bm, e), wm[e])
        acc += dot_nt(chosen(hot0, hot1, at, bt, e), wt[e])
    out[0] = acc.astype(BF)


def att_in_back_body(width, sc, route, gm, gt, wm, wt, prev, out):
    acc = jnp.zeros(out.shape[1:], F32)
    hot0, hot1 = one_hots(route)
    am, bm = gm[:, 0:width], gm[:, width : 2 * width]
    at, bt = gt[:, 0:width], gt[:, width : 2 * width]
    for e in range(E_A):
        acc += dot_nt(chosen(hot0, hot1, am, bm, e), wm[e])
        acc += dot_nt(chosen(hot0, hot1, at, bt, e), wt[e])
    for i in range(2):
        lo = (2 + i) * width
        acc += dot_nt(gm[:, lo : lo + width], wm[E_A + i]) + dot_nt(gt[:, lo : lo + width], wt[E_A + i])
    out[0] = acc.astype(BF)


def att_weight_body(width, n, with_gates, extra, sc, *refs):
    xt, route, gates = refs[0], refs[1], refs[2]
    pieces = refs[3 : 3 + 2 * n]
    out = refs[3 + 2 * n]
    out2 = refs[4 + 2 * n] if extra else None
    vals = refs[-1]
    seq = route.shape[1]
    half = pl.program_id(0)
    e = pl.program_id(1)
    for side in range(2):

        @pl.when((half == side) & (e == 0))
        def _():
            for k in range(n):
                piece = pieces[2 * k + side]
                if with_gates:
                    a, b = gated(piece, gates[sc[k]], width)
                else:
                    a, b = piece[:, 0:width], piece[:, width : 2 * width]
                vals[k, :, 0:width] = a
                vals[k, :, width : 2 * width] = b
            if extra:
                for i in range(2):
                    lo = (2 + i) * width
                    acc = jnp.zeros((xt.shape[1], width), F32)
                    for k in range(n):
                        acc += dot(xt[sc[k]], pieces[2 * k + side][:, lo : lo + width])
                    out2[:, i, :] = acc

    acc = jnp.zeros((xt.shape[1], width), F32)
    for k in range(n):
        r = route[sc[k]]
        hot0 = jnp.where(r[:, 0:1] == e, 1.0, 0.0).astype(BF)
        hot1 = jnp.where(r[:, 1:2] == e, 1.0, 0.0).astype(BF)
        sel = vals[k, :, 0:width] * hot0 + vals[k, :, width : 2 * width] * hot1
        acc += dot(xt[sc[k]], sel)
    for i in range(E_A):

        @pl.when(e == i)
        def _():
            out[:, i, :] = acc


def row_chunks(rows):
    step = min(rows, 1024)
    return [(i, step) for i in range(0, rows, step)]


def group_proj_body(n, parts, base, sc, pos, xo, xt, wm, wt, *refs):
    outs, xs = refs[:parts], refs[parts]
    i = pl.program_id(0)
    steps = pl.num_programs(0)
    ts = outs[0].shape[1]
    dc = xo.shape[1]
    at = base + n + i
    tile, e, kind = sc[at], sc[at + steps], sc[at + 2 * steps]
    p0 = sc[base + tile]

    @pl.when(kind == 2)
    def _():
        a = jnp.zeros((ts, dc), F32)
        b = a
        for lo, m in row_chunks(xo.shape[0]):
            ids = p0 + lax.broadcasted_iota(jnp.int32, (ts, m), 0)
            hot = (pos[0:1, lo : lo + m] == ids) | (pos[1:2, lo : lo + m] == ids)
            hot = jnp.where(hot, 1.0, 0.0).astype(BF)
            a = a + dot(hot, xo[lo : lo + m, :])
            b = b + dot(hot, xt[lo : lo + m, :])
        xs[:, 0:dc] = a.astype(BF)
        xs[:, dc : 2 * dc] = b.astype(BF)

    rows = p0 + lax.broadcasted_iota(jnp.int32, (ts, 1), 0)
    for t in range(n):
        out, at = outs[t // (n // parts)], t % (n // parts)

        @pl.when((kind == 2) & (tile == t))
        def _():
            out[at] = (dot(xs[:, 0:dc], wm[0]) + dot(xs[:, dc : 2 * dc], wt[0])).astype(BF)

        @pl.when((kind == 1) & (tile == t))
        def _():
            r = dot(xs[:, 0:dc], wm[0]) + dot(xs[:, dc : 2 * dc], wt[0])
            out[at] = jnp.where(rows >= sc[base + n + 3 * steps + e], r, out[at].astype(F32)).astype(BF)


def middle_body(fl, sc, pos, rowv, *refs):
    gu, da = refs[0:4], refs[4:6]
    dgu, act, tok = refs[6:]
    ts = gu[0].shape[0]
    rows = pos.shape[1]
    half = pl.program_id(0)
    p0 = sc[half]
    inv = jnp.zeros((ts, 1), F32)
    gate = inv
    for lo, n in row_chunks(rows):
        ids = p0 + lax.broadcasted_iota(jnp.int32, (ts, n), 0)
        is0 = pos[0:1, lo : lo + n] == ids
        is1 = pos[1:2, lo : lo + n] == ids
        inv += jnp.sum(jnp.where(is0 | is1, rowv[0:1, lo : lo + n], 0.0), axis=1, keepdims=True)
        picked = jnp.where(is0, rowv[1:2, lo : lo + n], jnp.where(is1, rowv[2:3, lo : lo + n], 0.0))
        gate += jnp.sum(picked, axis=1, keepdims=True)

    def work(g0, g1, d):
        dpf = jnp.zeros((ts, 128), F32)
        dn = dpf
        step = 128
        for lo in range(0, fl, step):
            gt = (g0[:, lo : lo + step].astype(F32) + g1[:, lo : lo + step].astype(F32)) * inv
            up = (g0[:, fl + lo : fl + lo + step].astype(F32) + g1[:, fl + lo : fl + lo + step].astype(F32)) * inv
            raw = d[:, lo : lo + step].astype(F32)
            sg = 1.0 / (1.0 + jnp.exp(-gt))
            silu = gt * sg
            a = silu * up
            act[0, :, lo : lo + step] = (a * gate).astype(BF)
            da = raw * gate
            dgt = da * up * (sg + silu * (1.0 - sg))
            dup = da * silu
            dgu[0, :, lo : lo + step] = (dgt * inv).astype(BF)
            dgu[0, :, fl + lo : fl + lo + step] = (dup * inv).astype(BF)
            dpf += raw * a
            dn += dgt * gt + dup * up
        dpf = jnp.sum(dpf, axis=1, keepdims=True)
        dn = jnp.sum(dn, axis=1, keepdims=True)
        for lo, n in row_chunks(rows):
            ids = p0 + lax.broadcasted_iota(jnp.int32, (ts, n), 0)
            is0 = pos[0:1, lo : lo + n] == ids
            is1 = pos[1:2, lo : lo + n] == ids
            t0 = jnp.sum(jnp.where(is0, dpf, 0.0), axis=0, keepdims=True)
            t1 = jnp.sum(jnp.where(is1, dpf, 0.0), axis=0, keepdims=True)
            t2 = jnp.sum(jnp.where(is0 | is1, dn, 0.0), axis=0, keepdims=True)
            new = jnp.concatenate((t0, t1, t2, jnp.zeros((5, n), F32)), axis=0)
            tok[:, lo : lo + n] = new + jnp.where(half == 0, 0.0, tok[:, lo : lo + n])

    for h in range(2):

        @pl.when(half == h)
        def _():
            work(*gu[2 * h : 2 * h + 2], da[h])


def piece_of(arrays, place):
    i, h = place
    return arrays[i][...] if h is None else arrays[i][h]


def group_back_body(where, base, sc, posc, *refs):
    n = len(where)
    arrays, (w, prev, out, dh) = refs[:-4], refs[-4:]
    i = pl.program_id(0)
    steps = pl.num_programs(0)
    ts = dh.shape[0] // n
    at = base + n + i
    tile, e, kind = sc[at], sc[at + steps], sc[at + 2 * steps]
    p0 = sc[base + tile]
    rows = p0 + lax.broadcasted_iota(jnp.int32, (ts, 1), 0)
    for t in range(n):

        @pl.when((kind == 2) & (tile == t))
        def _():
            dh[t * ts : (t + 1) * ts, :] = dot_nt(piece_of(arrays, where[t]), w[0])

        @pl.when((kind == 1) & (tile == t))
        def _():
            r = dot_nt(piece_of(arrays, where[t]), w[0])
            old = dh[t * ts : (t + 1) * ts, :]
            dh[t * ts : (t + 1) * ts, :] = jnp.where(rows >= sc[base + n + 3 * steps + e], r, old)

    @pl.when(i == steps - 1)
    def _():
        for lo, m in row_chunks(out.shape[0]):
            acc = prev[lo : lo + m, :]
            for t in range(n):
                ids = sc[base + t] + lax.broadcasted_iota(jnp.int32, (m, ts), 1)
                hot = (posc[lo : lo + m, 0:1] == ids) | (posc[lo : lo + m, 1:2] == ids)
                acc = acc + dot(jnp.where(hot, 1.0, 0.0).astype(BF), dh[t * ts : (t + 1) * ts, :].astype(BF))
            out[lo : lo + m, :] = acc


def sort_t_body(sc, pos, x, out):
    p0 = sc[pl.program_id(0)]
    ts = out.shape[1]
    acc = jnp.zeros((ts, x.shape[1]), F32)
    for lo, m in row_chunks(x.shape[0]):
        ids = p0 + lax.broadcasted_iota(jnp.int32, (ts, m), 0)
        hot = (pos[0:1, lo : lo + m] == ids) | (pos[1:2, lo : lo + m] == ids)
        acc += dot(jnp.where(hot, 1.0, 0.0).astype(BF), x[lo : lo + m, :])
    out[...] = jnp.transpose(acc).astype(BF)


def group_weight_body(where, fl, sc, xs, *refs):
    n = len(where)
    arrays, (out, acc) = refs[:-2], refs[-2:]
    ts = xs.shape[1] // n
    e = pl.program_id(0)
    lo, hi = sc[n + e], sc[n + e + 1]
    acc[...] = jnp.zeros_like(acc)
    for i in range(n):
        p0 = sc[i]

        @pl.when((p0 < hi) & (p0 + ts > lo))
        def _():
            ids = p0 + lax.broadcasted_iota(jnp.int32, (1, ts), 1)
            ok = jnp.where((ids >= lo) & (ids < hi), 1.0, 0.0).astype(BF)
            acc[...] += dot(xs[:, i * ts : (i + 1) * ts] * ok, piece_of(arrays, where[i]))

    if len(out.shape) == 4:
        real = out.shape[3]
        out[:, 0, 0, :] = acc[:, 0:real]
        out[:, 0, 1, :] = acc[:, fl : fl + real]
    else:
        for i in range(E_F):

            @pl.when(e == i)
            def _():
                out[:, i, :] = acc[:, 0 : out.shape[2]]


def hold_body(sc, out):
    out[...] = jnp.zeros_like(out)


def add_body(sc, x, got, out):
    out[...] = x[...] + got[...]


def join_body(axis, n, sc, *refs):
    size = refs[0].shape[axis]
    for k in range(n):
        if axis:
            refs[n][:, k * size : (k + 1) * size] = refs[k][...]
        else:
            refs[n][k * size : (k + 1) * size, :] = refs[k][...]


def join_scaled_body(n, sc, gain, *refs):
    size = refs[0].shape[0]
    for k in range(n):
        v = refs[k][...]
        refs[n][k * size : (k + 1) * size, :] = v
        refs[n + 1][k * size : (k + 1) * size, :] = (v.astype(F32) * gain[...]).astype(BF)


def pairs_body(sc, a0, a1, b0, b1, a, b):
    a[...] = (a0[...].astype(F32) + a1[...].astype(F32)).astype(BF)
    b[...] = (b0[...].astype(F32) + b1[...].astype(F32)).astype(BF)


def total_body(n, sc, *refs):
    total = refs[0][...].astype(F32)
    for v in refs[1:n]:
        total = total + v[...].astype(F32)
    refs[n][...] = total
    refs[n + 1][...] = total.astype(BF)


def step_body(sc, *refs):
    for h in range(2):
        refs[4 + h][...] = (refs[2 * h][...].astype(F32) + refs[2 * h + 1][...].astype(F32)).astype(BF)


def middle_grad_body(n, sc, dy, y1, dlf, coef, rf, gf, *refs):
    i = pl.program_id(0)
    dy1, dh2 = refs[n:]
    router = dot_tn(dlf[...], rf[...])

    def work(part):
        total = part[...].astype(F32) + router
        dy1[...] = (dy[...].astype(F32) + total * gf[...] - y1[...].astype(F32) * coef[...]).astype(BF)

        @pl.when(i == 0)
        def _():
            dh2[...] = total

    for k in range(n):

        @pl.when(i == k)
        def _():
            work(refs[k])


def prep_gate_up_body(fl, sc, w, out):
    real = w.shape[3]
    for e in range(E_F):
        for j in range(2):
            out[e, :, j * fl : j * fl + real] = w[:, e, j, :].astype(BF)
            if real != fl:
                out[e, :, j * fl + real : (j + 1) * fl] = jnp.zeros((w.shape[0], fl - real), BF)


def prep_down_body(fl, sc, w, out):
    real = w.shape[2]
    out[:, :, 0:real] = jnp.swapaxes(w[...].astype(BF), 0, 1)
    if real != fl:
        out[:, :, real:fl] = jnp.zeros((E_F, w.shape[0], fl - real), BF)


def per_device(
    inputs,
    cotangent,
    doc_lengths,
    att_routes,
    ffn_routes,
    kv_weight,
    query_weight,
    output_weight,
    att_router,
    att_gain,
    gate_up_weight,
    down_weight,
    ffn_router,
    ffn_gain,
):
    n_ctx = lax.axis_size("ctx")
    n_z = lax.axis_size("fsdp")
    c = lax.axis_index("ctx")
    f = lax.axis_index("fsdp")
    n_chip = n_ctx // 2
    chip, core = c // 2, c % 2
    tok = inputs.shape[1]
    seq = tok * n_ctx
    dc = D // n_ctx
    rows = n_z * seq
    hc = HEADS // n_z // 2
    width = hc * HD
    half = seq // 2
    fl_real = FF // n_z
    fl = -(-fl_real // 128) * 128
    ts = 2 * rows // n_ctx // 2
    assert n_chip == n_z

    chain = []
    launch = functools.partial(call, chain)

    def swap(x, axis, k, n):
        return lax.ppermute(x, axis, [(i, i ^ k) for i in range(n)])

    def core_swap(x):
        return swap(x, "ctx", 1, n_ctx)

    def chip_swap(x, k):
        return swap(x, "ctx", 2 * k, n_ctx)

    def z_swap(x, k):
        return swap(x, "fsdp", k, n_z)

    chip_bits = [1 << i for i in range(n_chip.bit_length() - 1)]
    z_bits = [1 << i for i in range(n_z.bit_length() - 1)]

    def z_gather(x):
        return [x] + [z_swap(x, k) for k in range(1, n_z)]

    def z_send(pieces):
        return [pieces[0]] + [z_swap(pieces[k], k) for k in range(1, n_z)]

    def z_total(got, *others):
        got = [*got, *others]
        return launch(
            functools.partial(total_body, len(got)),
            jnp.zeros((1,), jnp.int32),
            (1,),
            [spec((seq, dc))] * len(got),
            [spec((seq, dc))] * 2,
            [jax.ShapeDtypeStruct((seq, dc), F32), jax.ShapeDtypeStruct((seq, dc), BF)],
            us=1.5,
        )(*got)

    def mark(*values):
        chain.extend(values)

    one = jnp.zeros((1,), jnp.int32)

    def hold(*vals):
        out = launch(
            hold_body, one, (1,), [], spec((8, 128)), jax.ShapeDtypeStruct((8, 128), F32), us=0.5
        )(carry=vals)
        return list(out[1:])

    def join(vals, axis):
        m, n = vals[0].shape
        shape = (m, len(vals) * n) if axis else (len(vals) * m, n)
        return launch(
            functools.partial(join_body, axis, len(vals)),
            one,
            (1,),
            [spec((m, n))] * len(vals),
            spec(shape),
            jax.ShapeDtypeStruct(shape, vals[0].dtype),
            us=1.5,
        )(*vals)

    def join_scaled(vals, gain):
        m, n = vals[0].shape
        shape = (len(vals) * m, n)
        return launch(
            functools.partial(join_scaled_body, len(vals)),
            one,
            (1,),
            [spec((1, n))] + [spec((m, n))] * len(vals),
            [spec(shape)] * 2,
            [jax.ShapeDtypeStruct(shape, BF)] * 2,
            us=2,
        )(gain, *vals)

    class Small:
        def __init__(self, x, hops):
            self.x = x
            self.todo = [
                (kind, b)
                for kind in hops
                for b in {"c": [1], "x": [2 * b for b in chip_bits], "z": z_bits, "g": z_bits}[kind]
            ]
            self.send()

        def send(self):
            kind, b = self.todo[0]
            axis, n = ("ctx", n_ctx) if kind in "cx" else ("fsdp", n_z)
            self.got = swap(self.x, axis, b, n)

        def step(self):
            if not self.todo:
                return
            kind, _ = self.todo.pop(0)
            if kind == "g":
                self.x = join([self.x, self.got], 1)
            else:
                m = self.x.shape
                self.x = launch(
                    add_body,
                    one,
                    (1,),
                    [spec(m)] * 2,
                    spec(m),
                    jax.ShapeDtypeStruct(m, F32),
                    us=0.5,
                )(self.x, self.got)
            if self.todo:
                self.send()

        def finish(self):
            while self.todo:
                self.step()
            return self.x

    orders = (chip_bits, chip_bits[::-1])

    def kept(order):
        ks = [0]
        for b in reversed(order[1:]):
            ks = ks + [k ^ b for k in ks]
        return ks

    late = [(k, h) for h in range(2) for k in kept(orders[h])]
    early = [(k ^ orders[h][0], h) for k, h in late]
    groups = (early, late, early + late)

    def send_first(tiles):
        return [chip_swap(tiles[h], orders[h][0]) for h in range(2)]

    def send_next(keep, got, step):
        n, m, cols = keep[0].shape

        def add(first):
            some = spec((1, m, cols), lambda i, sc: (i + first, 0, 0))
            part = spec((1, m, cols), lambda i, sc: (i, 0, 0))
            return launch(
                step_body,
                one,
                (n // 2,),
                [some] * 4,
                [part] * 2,
                [jax.ShapeDtypeStruct((n // 2, m, cols), BF)] * 2,
                us=n * m * cols * 4e-6,
            )(keep[0], got[0], keep[1], got[1])

        left = add(n // 2)
        sent = [chip_swap(left[h], orders[h][step]) for h in range(2)]
        return add(0), sent

    def finish_reduce(keep, got, step):
        while keep[0].shape[0] > 1:
            keep, got = send_next(keep, got, step)
            step += 1
        return [v[0] for h in range(2) for v in (keep[h], got[h])]

    def rel(x):
        return jnp.take(x, f ^ jnp.arange(n_z, dtype=jnp.int32), axis=0)

    x_loc = inputs[0].astype(F32)
    ends = jnp.cumsum(doc_lengths, axis=1)
    my_pos = c * tok + jnp.arange(tok, dtype=jnp.int32)
    my_ends = lax.dynamic_slice_in_dim(ends, f, 1, 0)
    my_keep = (my_pos < my_ends[0, DOCS - 1]).astype(F32)[:, None]
    inv1_loc = lax.rsqrt(jnp.mean(x_loc * x_loc, axis=1, keepdims=True) + norm_eps)
    n1_loc = x_loc * inv1_loc
    dy_loc = cotangent[0].astype(F32) * my_keep
    payload = jnp.stack((n1_loc.astype(BF), dy_loc.astype(BF), inputs[0]), axis=1)
    payload = payload.reshape(tok, 3, n_ctx, dc).transpose(2, 0, 1, 3).reshape(n_ctx, tok, 3 * dc)
    payload = lax.all_to_all(payload, "ctx", 0, 0, tiled=True).reshape(seq, 3 * dc)
    n1_own, dy_own, x_own = payload[:, :dc], payload[:, dc : 2 * dc], payload[:, 2 * dc :]

    routes = jnp.concatenate((att_routes, ffn_routes), axis=2)[None]
    for b in [1] + [2 * v for v in chip_bits]:
        routes = jnp.concatenate((routes, swap(routes, "ctx", b, n_ctx)), axis=0)
    routes = jnp.take(routes, c ^ jnp.arange(n_ctx, dtype=jnp.int32), axis=0).reshape(seq, n_z, 4)
    routes = rel(jnp.transpose(routes, (1, 0, 2))).reshape(rows, 4)
    route_row = jnp.transpose(routes)
    att_route3 = routes[:, :2].reshape(n_z, seq, 2)
    experts = jnp.arange(E_F, dtype=jnp.int32)

    def split_halves(w):
        mine = lax.dynamic_slice_in_dim(w, core * width, width, 2)
        theirs = lax.dynamic_slice_in_dim(w, (1 - core) * width, width, 2)
        return mine, theirs, core_swap(theirs)

    def e_major(w):
        return jnp.transpose(w.astype(BF), (1, 0, 2))

    qk_weight = jnp.concatenate((e_major(query_weight), e_major(kv_weight)), axis=0)
    wqk_m, wqk_t, wqk_x = split_halves(qk_weight)
    small = jnp.concatenate((att_gain[None], ffn_gain[None]), axis=0)
    small_t = core_swap(small.astype(BF)).astype(F32)
    small = small.astype(BF).astype(F32)
    ga, gf, ga_t, gf_t = small[0:1], small[1:2], small_t[0:1], small_t[1:2]
    ra, rf = att_router.astype(BF), ffn_router.astype(BF)

    def row_logits(router, hidden):
        return lax.dot_general(router, hidden, (((0,), (1,)), ((), ())), preferred_element_type=F32)

    def gates_of(logits, route2):
        picked = jnp.sum(jnp.where(route2[:, None, :] == experts[None, :, None], logits[None], 0.0), axis=1)
        return jax.nn.softmax(picked, axis=0)

    n1 = z_gather(n1_own)
    la = Small(row_logits(ra, (n1_own.astype(F32) * ga).astype(BF)), "cxg")
    step = 32
    mark(n1_own)
    wg, dy_own = launch(
        functools.partial(prep_gate_up_body, fl),
        jnp.zeros((1,), jnp.int32),
        (dc // step,),
        [spec((step, E_F, 2, fl_real), lambda i, sc: (i, 0, 0, 0))],
        spec((E_F, step, 2 * fl), lambda i, sc: (0, i, 0)),
        jax.ShapeDtypeStruct((E_F, dc, 2 * fl), BF),
            us=26,
    )(gate_up_weight, carry=(dy_own,))
    n1, h1 = join_scaled(n1, ga)
    n1_t = core_swap(n1)
    wg_x = core_swap(wg)
    dy = dy_own
    dy_got = z_swap(dy, z_bits[0])
    h1_x = (n1_t.astype(F32) * ga_t).astype(BF)
    def project(xo, xt, weights, n_extra, g):
        cols = (2 + n_extra) * width
        group = groups[g]
        n = len(group)
        at = lambda i, sc: (sc[i], 0)
        return launch(
            functools.partial(proj_body, n_extra, width, n),
            jnp.stack([2 * (chip ^ k) + h for k, h in group]),
            (n,),
            [spec((half, 4), at), spec((half, dc), at), spec((half, dc), at)] + [spec(w.shape) for w in weights],
            [spec((n // 2, half, cols))] * 2,
            [jax.ShapeDtypeStruct((n // 2, half, cols), BF)] * 2,
            [pltpu.VMEM((half, cols), BF)],
            us=8 if n_extra else 7,
        )(routes, xo, xt, *weights)

    def prep_down():
        return launch(
            functools.partial(prep_down_body, fl),
            jnp.zeros((1,), jnp.int32),
            (dc // step,),
            [spec((step, E_F, fl_real), lambda i, sc: (i, 0, 0))],
            spec((E_F, step, fl), lambda i, sc: (0, i, 0)),
            jax.ShapeDtypeStruct((E_F, dc, fl), BF),
                us=9.5,
        )(down_weight)

    la.step()
    tiles = project(h1, h1_x, (wqk_m, wqk_x), 2, 0)
    la.step()
    sent = send_first(tiles)
    dy = join([dy, dy_got], 0)
    dy_got = z_swap(dy, z_bits[1])
    keep = project(h1, h1_x, (wqk_m, wqk_x), 2, 1)
    for b in z_bits[2:]:
        dy = join([dy, dy_got], 0)
        dy_got = z_swap(dy, b)
    dy_all = join([dy, dy_got], 0)
    la.step()

    hot = (route_row[2:4, None, :] == experts[None, :, None]).astype(F32)
    blocks = rows // 128
    hot_b = hot.reshape(2 * E_F, blocks, 128)
    lane = jnp.arange(128)
    tri = (lane[:, None] < lane[None, :]).astype(BF)
    before = jnp.einsum("anl,lm->anm", hot_b.astype(BF), tri, preferred_element_type=F32)
    totals = jnp.sum(hot_b, axis=2)
    lane_b = jnp.arange(blocks)
    tri_b = (lane_b[:, None] < lane_b[None, :]).astype(BF)
    before_b = jnp.dot(totals.astype(BF), tri_b, preferred_element_type=F32)
    rank = (before + before_b[:, :, None]).reshape(2, E_F, rows)
    counts = jnp.sum(totals, axis=1).reshape(2, E_F)
    per_expert = counts[0] + counts[1]
    off = jnp.sum(jnp.where(experts[:, None] > experts[None, :], per_expert[None, :], 0.0), axis=1)
    base = jnp.stack((off, off + counts[0]))
    pos_row = jnp.sum(hot * (base[:, :, None] + rank), axis=1).astype(jnp.int32)
    pos_col = jnp.transpose(pos_row)
    offsets = jnp.concatenate((off, jnp.sum(per_expert)[None])).astype(jnp.int32)

    def start_of(k, other, h):
        return 2 * ts * (2 * (chip ^ k) + (core ^ other)) + h * ts

    def tile_scalars(table):
        ks, others, hs = (jnp.array([[t[i] for t in row] for row in table], jnp.int32) for i in range(3))
        p0 = start_of(ks, others, hs)
        n = p0.shape[1]
        first = jnp.sum((offsets[1:] <= p0[..., None]).astype(jnp.int32), axis=2)
        last = jnp.sum((offsets[1:] <= p0[..., None] + ts - 1).astype(jnp.int32), axis=2)
        count = last - first + 1
        lower = jnp.arange(n)[:, None] >= jnp.arange(n)[None, :]
        upto = jnp.sum(jnp.where(lower, count[:, None, :], 0), axis=2)
        v = jnp.arange(n + E_F - 1, dtype=jnp.int32)
        tile = jnp.minimum(jnp.sum((upto[:, None, :] <= v[:, None]).astype(jnp.int32), axis=2), n - 1)
        mine = tile[:, :, None] == jnp.arange(n)
        begin_v = jnp.sum(jnp.where(mine, (upto - count)[:, None, :], 0), axis=2)
        first_v = jnp.sum(jnp.where(mine, first[:, None, :], 0), axis=2)
        last_v = jnp.sum(jnp.where(mine, last[:, None, :], 0), axis=2)
        e = jnp.minimum(first_v + v - begin_v, last_v)
        kind = jnp.where(v < upto[:, -1:], jnp.where(v == begin_v, 2, 1), 0)
        ends = jnp.broadcast_to(offsets, (len(table), E_F + 1))
        return jnp.concatenate((p0, tile, e, kind, ends), axis=1).astype(jnp.int32)

    proj_scalars = tile_scalars([[(k, 0, h) for k, h in group] for group in groups[:2]])
    all_scalars = tile_scalars([[(k, 0, h) for k, h in groups[2]]]).reshape(-1)
    back_table = [[(k, other, h) for other in range(2) for h in range(2)] for k in range(n_chip)]
    n_pieces = 4 * n_chip
    starts_all = start_of(*(jnp.array([t[i] for row in back_table for t in row], jnp.int32) for i in range(3)))
    weight_scalars = jnp.concatenate((starts_all, offsets))
    proj_length = proj_scalars.shape[1]
    proj_scalars = proj_scalars.reshape(-1)

    def group_proj(xo, xt, wm, wx, g):
        m = wm.shape[2]
        n = len(groups[g])
        steps = n + E_F - 1
        lo = g * proj_length if g < 2 else 0
        parts = 2 if g < 2 else 4
        by_expert = spec((1, dc, m), lambda i, sc: (sc[lo + n + steps + i], 0, 0))
        return launch(
            functools.partial(group_proj_body, n, parts, lo),
            proj_scalars if g < 2 else all_scalars,
            (steps,),
            [spec((2, rows)), spec((rows, dc)), spec((rows, dc)), by_expert, by_expert],
            [spec((n // parts, ts, m))] * parts,
            [jax.ShapeDtypeStruct((n // parts, ts, m), BF)] * parts,
            [pltpu.VMEM((ts, 2 * dc), BF)],
            us=17 if m > fl else 27,
        )(pos_row, xo, xt, wm, wx)

    def sort_t(x):
        return launch(
            sort_t_body,
            starts_all,
            (n_pieces,),
            [spec((2, rows)), spec((rows, dc))],
            spec((dc, ts), lambda i, sc: (0, i)),
            jax.ShapeDtypeStruct((dc, 2 * rows), BF),
            us=13,
        )(pos_row, x)

    if keep[0].shape[0] > 1:
        keep, sent = send_next(keep, sent, 1)
    wd = prep_down()
    wd_x = core_swap(wd)
    dy_x = core_swap(dy_all)
    la.step()
    qkv_parts = finish_reduce(keep, sent, 2)

    s_abs = f ^ chip
    positions = jnp.arange(seq, dtype=jnp.int32)
    my_ends = lax.dynamic_index_in_dim(ends, s_abs, 0, keepdims=False)
    my_starts = my_ends - lax.dynamic_index_in_dim(doc_lengths, s_abs, 0, keepdims=False)
    doc_one = jnp.sum((positions[:, None] >= my_ends).astype(jnp.int32), axis=1)
    begin = jnp.sum(jnp.where(doc_one[:, None] == jnp.arange(DOCS, dtype=jnp.int32), my_starts, 0), axis=1)
    doc_col, doc_row = doc_one[:, None], doc_one[None, :]
    halves = jnp.arange(HD // 2, dtype=F32)
    angles = (positions - begin).astype(F32)[:, None] * (rope_base ** (-2.0 * halves / HD))[None, :]
    cos, sin = jnp.cos(angles), jnp.sin(angles)
    cosf = jnp.concatenate((cos, cos), axis=1)
    sinf = jnp.concatenate((-sin, sin), axis=1)

    qkv, ao, lse = launch(
        functools.partial(attend_body, hc),
        one,
        (1,),
        [spec((half, 4 * width))] * 4 + [spec((seq, 1)), spec((1, seq)), spec((seq, HD)), spec((seq, HD))],
        [spec((seq, 4 * width)), spec((seq, 2 * width)), spec((seq, 128))],
        [
            jax.ShapeDtypeStruct((seq, 4 * width), BF),
            jax.ShapeDtypeStruct((seq, 2 * width), BF),
            jax.ShapeDtypeStruct((seq, 128), F32),
        ],
            us=7,
    )(*qkv_parts, doc_col, doc_row, cosf, sinf)

    ao_m = [ao] + [chip_swap(ao, k) for k in range(1, n_chip)]
    ao_t = [core_swap(ao)]
    wo_m, wo_t, wo_x = split_halves(e_major(output_weight))
    la.step()
    (wg_x,) = hold(wg_x)
    da_all = group_proj(dy_all, dy_x, wd, wd_x, 2)
    da_tiles, da_keep = da_all[:2], da_all[2:]
    ao_m = [ao] + hold(*ao_m[1:])
    ao_t += [core_swap(v) for v in ao_m[1:]]
    pa = gates_of(la.finish(), route_row[0:2])
    pa3 = jnp.transpose(pa).reshape(n_z, seq, 2)

    def into_stream(body, k, streams, vals, weights, buf, us, cols, carry=()):
        sc = jnp.reshape(chip ^ k, (1,))
        by_stream = [spec((pl.squeezed, seq, 2), lambda i, sc: (sc[0], 0, 0))] * len(streams)
        n_in = len(streams) + 2 + len(weights)
        return launch(
            body,
            sc,
            (1,),
            by_stream
            + [spec((seq, cols))] * 2
            + [spec(w.shape) for w in weights]
            + [pl.BlockSpec(memory_space=pl.ANY)],
            spec((1, seq, dc), lambda i, sc: (sc[0], 0, 0)),
            jax.ShapeDtypeStruct((n_z, seq, dc), BF),
            aliases={n_in + 1: 0},
            us=us,
        )(*streams, *vals, *weights, buf, carry=carry)

    buf = jnp.zeros((n_z, seq, dc), BF)
    for k in range(n_chip):
        buf = into_stream(
            functools.partial(att_out_body, width),
            k,
            (att_route3, pa3),
            (ao_m[k], ao_t[k]),
            (wo_m, wo_t),
            buf,
            4.3,
            2 * width,
            da_tiles if k == n_chip - 1 else (),
        )
    buf, *da_tiles = buf
    y1_sent = z_send([buf[k] for k in range(n_z)])
    da_sent = send_first(da_tiles)
    y1, y1_own = z_total(y1_sent, x_own)

    y1_got = z_gather(y1_own)
    y1_f = y1_own.astype(F32)
    stat = jnp.concatenate(
        (
            row_logits(rf, (y1_f * gf).astype(BF)),
            jnp.sum(y1_f * y1_f, axis=1)[None],
            jnp.zeros((7, seq), F32),
        ),
        axis=0,
    )
    stat = Small(stat, "cxg")
    if da_keep[0].shape[0] > 1:
        da_keep, da_sent = send_next(da_keep, da_sent, 1)
    for _ in range(1 + len(chip_bits)):
        stat.step()
    y1_low, yg = join_scaled(y1_got, gf)
    yg_x = (core_swap(y1_low).astype(F32) * gf_t).astype(BF)

    gu_tiles = group_proj(yg, yg_x, wg, wg_x, 0)
    gu_sent = send_first(gu_tiles)
    da_parts = finish_reduce(da_keep, da_sent, 2)
    da_parts = launch(
        pairs_body,
        one,
        (1,),
        [spec((ts, fl))] * 4,
        [spec((ts, fl))] * 2,
        [jax.ShapeDtypeStruct((ts, fl), BF)] * 2,
        us=3,
    )(*da_parts)
    gu_keep = group_proj(yg, yg_x, wg, wg_x, 1)
    stat.step()
    yg_s = sort_t(yg)
    dy_s = sort_t(dy_all)
    if gu_keep[0].shape[0] > 1:
        gu_keep, gu_sent = send_next(gu_keep, gu_sent, 1)
    stat = stat.finish()
    inv2 = lax.rsqrt(stat[8:9] / D + norm_eps)
    lf = stat[0:E_F] * inv2
    pf = gates_of(lf, route_row[2:4])
    rowv = jnp.concatenate((inv2, pf, jnp.zeros((5, rows), F32)), axis=0)
    gu_parts = finish_reduce(gu_keep, gu_sent, 2)

    by_half = lambda n: spec((1, ts, n), lambda h, sc: (h, 0, 0))
    dgu, act, tok_sum = launch(
        functools.partial(middle_body, fl),
        jnp.stack([start_of(0, 0, h) for h in range(2)]),
        (2,),
        [spec((2, rows)), spec((8, rows))] + [spec((ts, 2 * fl))] * 4 + [spec((ts, fl))] * 2,
        [by_half(2 * fl), by_half(fl), spec((8, rows))],
        [
            jax.ShapeDtypeStruct((2, ts, 2 * fl), BF),
            jax.ShapeDtypeStruct((2, ts, fl), BF),
            jax.ShapeDtypeStruct((8, rows), F32),
        ],
            us=13,
    )(pos_row, rowv, *gu_parts, *da_parts)

    def router_back(dgate, gates, route2):
        dlog = gates * (dgate - jnp.sum(gates * dgate, axis=0, keepdims=True))
        return jnp.sum(jnp.where(route2[:, None, :] == experts[None, :, None], dlog[:, None, :], 0.0), axis=0)

    near = list(chip_bits)
    far = [k for k in range(1, n_chip) if k not in near]

    def gather_near(own):
        return {0: own} | {b: chip_swap(own, b) for b in near}

    def gather_far(got):
        result = {}
        for h in range(2):
            have = {k: got[k][h] for k in got}
            seen = orders[h][0]
            for b in orders[h][1:]:
                for k in [k for k in list(have) if k and not k & ~seen]:
                    have[k ^ b] = result[k ^ b, h] = chip_swap(have[k], b)
                seen |= b
        return result

    def whole(v):
        w = core_swap(v)
        return [(v, 0), (v, 1), (w, 0), (w, 1)]

    def apart(got, k):
        mine = [got[k, h] for h in range(2)]
        return [(v, None) for v in mine] + [(core_swap(v), None) for v in mine]

    def arrays_of(pieces):
        arrays, where = [], []
        for v, h in pieces:
            i = next((i for i, u in enumerate(arrays) if u is v), None)
            if i is None:
                i = len(arrays)
                arrays.append(v)
            where.append((i, h))
        return arrays, tuple(where)

    back_groups = ([0], near, far)
    back_scalars = [tile_scalars([[t for k in ks for t in back_table[k]]]).reshape(-1) for ks in back_groups]

    def group_back(g, pieces, w, acc, carry=()):
        m = w.shape[2]
        arrays, where = arrays_of([v for k in back_groups[g] for v in pieces[k]])
        n = len(where)
        steps = n + E_F - 1
        return launch(
            functools.partial(group_back_body, where, 0),
            back_scalars[g],
            (steps,),
            [spec((rows, 2))]
            + [spec(v.shape) for v in arrays]
            + [spec((1, dc, m), lambda i, sc: (sc[n + steps + i], 0, 0)), spec((rows, dc))],
            spec((rows, dc)),
            jax.ShapeDtypeStruct((rows, dc), F32),
            [pltpu.VMEM((n * ts, dc), F32)],
            aliases={3 + len(arrays): 0},
            us=3.4 * n if m > fl else 2.8 * n,
        )(pos_col, *arrays, w, acc, carry=carry)

    def group_weight(xs, pieces, out, out_spec):
        arrays, where = arrays_of([v for k in range(n_chip) for v in pieces[k]])
        m = arrays[0].shape[-1]
        return launch(
            functools.partial(group_weight_body, where, fl),
            weight_scalars,
            (E_F,),
            [spec((dc, 2 * rows))] + [spec(v.shape) for v in arrays],
            out_spec,
            out,
            [pltpu.VMEM((dc, m), F32)],
            us=30 if m > fl else 24,
        )(xs, *arrays)

    dgu_pieces = {0: whole(dgu)}
    act_x = core_swap(act)
    dgu_got = gather_near(dgu)

    tok_sum = Small(rel(tok_sum.reshape(8, n_z, seq).transpose(1, 0, 2)[:, :3]).reshape(n_z * 3, seq), "czx")
    for _ in range(len(z_bits)):
        tok_sum.step()

    dh2 = group_back(0, dgu_pieces, wg, jnp.zeros((rows, dc), F32))
    act_pieces = {0: [(act, 0), (act, 1), (act_x, 0), (act_x, 1)]}
    ffn = group_back(0, act_pieces, wd, jnp.zeros((rows, dc), F32))
    got = hold(*[dgu_got[b] for b in near])
    for b, v in zip(near, got):
        dgu_got[b] = v
        dgu_pieces[b] = whole(v)
    tok_sum.step()
    dgu_far = gather_far({b: dgu_got[b] for b in near})
    dh2, act = group_back(1, dgu_pieces, wg, dh2, carry=(act,))
    act_pieces[0] = [(act, 0), (act, 1), (act_x, 0), (act_x, 1)]
    tok_sum.step()
    dgu_far = dict(zip(dgu_far, hold(*dgu_far.values())))
    for k in far:
        dgu_pieces[k] = apart(dgu_far, k)
    act_got = gather_near(act)
    dh2 = group_back(2, dgu_pieces, wg, dh2)
    dh2_sent = z_send([dh2[k * seq : (k + 1) * seq].astype(BF) for k in range(n_z)])
    gate_up_grad = group_weight(
        yg_s,
        dgu_pieces,
        jax.ShapeDtypeStruct((dc, E_F, 2, fl_real), F32),
        spec((dc, 1, 2, fl_real), lambda e, sc: (0, e, 0, 0)),
    )
    _, dh2 = z_total(dh2_sent)
    dh2_got = z_gather(dh2)
    got = hold(*[act_got[b] for b in near])
    for b, v in zip(near, got):
        act_got[b] = v
        act_pieces[b] = whole(v)
    act_far = gather_far({b: act_got[b] for b in near})
    ffn = group_back(1, act_pieces, wd, ffn)
    act_far = dict(zip(act_far, hold(*act_far.values())))
    for k in far:
        act_pieces[k] = apart(act_far, k)
    tok_sum = rel(tok_sum.finish().reshape(n_z, 3, seq)).transpose(1, 0, 2).reshape(3, rows)
    dlf = router_back(tok_sum[0:2], pf, route_row[2:4])
    m2 = (tok_sum[2:3] + jnp.sum(dlf * lf, axis=0, keepdims=True)) / D
    dlf_inv = (dlf * inv2).astype(BF)
    by_row = lambda n: spec((seq, n), lambda i, sc: (i, 0))
    dy1_low, dh2_own = launch(
        functools.partial(middle_grad_body, n_z),
        jnp.zeros((1,), jnp.int32),
        (n_z,),
        [by_row(dc), by_row(dc), spec((E_F, seq), lambda i, sc: (0, i)), by_row(1), spec((E_F, dc)), spec((1, dc))]
        + [spec((seq, dc))] * n_z,
        [by_row(dc), spec((seq, dc))],
        [jax.ShapeDtypeStruct((rows, dc), BF), jax.ShapeDtypeStruct((seq, dc), F32)],
        us=4,
    )(dy_all, y1_low, dlf_inv, jnp.transpose(m2 * inv2 * inv2), jnp.transpose(rf), gf, *dh2_got)
    dy1_x = core_swap(dy1_low)

    tiles = project(dy1_low, dy1_x, (wo_m, wo_x), 0, 0)
    sent = send_first(tiles)
    keep = project(dy1_low, dy1_x, (wo_m, wo_x), 0, 1)
    if keep[0].shape[0] > 1:
        keep, sent = send_next(keep, sent, 1)

    def att_weight(xt, with_gates, extra, mine, theirs, cols):
        pieces = [v for pair in zip(mine, theirs) for v in pair]
        sc = jnp.concatenate((chip ^ jnp.arange(n_chip, dtype=jnp.int32), core[None]))
        at = lambda i, e, sc: (0, 0, sc[n_chip] ^ i)
        outs = [E_A] + ([2] if extra else [])
        return launch(
            functools.partial(att_weight_body, width, n_chip, with_gates, extra),
            sc,
            (2, E_A),
            [spec(xt.shape), spec((n_z, seq, 2)), spec((n_z, seq, 2))] + [spec((seq, cols))] * len(pieces),
            [spec((dc, n, width), at) for n in outs],
            [jax.ShapeDtypeStruct((dc, n, 2 * width), F32) for n in outs],
            [pltpu.VMEM((n_chip, seq, 2 * width), BF)],
            us=20,
        )(xt, att_route3, pa3, *pieces)

    def stream_t(v):
        return jnp.transpose(v.reshape(n_z, seq, dc), (0, 2, 1))

    ffn = group_back(2, act_pieces, wd, ffn)
    dao_parts = finish_reduce(keep, sent, 2)

    pa_one = lax.dynamic_index_in_dim(pa3, chip, 0, keepdims=False)
    grads, dgate = launch(
        functools.partial(attend_back_body, hc),
        one,
        (1,),
        [spec((half, 2 * width))] * 4
        + [spec((seq, 4 * width)), spec((seq, 2 * width)), spec((seq, 128)), spec((seq, 2))]
        + [spec((seq, 1)), spec((1, seq)), spec((seq, HD)), spec((seq, HD))],
        [spec((seq, 4 * width)), spec((seq, 128))],
        [jax.ShapeDtypeStruct((seq, 4 * width), BF), jax.ShapeDtypeStruct((seq, 128), F32)],
            us=7,
    )(*dao_parts, qkv, ao, lse, pa_one, doc_col, doc_row, cosf, sinf)
    g_m = [grads] + [chip_swap(grads, k) for k in range(1, n_chip)]
    g_t = [core_swap(grads)]
    dpa = jnp.zeros((n_z, 2, seq), F32)
    dpa = lax.dynamic_update_slice(dpa, jnp.transpose(dgate[:, :2])[None], (s_abs, 0, 0))
    dpa = Small(dpa.reshape(n_z * 2, seq), "czx")
    ffn_sent = z_send([ffn[k * seq : (k + 1) * seq].astype(BF) for k in range(n_z)])
    down_grad = group_weight(
        dy_s,
        act_pieces,
        jax.ShapeDtypeStruct((dc, E_F, fl_real), F32),
        spec((dc, E_F, fl_real)),
    )
    ffn = z_total(ffn_sent, y1)[1]
    for _ in range(1 + len(z_bits)):
        dpa.step()
    g_m = [grads] + hold(*g_m[1:])
    dpa.step()
    g_t += [core_swap(v) for v in g_m[1:]]

    def to_rows(v):
        n = v.shape[1] // dc
        v = lax.all_to_all(v.reshape(n_ctx, tok, n * dc), "ctx", 0, 0, tiled=True)
        v = v.reshape(n_ctx, tok, n, dc).transpose(2, 1, 0, 3)
        return v.reshape(n, tok, D)

    buf = jnp.zeros((n_z, seq, dc), BF)
    for k in range(n_chip):
        buf = into_stream(
            functools.partial(att_in_back_body, width),
            k,
            (att_route3,),
            (g_m[k], g_t[k]),
            (wqk_m, wqk_t),
            buf,
            5,
            4 * width,
        )
        if k == 0:
            dpa.finish()
    dpa = lax.dynamic_index_in_dim(dpa.finish().reshape(n_z, 2, seq), f, 0, keepdims=False)
    dh1_sent = z_send([buf[k] for k in range(n_z)])
    query_grad, kv_grad = att_weight(stream_t(h1), False, True, g_m, g_t, 4 * width)
    dh1, _ = z_total(dh1_sent)
    dla = router_back(dpa, pa[:, :seq], route_row[0:2, :seq]).astype(BF)
    dh1 = dh1 + lax.dot_general(dla, ra, (((0,), (1,)), ((), ())), preferred_element_type=F32)
    back_col = jnp.concatenate(((dh1 * ga).astype(BF), dy1_low[:seq]), axis=1)

    back = to_rows(jnp.concatenate((back_col, ffn), axis=1))
    outputs, back = back[2:], back[:2].astype(F32)
    input_grad = back[1] + inv1_loc * (back[0] - n1_loc * jnp.mean(back[0] * n1_loc, axis=1, keepdims=True))
    input_grad = input_grad.astype(BF)[None]

    mark(back_col)
    (output_grad,) = att_weight(stream_t(dy1_low), True, False, ao_m, ao_t, 2 * width)

    own = slice(0, seq)
    tail = jnp.concatenate(
        (
            jnp.dot(dla, h1[own], preferred_element_type=F32),
            jnp.dot(dlf_inv[:, own], yg[own], preferred_element_type=F32),
            jnp.sum(dh1 * n1_own.astype(F32), axis=0, keepdims=True),
            jnp.sum(dh2_own * y1_f, axis=0, keepdims=True),
            jnp.zeros((6, dc), F32),
        ),
        axis=0,
    )
    tail = Small(tail, "z").finish()
    att_router_grad = jnp.transpose(tail[0:E_A])
    ffn_router_grad = jnp.transpose(tail[E_A : E_A + E_F])
    att_gain_grad = tail[E_A + E_F]
    ffn_gain_grad = tail[E_A + E_F + 1]

    return (
        outputs,
        input_grad,
        kv_grad,
        query_grad,
        output_grad,
        att_router_grad,
        att_gain_grad,
        gate_up_grad,
        down_grad,
        ffn_router_grad,
        ffn_gain_grad,
    )


def solution(mesh):
    in_specs = (
        P("fsdp", "ctx", None),
        P("fsdp", "ctx", None),
        P(),
        P("ctx", None, None),
        P("ctx", None, None),
        P("ctx", None, "fsdp"),
        P("ctx", None, "fsdp"),
        P("ctx", None, "fsdp"),
        P("ctx", None),
        P("ctx"),
        P("ctx", None, None, "fsdp"),
        P("ctx", None, "fsdp"),
        P("ctx", None),
        P("ctx"),
    )
    out_specs = (
        P("fsdp", "ctx", None),
        P("fsdp", "ctx", None),
        P("ctx", None, "fsdp"),
        P("ctx", None, "fsdp"),
        P("ctx", None, "fsdp"),
        P("ctx", None),
        P("ctx"),
        P("ctx", None, None, "fsdp"),
        P("ctx", None, "fsdp"),
        P("ctx", None),
        P("ctx"),
    )
    return jax.shard_map(
        per_device, mesh=mesh, in_specs=in_specs, out_specs=out_specs, check_vma=False
    )
```

```python
import functools

import jax
import jax.numpy as jnp
from jax import lax
from jax.experimental import pallas as pl
from jax.experimental.pallas import tpu as pltpu
from jax.sharding import PartitionSpec as P

D = 2048
HEADS = 16
HD = 128
E_A = 8
E_F = 8
FF = 5632
DOCS = 3

norm_eps = 1e-06
rope_base = 10000.0
masked_score = -1e30

BF = jnp.bfloat16
F32 = jnp.float32
VMEM_CAP = 60 * 1024 * 1024
PER_US = 1.1e9


def dot(a, b):
    return lax.dot_general(a, b, (((1,), (0,)), ((), ())), preferred_element_type=F32)


def dot_nt(a, b):
    return lax.dot_general(a, b, (((1,), (1,)), ((), ())), preferred_element_type=F32)


def dot_tn(a, b):
    return lax.dot_general(a, b, (((0,), (0,)), ((), ())), preferred_element_type=F32)


def spec(shape, index=None):
    if index is not None:
        return pl.BlockSpec(shape, index)
    zeros = (0,) * len(shape)
    return pl.BlockSpec(shape, lambda *_: zeros, pipeline_mode=pl.Buffered(1))


def call(chain, body, sc, grid, in_specs, out_specs, out_shape, scratch=(), aliases=None, us=5):
    single = not isinstance(out_shape, (list, tuple))
    out_specs, out_shape = ([out_specs], [out_shape]) if single else (list(out_specs), list(out_shape))
    out_specs = [pl.BlockSpec(v.block_shape, v.index_map) for v in out_specs]
    anywhere = pl.BlockSpec(memory_space=pl.ANY)

    def go(*operands, carry=()):
        waits = [v for v in chain if not any(v is u for u in operands) and not any(v is u for u in carry)]
        n_in, n_extra, n_out, n_carry = len(operands), len(waits) + len(carry), len(out_shape), len(carry)

        def kernel_body(first, *refs):
            outs = refs[n_in + n_extra :]
            body(first, *refs[:n_in], *outs[:n_out], *outs[n_out + n_carry :])

        alias = dict(aliases or {})
        for i in range(n_carry):
            alias[1 + n_in + len(waits) + i] = n_out + i
        out = pl.pallas_call(
            kernel_body,
            out_shape=out_shape + [jax.ShapeDtypeStruct(v.shape, v.dtype) for v in carry],
            grid_spec=pltpu.PrefetchScalarGridSpec(
                num_scalar_prefetch=1,
                grid=grid,
                in_specs=list(in_specs) + [anywhere] * n_extra,
                out_specs=out_specs + [anywhere] * n_carry,
                scratch_shapes=list(scratch),
            ),
            input_output_aliases=alias,
            compiler_params=pltpu.CompilerParams(
                dimension_semantics=("arbitrary",) * len(grid), vmem_limit_bytes=VMEM_CAP
            ),
            cost_estimate=pl.CostEstimate(flops=int(us * PER_US), bytes_accessed=0, transcendentals=0),
        )(sc, *operands, *waits, *carry)
        chain[:] = out[:1]
        result = out[0] if single else out[:n_out]
        return (result, *out[n_out:]) if carry else result

    return go


def proj_body(n_extra, width, n, sc, route, xo, xt, *refs):
    wm, wt = refs[0], refs[1]
    outs, tile = refs[-3:-1], refs[-1]
    a, b = xo[...], xt[...]
    r0, r1 = route[:, 0:1], route[:, 1:2]
    acc0 = jnp.zeros((a.shape[0], width), F32)
    acc1 = acc0
    for e in range(E_A):
        r = dot(a, wm[e]) + dot(b, wt[e])
        acc0 = jnp.where(r0 == e, r, acc0)
        acc1 = jnp.where(r1 == e, r, acc1)
    tile[:, 0:width] = acc0.astype(BF)
    tile[:, width : 2 * width] = acc1.astype(BF)
    for i in range(n_extra):
        r = dot(a, wm[E_A + i]) + dot(b, wt[E_A + i])
        tile[:, (2 + i) * width : (3 + i) * width] = r.astype(BF)
    for i in range(n):

        @pl.when(pl.program_id(0) == i)
        def _():
            outs[i // (n // 2)][i % (n // 2)] = tile[...]


def rotate(u, cosf, sinf):
    return u * cosf + pltpu.roll(u, HD // 2, 1) * sinf


def unrotate(u, cosf, sinf):
    return u * cosf - pltpu.roll(u, HD // 2, 1) * sinf


def add_halves(refs):
    a0, a1, b0, b1 = refs
    top = a0[...].astype(F32) + a1[...].astype(F32)
    low = b0[...].astype(F32) + b1[...].astype(F32)
    return jnp.concatenate((top, low), axis=0)


def allowed_pairs(doc_col, doc_row):
    n = doc_col.shape[0]
    t = lax.broadcasted_iota(jnp.int32, (n, n), 0)
    u = lax.broadcasted_iota(jnp.int32, (n, n), 1)
    return (doc_col[...] == doc_row[...]) & (u <= t) & (doc_col[...] < DOCS)


def attend_body(hc, sc, a0, a1, b0, b1, doc_col, doc_row, cosr, sinr, qkv, out, lse):
    width = hc * HD
    u = add_halves((a0, a1, b0, b1))
    cosf, sinf = cosr[...], sinr[...]
    ok = allowed_pairs(doc_col, doc_row)
    for h in range(hc):
        at = 2 * width + h * HD
        k = rotate(u[:, at : at + HD], cosf, sinf).astype(BF)
        v = u[:, at + width : at + width + HD].astype(BF)
        qkv[:, at : at + HD] = k
        qkv[:, at + width : at + width + HD] = v
        for j in range(2):
            lo = j * width + h * HD
            q = rotate(u[:, lo : lo + HD], cosf, sinf).astype(BF)
            qkv[:, lo : lo + HD] = q
            s = jnp.where(ok, dot_nt(q, k) * (HD**-0.5), masked_score)
            m = jnp.max(s, axis=1, keepdims=True)
            p = jnp.where(ok, jnp.exp(s - m), 0.0)
            total = jnp.sum(p, axis=1, keepdims=True)
            total = jnp.where(total > 0, total, 1.0)
            out[:, lo : lo + HD] = (dot(p.astype(BF), v) / total).astype(BF)
            lse[:, 2 * h + j : 2 * h + j + 1] = m + jnp.log(total)


def attend_back_body(hc, sc, a0, a1, b0, b1, qkv, att, lse, gates, doc_col, doc_row, cosr, sinr, grads, dgate):
    width = hc * HD
    u = add_halves((a0, a1, b0, b1))
    cosf, sinf = cosr[...], sinr[...]
    ok = allowed_pairs(doc_col, doc_row)
    keep = (doc_col[...] < DOCS).astype(F32)
    dg = [jnp.zeros((u.shape[0], 1), F32) for _ in range(2)]
    for h in range(hc):
        at = 2 * width + h * HD
        k = qkv[:, at : at + HD]
        v = qkv[:, at + width : at + width + HD]
        dk = jnp.zeros((u.shape[0], HD), F32)
        dv = dk
        for j in range(2):
            lo = j * width + h * HD
            q = qkv[:, lo : lo + HD]
            o = att[:, lo : lo + HD].astype(F32)
            raw = u[:, lo : lo + HD]
            dg[j] = dg[j] + jnp.sum(raw * o, axis=1, keepdims=True)
            do = (raw * (gates[:, j : j + 1] * keep)).astype(BF)
            delta = jnp.sum(do.astype(F32) * o, axis=1, keepdims=True)
            s = dot_nt(q, k) * (HD**-0.5)
            p = jnp.where(ok, jnp.exp(s - lse[:, 2 * h + j : 2 * h + j + 1]), 0.0)
            ds = (p * (dot_nt(do, v) - delta)).astype(BF)
            dq = dot(ds, k) * (HD**-0.5)
            grads[:, lo : lo + HD] = unrotate(dq, cosf, sinf).astype(BF)
            dk = dk + dot_tn(ds, q)
            dv = dv + dot_tn(p.astype(BF), do)
        grads[:, at : at + HD] = unrotate(dk * (HD**-0.5), cosf, sinf).astype(BF)
        grads[:, at + width : at + width + HD] = dv.astype(BF)
    dgate[...] = jnp.zeros_like(dgate)
    dgate[:, 0:1] = dg[0]
    dgate[:, 1:2] = dg[1]


def chosen(hot0, hot1, a, b, e):
    return a * hot0[e] + b * hot1[e]


def one_hots(route):
    return [[jnp.where(route[:, j : j + 1] == e, 1.0, 0.0).astype(BF) for e in range(E_A)] for j in range(2)]


def gated(vals, gates, width):
    a = (vals[:, 0:width].astype(F32) * gates[:, 0:1]).astype(BF)
    b = (vals[:, width : 2 * width].astype(F32) * gates[:, 1:2]).astype(BF)
    return a, b


def att_out_body(width, sc, route, gates, om, ot, wm, wt, prev, out):
    acc = jnp.zeros(out.shape[1:], F32)
    hot0, hot1 = one_hots(route)
    am, bm = gated(om, gates, width)
    at, bt = gated(ot, gates, width)
    for e in range(E_A):
        acc += dot_nt(chosen(hot0, hot1, am, bm, e), wm[e])
        acc += dot_nt(chosen(hot0, hot1, at, bt, e), wt[e])
    out[0] = acc.astype(BF)


def att_in_back_body(width, sc, route, gm, gt, wm, wt, prev, out):
    acc = jnp.zeros(out.shape[1:], F32)
    hot0, hot1 = one_hots(route)
    am, bm = gm[:, 0:width], gm[:, width : 2 * width]
    at, bt = gt[:, 0:width], gt[:, width : 2 * width]
    for e in range(E_A):
        acc += dot_nt(chosen(hot0, hot1, am, bm, e), wm[e])
        acc += dot_nt(chosen(hot0, hot1, at, bt, e), wt[e])
    for i in range(2):
        lo = (2 + i) * width
        acc += dot_nt(gm[:, lo : lo + width], wm[E_A + i]) + dot_nt(gt[:, lo : lo + width], wt[E_A + i])
    out[0] = acc.astype(BF)


def att_weight_body(width, n, with_gates, extra, sc, *refs):
    xt, route, gates = refs[0], refs[1], refs[2]
    pieces = refs[3 : 3 + 2 * n]
    out = refs[3 + 2 * n]
    out2 = refs[4 + 2 * n] if extra else None
    vals = refs[-1]
    seq = route.shape[1]
    half = pl.program_id(0)
    e = pl.program_id(1)
    for side in range(2):

        @pl.when((half == side) & (e == 0))
        def _():
            for k in range(n):
                piece = pieces[2 * k + side]
                if with_gates:
                    a, b = gated(piece, gates[sc[k]], width)
                else:
                    a, b = piece[:, 0:width], piece[:, width : 2 * width]
                vals[k, :, 0:width] = a
                vals[k, :, width : 2 * width] = b
            if extra:
                for i in range(2):
                    lo = (2 + i) * width
                    acc = jnp.zeros((xt.shape[1], width), F32)
                    for k in range(n):
                        acc += dot(xt[sc[k]], pieces[2 * k + side][:, lo : lo + width])
                    out2[:, i, :] = acc

    acc = jnp.zeros((xt.shape[1], width), F32)
    for k in range(n):
        r = route[sc[k]]
        hot0 = jnp.where(r[:, 0:1] == e, 1.0, 0.0).astype(BF)
        hot1 = jnp.where(r[:, 1:2] == e, 1.0, 0.0).astype(BF)
        sel = vals[k, :, 0:width] * hot0 + vals[k, :, width : 2 * width] * hot1
        acc += dot(xt[sc[k]], sel)
    for i in range(E_A):

        @pl.when(e == i)
        def _():
            out[:, i, :] = acc


def row_chunks(rows):
    step = min(rows, 1024)
    return [(i, step) for i in range(0, rows, step)]


def group_proj_body(n, parts, base, sc, pos, xo, xt, wm, wt, *refs):
    outs, xs = refs[:parts], refs[parts]
    i = pl.program_id(0)
    steps = pl.num_programs(0)
    ts = outs[0].shape[1]
    dc = xo.shape[1]
    at = base + n + i
    tile, e, kind = sc[at], sc[at + steps], sc[at + 2 * steps]
    p0 = sc[base + tile]

    @pl.when(kind == 2)
    def _():
        a = jnp.zeros((ts, dc), F32)
        b = a
        for lo, m in row_chunks(xo.shape[0]):
            ids = p0 + lax.broadcasted_iota(jnp.int32, (ts, m), 0)
            hot = (pos[0:1, lo : lo + m] == ids) | (pos[1:2, lo : lo + m] == ids)
            hot = jnp.where(hot, 1.0, 0.0).astype(BF)
            a = a + dot(hot, xo[lo : lo + m, :])
            b = b + dot(hot, xt[lo : lo + m, :])
        xs[:, 0:dc] = a.astype(BF)
        xs[:, dc : 2 * dc] = b.astype(BF)

    rows = p0 + lax.broadcasted_iota(jnp.int32, (ts, 1), 0)
    for t in range(n):
        out, at = outs[t // (n // parts)], t % (n // parts)

        @pl.when((kind == 2) & (tile == t))
        def _():
            out[at] = (dot(xs[:, 0:dc], wm[0]) + dot(xs[:, dc : 2 * dc], wt[0])).astype(BF)

        @pl.when((kind == 1) & (tile == t))
        def _():
            r = dot(xs[:, 0:dc], wm[0]) + dot(xs[:, dc : 2 * dc], wt[0])
            out[at] = jnp.where(rows >= sc[base + n + 3 * steps + e], r, out[at].astype(F32)).astype(BF)


def middle_body(fl, sc, pos, rowv, *refs):
    gu, da = refs[0:4], refs[4:6]
    dgu, act, tok = refs[6:]
    ts = gu[0].shape[0]
    rows = pos.shape[1]
    half = pl.program_id(0)
    p0 = sc[half]
    inv = jnp.zeros((ts, 1), F32)
    gate = inv
    for lo, n in row_chunks(rows):
        ids = p0 + lax.broadcasted_iota(jnp.int32, (ts, n), 0)
        is0 = pos[0:1, lo : lo + n] == ids
        is1 = pos[1:2, lo : lo + n] == ids
        inv += jnp.sum(jnp.where(is0 | is1, rowv[0:1, lo : lo + n], 0.0), axis=1, keepdims=True)
        picked = jnp.where(is0, rowv[1:2, lo : lo + n], jnp.where(is1, rowv[2:3, lo : lo + n], 0.0))
        gate += jnp.sum(picked, axis=1, keepdims=True)

    def work(g0, g1, d):
        dpf = jnp.zeros((ts, 128), F32)
        dn = dpf
        step = 128
        for lo in range(0, fl, step):
            gt = (g0[:, lo : lo + step].astype(F32) + g1[:, lo : lo + step].astype(F32)) * inv
            up = (g0[:, fl + lo : fl + lo + step].astype(F32) + g1[:, fl + lo : fl + lo + step].astype(F32)) * inv
            raw = d[:, lo : lo + step].astype(F32)
            sg = 1.0 / (1.0 + jnp.exp(-gt))
            silu = gt * sg
            a = silu * up
            act[0, :, lo : lo + step] = (a * gate).astype(BF)
            da = raw * gate
            dgt = da * up * (sg + silu * (1.0 - sg))
            dup = da * silu
            dgu[0, :, lo : lo + step] = (dgt * inv).astype(BF)
            dgu[0, :, fl + lo : fl + lo + step] = (dup * inv).astype(BF)
            dpf += raw * a
            dn += dgt * gt + dup * up
        dpf = jnp.sum(dpf, axis=1, keepdims=True)
        dn = jnp.sum(dn, axis=1, keepdims=True)
        for lo, n in row_chunks(rows):
            ids = p0 + lax.broadcasted_iota(jnp.int32, (ts, n), 0)
            is0 = pos[0:1, lo : lo + n] == ids
            is1 = pos[1:2, lo : lo + n] == ids
            t0 = jnp.sum(jnp.where(is0, dpf, 0.0), axis=0, keepdims=True)
            t1 = jnp.sum(jnp.where(is1, dpf, 0.0), axis=0, keepdims=True)
            t2 = jnp.sum(jnp.where(is0 | is1, dn, 0.0), axis=0, keepdims=True)
            new = jnp.concatenate((t0, t1, t2, jnp.zeros((5, n), F32)), axis=0)
            tok[:, lo : lo + n] = new + jnp.where(half == 0, 0.0, tok[:, lo : lo + n])

    for h in range(2):

        @pl.when(half == h)
        def _():
            work(*gu[2 * h : 2 * h + 2], da[h])


def piece_of(arrays, place):
    i, h = place
    return arrays[i][...] if h is None else arrays[i][h]


def group_back_body(where, base, sc, posc, *refs):
    n = len(where)
    arrays, (w, prev, out, dh) = refs[:-4], refs[-4:]
    i = pl.program_id(0)
    steps = pl.num_programs(0)
    ts = dh.shape[0] // n
    at = base + n + i
    tile, e, kind = sc[at], sc[at + steps], sc[at + 2 * steps]
    p0 = sc[base + tile]
    rows = p0 + lax.broadcasted_iota(jnp.int32, (ts, 1), 0)
    for t in range(n):

        @pl.when((kind == 2) & (tile == t))
        def _():
            dh[t * ts : (t + 1) * ts, :] = dot_nt(piece_of(arrays, where[t]), w[0])

        @pl.when((kind == 1) & (tile == t))
        def _():
            r = dot_nt(piece_of(arrays, where[t]), w[0])
            old = dh[t * ts : (t + 1) * ts, :]
            dh[t * ts : (t + 1) * ts, :] = jnp.where(rows >= sc[base + n + 3 * steps + e], r, old)

    @pl.when(i == steps - 1)
    def _():
        for lo, m in row_chunks(out.shape[0]):
            acc = prev[lo : lo + m, :]
            for t in range(n):
                ids = sc[base + t] + lax.broadcasted_iota(jnp.int32, (m, ts), 1)
                hot = (posc[lo : lo + m, 0:1] == ids) | (posc[lo : lo + m, 1:2] == ids)
                acc = acc + dot(jnp.where(hot, 1.0, 0.0).astype(BF), dh[t * ts : (t + 1) * ts, :].astype(BF))
            out[lo : lo + m, :] = acc


def sort_t_body(sc, pos, x, out):
    p0 = sc[pl.program_id(0)]
    ts = out.shape[1]
    acc = jnp.zeros((ts, x.shape[1]), F32)
    for lo, m in row_chunks(x.shape[0]):
        ids = p0 + lax.broadcasted_iota(jnp.int32, (ts, m), 0)
        hot = (pos[0:1, lo : lo + m] == ids) | (pos[1:2, lo : lo + m] == ids)
        acc += dot(jnp.where(hot, 1.0, 0.0).astype(BF), x[lo : lo + m, :])
    out[...] = jnp.transpose(acc).astype(BF)


def group_weight_body(where, fl, sc, xs, *refs):
    n = len(where)
    arrays, (out, acc) = refs[:-2], refs[-2:]
    ts = xs.shape[1] // n
    e = pl.program_id(0)
    lo, hi = sc[n + e], sc[n + e + 1]
    acc[...] = jnp.zeros_like(acc)
    for i in range(n):
        p0 = sc[i]

        @pl.when((p0 < hi) & (p0 + ts > lo))
        def _():
            ids = p0 + lax.broadcasted_iota(jnp.int32, (1, ts), 1)
            ok = jnp.where((ids >= lo) & (ids < hi), 1.0, 0.0).astype(BF)
            acc[...] += dot(xs[:, i * ts : (i + 1) * ts] * ok, piece_of(arrays, where[i]))

    if len(out.shape) == 4:
        real = out.shape[3]
        out[:, 0, 0, :] = acc[:, 0:real]
        out[:, 0, 1, :] = acc[:, fl : fl + real]
    else:
        for i in range(E_F):

            @pl.when(e == i)
            def _():
                out[:, i, :] = acc[:, 0 : out.shape[2]]


def hold_body(sc, out):
    out[...] = jnp.zeros_like(out)


def add_body(sc, x, got, out):
    out[...] = x[...] + got[...]


def join_body(axis, n, sc, *refs):
    size = refs[0].shape[axis]
    for k in range(n):
        if axis:
            refs[n][:, k * size : (k + 1) * size] = refs[k][...]
        else:
            refs[n][k * size : (k + 1) * size, :] = refs[k][...]


def join_scaled_body(n, sc, gain, *refs):
    size = refs[0].shape[0]
    for k in range(n):
        v = refs[k][...]
        refs[n][k * size : (k + 1) * size, :] = v
        refs[n + 1][k * size : (k + 1) * size, :] = (v.astype(F32) * gain[...]).astype(BF)


def pairs_body(sc, a0, a1, b0, b1, a, b):
    a[...] = (a0[...].astype(F32) + a1[...].astype(F32)).astype(BF)
    b[...] = (b0[...].astype(F32) + b1[...].astype(F32)).astype(BF)


def total_body(n, sc, *refs):
    total = refs[0][...].astype(F32)
    for v in refs[1:n]:
        total = total + v[...].astype(F32)
    refs[n][...] = total
    refs[n + 1][...] = total.astype(BF)


def step_body(sc, *refs):
    for h in range(2):
        refs[4 + h][...] = (refs[2 * h][...].astype(F32) + refs[2 * h + 1][...].astype(F32)).astype(BF)


def middle_grad_body(n, sc, dy, y1, dlf, coef, rf, gf, *refs):
    i = pl.program_id(0)
    dy1, dh2 = refs[n:]
    router = dot_tn(dlf[...], rf[...])

    def work(part):
        total = part[...].astype(F32) + router
        dy1[...] = (dy[...].astype(F32) + total * gf[...] - y1[...].astype(F32) * coef[...]).astype(BF)

        @pl.when(i == 0)
        def _():
            dh2[...] = total

    for k in range(n):

        @pl.when(i == k)
        def _():
            work(refs[k])


def prep_gate_up_body(fl, sc, w, out):
    real = w.shape[3]
    for e in range(E_F):
        for j in range(2):
            out[e, :, j * fl : j * fl + real] = w[:, e, j, :].astype(BF)
            if real != fl:
                out[e, :, j * fl + real : (j + 1) * fl] = jnp.zeros((w.shape[0], fl - real), BF)


def prep_down_body(fl, sc, w, out):
    real = w.shape[2]
    out[:, :, 0:real] = jnp.swapaxes(w[...].astype(BF), 0, 1)
    if real != fl:
        out[:, :, real:fl] = jnp.zeros((E_F, w.shape[0], fl - real), BF)


def per_device(
    inputs,
    cotangent,
    doc_lengths,
    att_routes,
    ffn_routes,
    kv_weight,
    query_weight,
    output_weight,
    att_router,
    att_gain,
    gate_up_weight,
    down_weight,
    ffn_router,
    ffn_gain,
):
    n_ctx = lax.axis_size("ctx")
    n_z = lax.axis_size("fsdp")
    c = lax.axis_index("ctx")
    f = lax.axis_index("fsdp")
    n_chip = n_ctx // 2
    chip, core = c // 2, c % 2
    tok = inputs.shape[1]
    seq = tok * n_ctx
    dc = D // n_ctx
    rows = n_z * seq
    hc = HEADS // n_z // 2
    width = hc * HD
    half = seq // 2
    fl_real = FF // n_z
    fl = -(-fl_real // 128) * 128
    ts = 2 * rows // n_ctx // 2
    assert n_chip == n_z

    chain = []
    launch = functools.partial(call, chain)

    def swap(x, axis, k, n):
        return lax.ppermute(x, axis, [(i, i ^ k) for i in range(n)])

    def core_swap(x):
        return swap(x, "ctx", 1, n_ctx)

    def chip_swap(x, k):
        return swap(x, "ctx", 2 * k, n_ctx)

    def z_swap(x, k):
        return swap(x, "fsdp", k, n_z)

    chip_bits = [1 << i for i in range(n_chip.bit_length() - 1)]
    z_bits = [1 << i for i in range(n_z.bit_length() - 1)]

    def z_gather(x):
        return [x] + [z_swap(x, k) for k in range(1, n_z)]

    def z_send(pieces):
        return [pieces[0]] + [z_swap(pieces[k], k) for k in range(1, n_z)]

    def z_total(got, *others):
        got = [*got, *others]
        return launch(
            functools.partial(total_body, len(got)),
            jnp.zeros((1,), jnp.int32),
            (1,),
            [spec((seq, dc))] * len(got),
            [spec((seq, dc))] * 2,
            [jax.ShapeDtypeStruct((seq, dc), F32), jax.ShapeDtypeStruct((seq, dc), BF)],
            us=1.5,
        )(*got)

    def mark(*values):
        chain.extend(values)

    one = jnp.zeros((1,), jnp.int32)
    always = doc_lengths[0, 0] > 0

    def window(work, *args):
        outer = list(chain)

        def inside(tokens, args):
            chain[:] = tokens
            return work(*args)

        shapes = jax.eval_shape(inside, outer, args)
        nothing = lambda tokens, args: jax.tree.map(lambda v: jnp.zeros(v.shape, v.dtype), shapes)
        out = lax.cond(always, inside, nothing, outer, args)
        chain[:] = jax.tree.leaves(out)[:1]
        return out

    def hold(*vals):
        out = launch(
            hold_body, one, (1,), [], spec((8, 128)), jax.ShapeDtypeStruct((8, 128), F32), us=0.5
        )(carry=vals)
        return list(out[1:])

    def join(vals, axis):
        m, n = vals[0].shape
        shape = (m, len(vals) * n) if axis else (len(vals) * m, n)
        return launch(
            functools.partial(join_body, axis, len(vals)),
            one,
            (1,),
            [spec((m, n))] * len(vals),
            spec(shape),
            jax.ShapeDtypeStruct(shape, vals[0].dtype),
            us=1.5,
        )(*vals)

    def join_scaled(vals, gain):
        m, n = vals[0].shape
        shape = (len(vals) * m, n)
        return launch(
            functools.partial(join_scaled_body, len(vals)),
            one,
            (1,),
            [spec((1, n))] + [spec((m, n))] * len(vals),
            [spec(shape)] * 2,
            [jax.ShapeDtypeStruct(shape, BF)] * 2,
            us=2,
        )(gain, *vals)

    class Small:
        def __init__(self, x, hops):
            self.x = x
            self.todo = [
                (kind, b)
                for kind in hops
                for b in {"c": [1], "x": [2 * b for b in chip_bits], "z": z_bits, "g": z_bits}[kind]
            ]
            self.send()

        def send(self):
            kind, b = self.todo[0]
            axis, n = ("ctx", n_ctx) if kind in "cx" else ("fsdp", n_z)
            self.got = swap(self.x, axis, b, n)

        def step(self):
            if not self.todo:
                return
            kind, _ = self.todo.pop(0)
            if kind == "g":
                self.x = join([self.x, self.got], 1)
            else:
                m = self.x.shape
                self.x = launch(
                    add_body,
                    one,
                    (1,),
                    [spec(m)] * 2,
                    spec(m),
                    jax.ShapeDtypeStruct(m, F32),
                    us=0.5,
                )(self.x, self.got)
            if self.todo:
                self.send()

        def finish(self):
            while self.todo:
                self.step()
            return self.x

    orders = (chip_bits, chip_bits[::-1])

    def kept(order):
        ks = [0]
        for b in reversed(order[1:]):
            ks = ks + [k ^ b for k in ks]
        return ks

    late = [(k, h) for h in range(2) for k in kept(orders[h])]
    early = [(k ^ orders[h][0], h) for k, h in late]
    groups = (early, late, early + late)

    def send_first(tiles):
        return [chip_swap(tiles[h], orders[h][0]) for h in range(2)]

    def send_next(keep, got, step):
        n, m, cols = keep[0].shape

        def add(first):
            some = spec((1, m, cols), lambda i, sc: (i + first, 0, 0))
            part = spec((1, m, cols), lambda i, sc: (i, 0, 0))
            return launch(
                step_body,
                one,
                (n // 2,),
                [some] * 4,
                [part] * 2,
                [jax.ShapeDtypeStruct((n // 2, m, cols), BF)] * 2,
                us=n * m * cols * 4e-6,
            )(keep[0], got[0], keep[1], got[1])

        left = add(n // 2)
        sent = [chip_swap(left[h], orders[h][step]) for h in range(2)]
        return add(0), sent

    def finish_reduce(keep, got, step):
        while keep[0].shape[0] > 1:
            keep, got = send_next(keep, got, step)
            step += 1
        return [v[0] for h in range(2) for v in (keep[h], got[h])]

    def rel(x):
        return jnp.take(x, f ^ jnp.arange(n_z, dtype=jnp.int32), axis=0)

    x_loc = inputs[0].astype(F32)
    ends = jnp.cumsum(doc_lengths, axis=1)
    my_pos = c * tok + jnp.arange(tok, dtype=jnp.int32)
    my_ends = lax.dynamic_slice_in_dim(ends, f, 1, 0)
    my_keep = (my_pos < my_ends[0, DOCS - 1]).astype(F32)[:, None]
    inv1_loc = lax.rsqrt(jnp.mean(x_loc * x_loc, axis=1, keepdims=True) + norm_eps)
    n1_loc = x_loc * inv1_loc
    dy_loc = cotangent[0].astype(F32) * my_keep
    payload = jnp.stack((n1_loc.astype(BF), dy_loc.astype(BF), inputs[0]), axis=1)
    payload = payload.reshape(tok, 3, n_ctx, dc).transpose(2, 0, 1, 3).reshape(n_ctx, tok, 3 * dc)
    def split_halves(w):
        mine = lax.dynamic_slice_in_dim(w, core * width, width, 2)
        theirs = lax.dynamic_slice_in_dim(w, (1 - core) * width, width, 2)
        return mine, theirs, core_swap(theirs)

    def e_major(w):
        return jnp.transpose(w.astype(BF), (1, 0, 2))

    payload = lax.all_to_all(payload, "ctx", 0, 0, tiled=True).reshape(seq, 3 * dc)
    qk_weight = jnp.concatenate((e_major(query_weight), e_major(kv_weight)), axis=0)
    routes = jnp.concatenate((att_routes, ffn_routes), axis=2)[None]
    for b in [1] + [2 * v for v in chip_bits]:
        routes = jnp.concatenate((routes, swap(routes, "ctx", b, n_ctx)), axis=0)
    routes = jnp.take(routes, c ^ jnp.arange(n_ctx, dtype=jnp.int32), axis=0).reshape(seq, n_z, 4)
    small = jnp.concatenate((att_gain[None], ffn_gain[None]), axis=0).astype(BF)
    small_t = core_swap(small).astype(F32)
    small = small.astype(F32)
    wqk_m, wqk_t, wqk_x = split_halves(qk_weight)
    n1_own, dy_own, x_own = payload[:, :dc], payload[:, dc : 2 * dc], payload[:, 2 * dc :]

    routes = rel(jnp.transpose(routes, (1, 0, 2))).reshape(rows, 4)
    route_row = jnp.transpose(routes)
    att_route3 = routes[:, :2].reshape(n_z, seq, 2)
    experts = jnp.arange(E_F, dtype=jnp.int32)

    ga, gf, ga_t, gf_t = small[0:1], small[1:2], small_t[0:1], small_t[1:2]
    ra, rf = att_router.astype(BF), ffn_router.astype(BF)

    def row_logits(router, hidden):
        return lax.dot_general(router, hidden, (((0,), (1,)), ((), ())), preferred_element_type=F32)

    def gates_of(logits, route2):
        picked = jnp.sum(jnp.where(route2[:, None, :] == experts[None, :, None], logits[None], 0.0), axis=1)
        return jax.nn.softmax(picked, axis=0)

    la = Small(row_logits(ra, (n1_own.astype(F32) * ga).astype(BF)), "cxg")
    step = 32

    def first_window(n1_own, dy_own, gate_up_weight):
        n1 = z_gather(n1_own)
        dy_got = z_swap(dy_own, z_bits[0])
        wg = launch(
            functools.partial(prep_gate_up_body, fl),
            jnp.zeros((1,), jnp.int32),
            (dc // step,),
            [spec((step, E_F, 2, fl_real), lambda i, sc: (i, 0, 0, 0))],
            spec((E_F, step, 2 * fl), lambda i, sc: (0, i, 0)),
            jax.ShapeDtypeStruct((E_F, dc, 2 * fl), BF),
            us=26,
        )(gate_up_weight)
        n1, h1 = join_scaled(n1, ga)
        return n1, h1, join([dy_own, dy_got], 0), wg

    mark(routes, wqk_x, small_t)
    n1, h1, dy, wg = window(first_window, n1_own, dy_own, gate_up_weight)
    n1_t = core_swap(n1)
    wg_x = core_swap(wg)
    h1_x = (n1_t.astype(F32) * ga_t).astype(BF)
    def project(xo, xt, weights, n_extra, g):
        cols = (2 + n_extra) * width
        group = groups[g]
        n = len(group)
        at = lambda i, sc: (sc[i], 0)
        return launch(
            functools.partial(proj_body, n_extra, width, n),
            jnp.stack([2 * (chip ^ k) + h for k, h in group]),
            (n,),
            [spec((half, 4), at), spec((half, dc), at), spec((half, dc), at)] + [spec(w.shape) for w in weights],
            [spec((n // 2, half, cols))] * 2,
            [jax.ShapeDtypeStruct((n // 2, half, cols), BF)] * 2,
            [pltpu.VMEM((half, cols), BF)],
            us=8 if n_extra else 7,
        )(routes, xo, xt, *weights)

    def prep_down():
        return launch(
            functools.partial(prep_down_body, fl),
            jnp.zeros((1,), jnp.int32),
            (dc // step,),
            [spec((step, E_F, fl_real), lambda i, sc: (i, 0, 0))],
            spec((E_F, step, fl), lambda i, sc: (0, i, 0)),
            jax.ShapeDtypeStruct((E_F, dc, fl), BF),
                us=9.5,
        )(down_weight)

    la.step()
    tiles = project(h1, h1_x, (wqk_m, wqk_x), 2, 0)
    la.step()
    def start_of(k, other, h):
        return 2 * ts * (2 * (chip ^ k) + (core ^ other)) + h * ts

    def tile_scalars(table, offsets):
        ks, others, hs = (jnp.array([[t[i] for t in row] for row in table], jnp.int32) for i in range(3))
        p0 = start_of(ks, others, hs)
        n = p0.shape[1]
        first = jnp.sum((offsets[1:] <= p0[..., None]).astype(jnp.int32), axis=2)
        last = jnp.sum((offsets[1:] <= p0[..., None] + ts - 1).astype(jnp.int32), axis=2)
        count = last - first + 1
        lower = jnp.arange(n)[:, None] >= jnp.arange(n)[None, :]
        upto = jnp.sum(jnp.where(lower, count[:, None, :], 0), axis=2)
        v = jnp.arange(n + E_F - 1, dtype=jnp.int32)
        tile = jnp.minimum(jnp.sum((upto[:, None, :] <= v[:, None]).astype(jnp.int32), axis=2), n - 1)
        mine = tile[:, :, None] == jnp.arange(n)
        begin_v = jnp.sum(jnp.where(mine, (upto - count)[:, None, :], 0), axis=2)
        first_v = jnp.sum(jnp.where(mine, first[:, None, :], 0), axis=2)
        last_v = jnp.sum(jnp.where(mine, last[:, None, :], 0), axis=2)
        e = jnp.minimum(first_v + v - begin_v, last_v)
        kind = jnp.where(v < upto[:, -1:], jnp.where(v == begin_v, 2, 1), 0)
        ends = jnp.broadcast_to(offsets, (len(table), E_F + 1))
        return jnp.concatenate((p0, tile, e, kind, ends), axis=1).astype(jnp.int32)

    near = list(chip_bits)
    far = [k for k in range(1, n_chip) if k not in near]
    back_groups = ([0], near, far)
    back_table = [[(k, other, h) for other in range(2) for h in range(2)] for k in range(n_chip)]
    n_pieces = 4 * n_chip
    def places():
        hot = (route_row[2:4, None, :] == experts[None, :, None]).astype(F32)
        blocks = rows // 128
        hot_b = hot.reshape(2 * E_F, blocks, 128)
        lane = jnp.arange(128)
        tri = (lane[:, None] < lane[None, :]).astype(BF)
        before = jnp.einsum("anl,lm->anm", hot_b.astype(BF), tri, preferred_element_type=F32)
        totals = jnp.sum(hot_b, axis=2)
        lane_b = jnp.arange(blocks)
        tri_b = (lane_b[:, None] < lane_b[None, :]).astype(BF)
        before_b = jnp.dot(totals.astype(BF), tri_b, preferred_element_type=F32)
        rank = (before + before_b[:, :, None]).reshape(2, E_F, rows)
        counts = jnp.sum(totals, axis=1).reshape(2, E_F)
        per_expert = counts[0] + counts[1]
        off = jnp.sum(jnp.where(experts[:, None] > experts[None, :], per_expert[None, :], 0.0), axis=1)
        base = jnp.stack((off, off + counts[0]))
        pos_row = jnp.sum(hot * (base[:, :, None] + rank), axis=1).astype(jnp.int32)
        pos_col = jnp.transpose(pos_row)
        offsets = jnp.concatenate((off, jnp.sum(per_expert)[None])).astype(jnp.int32)
        proj_scalars = tile_scalars([[(k, 0, h) for k, h in group] for group in groups[:2]], offsets)
        all_scalars = tile_scalars([[(k, 0, h) for k, h in groups[2]]], offsets).reshape(-1)
        starts_all = start_of(*(jnp.array([t[i] for row in back_table for t in row], jnp.int32) for i in range(3)))
        weight_scalars = jnp.concatenate((starts_all, offsets))
        back_scalars = [
            tile_scalars([[t for k in ks for t in back_table[k]]], offsets).reshape(-1) for ks in back_groups
        ]
        return pos_row, pos_col, proj_scalars.reshape(-1), all_scalars, back_scalars, starts_all, weight_scalars

    n_tile = len(groups[0])
    proj_length = 4 * n_tile + 3 * (E_F - 1) + E_F + 1

    def group_proj(xo, xt, wm, wx, g):
        m = wm.shape[2]
        n = len(groups[g])
        steps = n + E_F - 1
        lo = g * proj_length if g < 2 else 0
        parts = 2 if g < 2 else 4
        by_expert = spec((1, dc, m), lambda i, sc: (sc[lo + n + steps + i], 0, 0))
        return launch(
            functools.partial(group_proj_body, n, parts, lo),
            proj_scalars if g < 2 else all_scalars,
            (steps,),
            [spec((2, rows)), spec((rows, dc)), spec((rows, dc)), by_expert, by_expert],
            [spec((n // parts, ts, m))] * parts,
            [jax.ShapeDtypeStruct((n // parts, ts, m), BF)] * parts,
            [pltpu.VMEM((ts, 2 * dc), BF)],
            us=17 if m > fl else 27,
        )(pos_row, xo, xt, wm, wx)

    def sort_t(x):
        return launch(
            sort_t_body,
            starts_all,
            (n_pieces,),
            [spec((2, rows)), spec((rows, dc))],
            spec((dc, ts), lambda i, sc: (0, i)),
            jax.ShapeDtypeStruct((dc, 2 * rows), BF),
            us=13,
        )(pos_row, x)

    def query_window(tiles, dy):
        sent = send_first(tiles)
        for b in z_bits[1:-1]:
            dy = join([dy, z_swap(dy, b)], 0)
        dy_got = z_swap(dy, z_bits[-1])
        keep = project(h1, h1_x, (wqk_m, wqk_x), 2, 1)
        wd = prep_down()
        return sent, keep, wd, dy, dy_got

    def sum_window(sent, keep, wd, dy, dy_got):
        if keep[0].shape[0] > 1:
            keep, sent = send_next(keep, sent, 1)
        dy = join([dy, dy_got], 0)
        wd_x, dy_x = core_swap(wd), core_swap(dy)
        return finish_reduce(keep, sent, 2), dy, dy_x, wd_x, places()

    sent, keep, wd, dy, dy_got = window(query_window, tiles, dy)
    la.step()
    qkv_parts, dy_all, dy_x, wd_x, at_places = window(sum_window, sent, keep, wd, dy, dy_got)
    pos_row, pos_col, proj_scalars, all_scalars, back_scalars, starts_all, weight_scalars = at_places

    s_abs = f ^ chip
    positions = jnp.arange(seq, dtype=jnp.int32)
    my_ends = lax.dynamic_index_in_dim(ends, s_abs, 0, keepdims=False)
    my_starts = my_ends - lax.dynamic_index_in_dim(doc_lengths, s_abs, 0, keepdims=False)
    doc_one = jnp.sum((positions[:, None] >= my_ends).astype(jnp.int32), axis=1)
    begin = jnp.sum(jnp.where(doc_one[:, None] == jnp.arange(DOCS, dtype=jnp.int32), my_starts, 0), axis=1)
    doc_col, doc_row = doc_one[:, None], doc_one[None, :]
    halves = jnp.arange(HD // 2, dtype=F32)
    angles = (positions - begin).astype(F32)[:, None] * (rope_base ** (-2.0 * halves / HD))[None, :]
    cos, sin = jnp.cos(angles), jnp.sin(angles)
    cosf = jnp.concatenate((cos, cos), axis=1)
    sinf = jnp.concatenate((-sin, sin), axis=1)

    qkv, ao, lse = launch(
        functools.partial(attend_body, hc),
        one,
        (1,),
        [spec((half, 4 * width))] * 4 + [spec((seq, 1)), spec((1, seq)), spec((seq, HD)), spec((seq, HD))],
        [spec((seq, 4 * width)), spec((seq, 2 * width)), spec((seq, 128))],
        [
            jax.ShapeDtypeStruct((seq, 4 * width), BF),
            jax.ShapeDtypeStruct((seq, 2 * width), BF),
            jax.ShapeDtypeStruct((seq, 128), F32),
        ],
            us=7,
    )(*qkv_parts, doc_col, doc_row, cosf, sinf)

    ao_m = [ao] + [chip_swap(ao, k) for k in range(1, n_chip)]
    ao_t = [core_swap(ao)]
    wo_m, wo_t, wo_x = split_halves(e_major(output_weight))
    la.step()
    da_all = group_proj(dy_all, dy_x, wd, wd_x, 2)
    da_tiles, da_keep = da_all[:2], da_all[2:]
    ao_m = [ao] + hold(*ao_m[1:])
    ao_t += [core_swap(v) for v in ao_m[1:]]
    pa = gates_of(la.finish(), route_row[0:2])
    pa3 = jnp.transpose(pa).reshape(n_z, seq, 2)

    def into_stream(body, k, streams, vals, weights, buf, us, cols, carry=()):
        sc = jnp.reshape(chip ^ k, (1,))
        by_stream = [spec((pl.squeezed, seq, 2), lambda i, sc: (sc[0], 0, 0))] * len(streams)
        n_in = len(streams) + 2 + len(weights)
        return launch(
            body,
            sc,
            (1,),
            by_stream
            + [spec((seq, cols))] * 2
            + [spec(w.shape) for w in weights]
            + [pl.BlockSpec(memory_space=pl.ANY)],
            spec((1, seq, dc), lambda i, sc: (sc[0], 0, 0)),
            jax.ShapeDtypeStruct((n_z, seq, dc), BF),
            aliases={n_in + 1: 0},
            us=us,
        )(*streams, *vals, *weights, buf, carry=carry)

    buf = jnp.zeros((n_z, seq, dc), BF)
    for k in range(n_chip):
        buf = into_stream(
            functools.partial(att_out_body, width),
            k,
            (att_route3, pa3),
            (ao_m[k], ao_t[k]),
            (wo_m, wo_t),
            buf,
            4.3,
            2 * width,
            da_tiles if k == n_chip - 1 else (),
        )
    buf, *da_tiles = buf
    y1_sent = z_send([buf[k] for k in range(n_z)])
    da_sent = send_first(da_tiles)
    y1, y1_own = z_total(y1_sent, x_own)

    y1_got = z_gather(y1_own)
    y1_f = y1_own.astype(F32)
    stat = jnp.concatenate(
        (
            row_logits(rf, (y1_f * gf).astype(BF)),
            jnp.sum(y1_f * y1_f, axis=1)[None],
            jnp.zeros((7, seq), F32),
        ),
        axis=0,
    )
    stat = Small(stat, "cxg")
    if da_keep[0].shape[0] > 1:
        da_keep, da_sent = send_next(da_keep, da_sent, 1)
    for _ in range(1 + len(chip_bits)):
        stat.step()
    y1_low, yg = join_scaled(y1_got, gf)
    yg_x = (core_swap(y1_low).astype(F32) * gf_t).astype(BF)

    gu_tiles = group_proj(yg, yg_x, wg, wg_x, 0)
    gu_sent = send_first(gu_tiles)
    da_parts = finish_reduce(da_keep, da_sent, 2)
    da_parts = launch(
        pairs_body,
        one,
        (1,),
        [spec((ts, fl))] * 4,
        [spec((ts, fl))] * 2,
        [jax.ShapeDtypeStruct((ts, fl), BF)] * 2,
        us=3,
    )(*da_parts)
    gu_keep = group_proj(yg, yg_x, wg, wg_x, 1)
    stat.step()
    yg_s = sort_t(yg)
    dy_s = sort_t(dy_all)
    if gu_keep[0].shape[0] > 1:
        gu_keep, gu_sent = send_next(gu_keep, gu_sent, 1)
    stat = stat.finish()
    inv2 = lax.rsqrt(stat[8:9] / D + norm_eps)
    lf = stat[0:E_F] * inv2
    pf = gates_of(lf, route_row[2:4])
    rowv = jnp.concatenate((inv2, pf, jnp.zeros((5, rows), F32)), axis=0)
    gu_parts = finish_reduce(gu_keep, gu_sent, 2)

    by_half = lambda n: spec((1, ts, n), lambda h, sc: (h, 0, 0))
    dgu, act, tok_sum = launch(
        functools.partial(middle_body, fl),
        jnp.stack([start_of(0, 0, h) for h in range(2)]),
        (2,),
        [spec((2, rows)), spec((8, rows))] + [spec((ts, 2 * fl))] * 4 + [spec((ts, fl))] * 2,
        [by_half(2 * fl), by_half(fl), spec((8, rows))],
        [
            jax.ShapeDtypeStruct((2, ts, 2 * fl), BF),
            jax.ShapeDtypeStruct((2, ts, fl), BF),
            jax.ShapeDtypeStruct((8, rows), F32),
        ],
            us=13,
    )(pos_row, rowv, *gu_parts, *da_parts)

    def router_back(dgate, gates, route2):
        dlog = gates * (dgate - jnp.sum(gates * dgate, axis=0, keepdims=True))
        return jnp.sum(jnp.where(route2[:, None, :] == experts[None, :, None], dlog[:, None, :], 0.0), axis=0)


    def gather_near(own):
        return {0: own} | {b: chip_swap(own, b) for b in near}

    def gather_far(got):
        result = {}
        for h in range(2):
            have = {k: got[k][h] for k in got}
            seen = orders[h][0]
            for b in orders[h][1:]:
                for k in [k for k in list(have) if k and not k & ~seen]:
                    have[k ^ b] = result[k ^ b, h] = chip_swap(have[k], b)
                seen |= b
        return result

    def whole(v):
        w = core_swap(v)
        return [(v, 0), (v, 1), (w, 0), (w, 1)]

    def apart(got, k):
        mine = [got[k, h] for h in range(2)]
        return [(v, None) for v in mine] + [(core_swap(v), None) for v in mine]

    def arrays_of(pieces):
        arrays, where = [], []
        for v, h in pieces:
            i = next((i for i, u in enumerate(arrays) if u is v), None)
            if i is None:
                i = len(arrays)
                arrays.append(v)
            where.append((i, h))
        return arrays, tuple(where)


    def group_back(g, pieces, w, acc, carry=()):
        m = w.shape[2]
        arrays, where = arrays_of([v for k in back_groups[g] for v in pieces[k]])
        n = len(where)
        steps = n + E_F - 1
        return launch(
            functools.partial(group_back_body, where, 0),
            back_scalars[g],
            (steps,),
            [spec((rows, 2))]
            + [spec(v.shape) for v in arrays]
            + [spec((1, dc, m), lambda i, sc: (sc[n + steps + i], 0, 0)), spec((rows, dc))],
            spec((rows, dc)),
            jax.ShapeDtypeStruct((rows, dc), F32),
            [pltpu.VMEM((n * ts, dc), F32)],
            aliases={3 + len(arrays): 0},
            us=3.4 * n if m > fl else 2.8 * n,
        )(pos_col, *arrays, w, acc, carry=carry)

    def group_weight(xs, pieces, out, out_spec):
        arrays, where = arrays_of([v for k in range(n_chip) for v in pieces[k]])
        m = arrays[0].shape[-1]
        return launch(
            functools.partial(group_weight_body, where, fl),
            weight_scalars,
            (E_F,),
            [spec((dc, 2 * rows))] + [spec(v.shape) for v in arrays],
            out_spec,
            out,
            [pltpu.VMEM((dc, m), F32)],
            us=30 if m > fl else 0.1,
        )(xs, *arrays)

    dgu_pieces = {0: whole(dgu)}
    act_x = core_swap(act)
    dgu_got = gather_near(dgu)

    tok_sum = Small(rel(tok_sum.reshape(8, n_z, seq).transpose(1, 0, 2)[:, :3]).reshape(n_z * 3, seq), "czx")
    tok_sum.step()
    dh2 = group_back(0, dgu_pieces, wg, jnp.zeros((rows, dc), F32))
    act_pieces = {0: [(act, 0), (act, 1), (act_x, 0), (act_x, 1)]}
    tok_sum.step()
    ffn = group_back(0, act_pieces, wd, jnp.zeros((rows, dc), F32))
    tok_sum.step()
    got = hold(*[dgu_got[b] for b in near])
    dgu_far = gather_far(dict(zip(near, got)))
    for b, v in zip(near, got):
        dgu_pieces[b] = whole(v)
    dh2, act = group_back(1, dgu_pieces, wg, dh2, carry=(act,))
    act_pieces[0] = [(act, 0), (act, 1), (act_x, 0), (act_x, 1)]
    tok_sum.step()
    dgu_far = dict(zip(dgu_far, hold(*dgu_far.values())))
    for k in far:
        dgu_pieces[k] = apart(dgu_far, k)
    act_got = gather_near(act)
    dh2 = group_back(2, dgu_pieces, wg, dh2)
    def first_back_window(dh2):
        sent = z_send([dh2[k * seq : (k + 1) * seq].astype(BF) for k in range(n_z)])
        gate_up_grad = group_weight(
            yg_s,
            dgu_pieces,
            jax.ShapeDtypeStruct((dc, E_F, 2, fl_real), F32),
            spec((dc, 1, 2, fl_real), lambda e, sc: (0, e, 0, 0)),
        )
        return z_total(sent)[1], gate_up_grad

    dh2, gate_up_grad = window(first_back_window, dh2)
    act_got = hold(*[act_got[b] for b in near])
    for b, v in zip(near, act_got):
        act_pieces[b] = whole(v)
    act_far = gather_far(dict(zip(near, act_got)))

    def second_back_window(dh2, ffn):
        got = z_gather(dh2)
        return group_back(1, act_pieces, wd, ffn), got

    ffn, dh2_got = window(second_back_window, dh2, ffn)
    tok_sum = rel(tok_sum.finish().reshape(n_z, 3, seq)).transpose(1, 0, 2).reshape(3, rows)
    dlf = router_back(tok_sum[0:2], pf, route_row[2:4])
    m2 = (tok_sum[2:3] + jnp.sum(dlf * lf, axis=0, keepdims=True)) / D
    dlf_inv = (dlf * inv2).astype(BF)
    by_row = lambda n: spec((seq, n), lambda i, sc: (i, 0))
    dy1_low, dh2_own = launch(
        functools.partial(middle_grad_body, n_z),
        jnp.zeros((1,), jnp.int32),
        (n_z,),
        [by_row(dc), by_row(dc), spec((E_F, seq), lambda i, sc: (0, i)), by_row(1), spec((E_F, dc)), spec((1, dc))]
        + [spec((seq, dc))] * n_z,
        [by_row(dc), spec((seq, dc))],
        [jax.ShapeDtypeStruct((rows, dc), BF), jax.ShapeDtypeStruct((seq, dc), F32)],
        us=4,
    )(dy_all, y1_low, dlf_inv, jnp.transpose(m2 * inv2 * inv2), jnp.transpose(rf), gf, *dh2_got)
    dy1_x = core_swap(dy1_low)

    tiles = project(dy1_low, dy1_x, (wo_m, wo_x), 0, 0)
    sent, keep = window(
        lambda tiles: (send_first(tiles), project(dy1_low, dy1_x, (wo_m, wo_x), 0, 1)), tiles
    )
    if keep[0].shape[0] > 1:
        keep, sent = send_next(keep, sent, 1)

    def att_weight(xt, with_gates, extra, mine, theirs, cols):
        pieces = [v for pair in zip(mine, theirs) for v in pair]
        sc = jnp.concatenate((chip ^ jnp.arange(n_chip, dtype=jnp.int32), core[None]))
        at = lambda i, e, sc: (0, 0, sc[n_chip] ^ i)
        outs = [E_A] + ([2] if extra else [])
        return launch(
            functools.partial(att_weight_body, width, n_chip, with_gates, extra),
            sc,
            (2, E_A),
            [spec(xt.shape), spec((n_z, seq, 2)), spec((n_z, seq, 2))] + [spec((seq, cols))] * len(pieces),
            [spec((dc, n, width), at) for n in outs],
            [jax.ShapeDtypeStruct((dc, n, 2 * width), F32) for n in outs],
            [pltpu.VMEM((n_chip, seq, 2 * width), BF)],
            us=20,
        )(xt, att_route3, pa3, *pieces)

    def stream_t(v):
        return jnp.transpose(v.reshape(n_z, seq, dc), (0, 2, 1))

    act_far = dict(zip(act_far, hold(*act_far.values())))
    for k in far:
        act_pieces[k] = apart(act_far, k)
    ffn = group_back(2, act_pieces, wd, ffn)
    dao_parts = finish_reduce(keep, sent, 2)

    pa_one = lax.dynamic_index_in_dim(pa3, chip, 0, keepdims=False)
    grads, dgate = launch(
        functools.partial(attend_back_body, hc),
        one,
        (1,),
        [spec((half, 2 * width))] * 4
        + [spec((seq, 4 * width)), spec((seq, 2 * width)), spec((seq, 128)), spec((seq, 2))]
        + [spec((seq, 1)), spec((1, seq)), spec((seq, HD)), spec((seq, HD))],
        [spec((seq, 4 * width)), spec((seq, 128))],
        [jax.ShapeDtypeStruct((seq, 4 * width), BF), jax.ShapeDtypeStruct((seq, 128), F32)],
            us=7,
    )(*dao_parts, qkv, ao, lse, pa_one, doc_col, doc_row, cosf, sinf)
    dpa = jnp.zeros((n_z, 2, seq), F32)
    dpa = lax.dynamic_update_slice(dpa, jnp.transpose(dgate[:, :2])[None], (s_abs, 0, 0))
    dpa = Small(dpa.reshape(n_z * 2, seq), "czx")
    def grads_window(grads, ffn):
        got = [chip_swap(grads, k) for k in range(1, n_chip)]
        own = core_swap(grads)
        ffn_sent = z_swap(ffn[rows // 2 :], z_bits[-1])
        down_grad = group_weight(
            dy_s,
            act_pieces,
            jax.ShapeDtypeStruct((dc, E_F, fl_real), F32),
            spec((dc, E_F, fl_real)),
        )
        return got, own, ffn_sent, down_grad

    ffn = ffn.astype(BF)
    g_m, own_t, ffn_sent, down_grad = window(grads_window, grads, ffn)
    g_m, g_t = [grads, *g_m], [own_t]
    dpa.step()
    g_t += [core_swap(v) for v in g_m[1:]]

    def to_rows(v):
        n = v.shape[1] // dc
        v = lax.all_to_all(v.reshape(n_ctx, tok, n * dc), "ctx", 0, 0, tiled=True)
        v = v.reshape(n_ctx, tok, n, dc).transpose(2, 1, 0, 3)
        return v.reshape(n, tok, D)

    buf = jnp.zeros((n_z, seq, dc), BF)
    for k in range(n_chip):
        buf = into_stream(
            functools.partial(att_in_back_body, width),
            k,
            (att_route3,),
            (g_m[k], g_t[k]),
            (wqk_m, wqk_t),
            buf,
            5,
            4 * width,
        )
        dpa.step()
        if k == 0:
            for b in z_bits[-2::-1]:
                n = ffn_sent.shape[0] // 2
                both = [spec((n, dc), lambda i, sc: (i, 0))] * 2
                ffn, _ = launch(
                    functools.partial(total_body, 2),
                    one,
                    (2,),
                    both,
                    both,
                    [jax.ShapeDtypeStruct((2 * n, dc), F32), jax.ShapeDtypeStruct((2 * n, dc), BF)],
                    us=2,
                )(ffn, ffn_sent)[::-1]
                ffn_sent = z_swap(ffn[n:], b)
    dpa = lax.dynamic_index_in_dim(dpa.finish().reshape(n_z, 2, seq), f, 0, keepdims=False)
    ffn = z_total([ffn[:seq], ffn_sent], y1)[1]

    def last_window(buf):
        sent = z_send([buf[k] for k in range(n_z)])
        query_grad, kv_grad = att_weight(stream_t(h1), False, True, g_m, g_t, 4 * width)
        return z_total(sent)[0], query_grad, kv_grad

    dh1, query_grad, kv_grad = window(last_window, buf)
    dla = router_back(dpa, pa[:, :seq], route_row[0:2, :seq]).astype(BF)
    dh1 = dh1 + lax.dot_general(dla, ra, (((0,), (1,)), ((), ())), preferred_element_type=F32)
    back_col = jnp.concatenate(((dh1 * ga).astype(BF), dy1_low[:seq]), axis=1)

    back = to_rows(jnp.concatenate((back_col, ffn), axis=1))
    outputs, back = back[2:], back[:2].astype(F32)
    input_grad = back[1] + inv1_loc * (back[0] - n1_loc * jnp.mean(back[0] * n1_loc, axis=1, keepdims=True))
    input_grad = input_grad.astype(BF)[None]

    mark(back_col)
    (output_grad,) = att_weight(stream_t(dy1_low), True, False, ao_m, ao_t, 2 * width)

    own = slice(0, seq)
    tail = jnp.concatenate(
        (
            jnp.dot(dla, h1[own], preferred_element_type=F32),
            jnp.dot(dlf_inv[:, own], yg[own], preferred_element_type=F32),
            jnp.sum(dh1 * n1_own.astype(F32), axis=0, keepdims=True),
            jnp.sum(dh2_own * y1_f, axis=0, keepdims=True),
            jnp.zeros((6, dc), F32),
        ),
        axis=0,
    )
    tail = Small(tail, "z").finish()
    att_router_grad = jnp.transpose(tail[0:E_A])
    ffn_router_grad = jnp.transpose(tail[E_A : E_A + E_F])
    att_gain_grad = tail[E_A + E_F]
    ffn_gain_grad = tail[E_A + E_F + 1]

    return (
        outputs,
        input_grad,
        kv_grad,
        query_grad,
        output_grad,
        att_router_grad,
        att_gain_grad,
        gate_up_grad,
        down_grad,
        ffn_router_grad,
        ffn_gain_grad,
    )


def solution(mesh):
    in_specs = (
        P("fsdp", "ctx", None),
        P("fsdp", "ctx", None),
        P(),
        P("ctx", None, None),
        P("ctx", None, None),
        P("ctx", None, "fsdp"),
        P("ctx", None, "fsdp"),
        P("ctx", None, "fsdp"),
        P("ctx", None),
        P("ctx"),
        P("ctx", None, None, "fsdp"),
        P("ctx", None, "fsdp"),
        P("ctx", None),
        P("ctx"),
    )
    out_specs = (
        P("fsdp", "ctx", None),
        P("fsdp", "ctx", None),
        P("ctx", None, "fsdp"),
        P("ctx", None, "fsdp"),
        P("ctx", None, "fsdp"),
        P("ctx", None),
        P("ctx"),
        P("ctx", None, None, "fsdp"),
        P("ctx", None, "fsdp"),
        P("ctx", None),
        P("ctx"),
    )
    return jax.shard_map(
        per_device, mesh=mesh, in_specs=in_specs, out_specs=out_specs, check_vma=False
    )
```

```python
import functools

import jax
import jax.numpy as jnp
from jax import lax
from jax.experimental import pallas as pl
from jax.experimental.pallas import tpu as pltpu
from jax.sharding import PartitionSpec as P

D = 2048
HEADS = 16
HD = 128
E_A = 8
E_F = 8
FF = 5632
DOCS = 3

norm_eps = 1e-06
rope_base = 10000.0
masked_score = -1e30

BF = jnp.bfloat16
F32 = jnp.float32
VMEM_CAP = 60 * 1024 * 1024
PER_US = 1.1e9


def dot(a, b):
    return lax.dot_general(a, b, (((1,), (0,)), ((), ())), preferred_element_type=F32)


def dot_nt(a, b):
    return lax.dot_general(a, b, (((1,), (1,)), ((), ())), preferred_element_type=F32)


def dot_tn(a, b):
    return lax.dot_general(a, b, (((0,), (0,)), ((), ())), preferred_element_type=F32)


def spec(shape, index=None):
    if index is not None:
        return pl.BlockSpec(shape, index)
    zeros = (0,) * len(shape)
    return pl.BlockSpec(shape, lambda *_: zeros, pipeline_mode=pl.Buffered(1))


def call(chain, body, sc, grid, in_specs, out_specs, out_shape, scratch=(), aliases=None, us=5):
    single = not isinstance(out_shape, (list, tuple))
    out_specs, out_shape = ([out_specs], [out_shape]) if single else (list(out_specs), list(out_shape))
    out_specs = [pl.BlockSpec(v.block_shape, v.index_map) for v in out_specs]
    anywhere = pl.BlockSpec(memory_space=pl.ANY)

    def go(*operands, carry=()):
        waits = [v for v in chain if not any(v is u for u in operands) and not any(v is u for u in carry)]
        n_in, n_extra, n_out, n_carry = len(operands), len(waits) + len(carry), len(out_shape), len(carry)

        def kernel_body(first, *refs):
            outs = refs[n_in + n_extra :]
            body(first, *refs[:n_in], *outs[:n_out], *outs[n_out + n_carry :])

        alias = dict(aliases or {})
        for i in range(n_carry):
            alias[1 + n_in + len(waits) + i] = n_out + i
        out = pl.pallas_call(
            kernel_body,
            out_shape=out_shape + [jax.ShapeDtypeStruct(v.shape, v.dtype) for v in carry],
            grid_spec=pltpu.PrefetchScalarGridSpec(
                num_scalar_prefetch=1,
                grid=grid,
                in_specs=list(in_specs) + [anywhere] * n_extra,
                out_specs=out_specs + [anywhere] * n_carry,
                scratch_shapes=list(scratch),
            ),
            input_output_aliases=alias,
            compiler_params=pltpu.CompilerParams(
                dimension_semantics=("arbitrary",) * len(grid), vmem_limit_bytes=VMEM_CAP
            ),
            cost_estimate=pl.CostEstimate(flops=int(us * PER_US), bytes_accessed=0, transcendentals=0),
        )(sc, *operands, *waits, *carry)
        chain[:] = out[:1]
        result = out[0] if single else out[:n_out]
        return (result, *out[n_out:]) if carry else result

    return go


def proj_body(n_extra, width, n, sc, route, xo, xt, *refs):
    wm, wt = refs[0], refs[1]
    outs, tile = refs[-3:-1], refs[-1]
    a, b = xo[...], xt[...]
    r0, r1 = route[:, 0:1], route[:, 1:2]
    acc0 = jnp.zeros((a.shape[0], width), F32)
    acc1 = acc0
    for e in range(E_A):
        r = dot(a, wm[e]) + dot(b, wt[e])
        acc0 = jnp.where(r0 == e, r, acc0)
        acc1 = jnp.where(r1 == e, r, acc1)
    tile[:, 0:width] = acc0.astype(BF)
    tile[:, width : 2 * width] = acc1.astype(BF)
    for i in range(n_extra):
        r = dot(a, wm[E_A + i]) + dot(b, wt[E_A + i])
        tile[:, (2 + i) * width : (3 + i) * width] = r.astype(BF)
    for i in range(n):

        @pl.when(pl.program_id(0) == i)
        def _():
            outs[i // (n // 2)][i % (n // 2)] = tile[...]


def rotate(u, cosf, sinf):
    return u * cosf + pltpu.roll(u, HD // 2, 1) * sinf


def unrotate(u, cosf, sinf):
    return u * cosf - pltpu.roll(u, HD // 2, 1) * sinf


def add_halves(refs):
    a0, a1, b0, b1 = refs
    top = a0[...].astype(F32) + a1[...].astype(F32)
    low = b0[...].astype(F32) + b1[...].astype(F32)
    return jnp.concatenate((top, low), axis=0)


def allowed_pairs(doc_col, doc_row):
    n = doc_col.shape[0]
    t = lax.broadcasted_iota(jnp.int32, (n, n), 0)
    u = lax.broadcasted_iota(jnp.int32, (n, n), 1)
    return (doc_col[...] == doc_row[...]) & (u <= t) & (doc_col[...] < DOCS)


def attend_body(hc, sc, a0, a1, b0, b1, doc_col, doc_row, cosr, sinr, qkv, out, lse):
    width = hc * HD
    u = add_halves((a0, a1, b0, b1))
    cosf, sinf = cosr[...], sinr[...]
    ok = allowed_pairs(doc_col, doc_row)
    for h in range(hc):
        at = 2 * width + h * HD
        k = rotate(u[:, at : at + HD], cosf, sinf).astype(BF)
        v = u[:, at + width : at + width + HD].astype(BF)
        qkv[:, at : at + HD] = k
        qkv[:, at + width : at + width + HD] = v
        for j in range(2):
            lo = j * width + h * HD
            q = rotate(u[:, lo : lo + HD], cosf, sinf).astype(BF)
            qkv[:, lo : lo + HD] = q
            s = jnp.where(ok, dot_nt(q, k) * (HD**-0.5), masked_score)
            m = jnp.max(s, axis=1, keepdims=True)
            p = jnp.where(ok, jnp.exp(s - m), 0.0)
            total = jnp.sum(p, axis=1, keepdims=True)
            total = jnp.where(total > 0, total, 1.0)
            out[:, lo : lo + HD] = (dot(p.astype(BF), v) / total).astype(BF)
            lse[:, 2 * h + j : 2 * h + j + 1] = m + jnp.log(total)


def attend_back_body(hc, sc, a0, a1, b0, b1, qkv, att, lse, gates, doc_col, doc_row, cosr, sinr, grads, dgate):
    width = hc * HD
    u = add_halves((a0, a1, b0, b1))
    cosf, sinf = cosr[...], sinr[...]
    ok = allowed_pairs(doc_col, doc_row)
    keep = (doc_col[...] < DOCS).astype(F32)
    dg = [jnp.zeros((u.shape[0], 1), F32) for _ in range(2)]
    for h in range(hc):
        at = 2 * width + h * HD
        k = qkv[:, at : at + HD]
        v = qkv[:, at + width : at + width + HD]
        dk = jnp.zeros((u.shape[0], HD), F32)
        dv = dk
        for j in range(2):
            lo = j * width + h * HD
            q = qkv[:, lo : lo + HD]
            o = att[:, lo : lo + HD].astype(F32)
            raw = u[:, lo : lo + HD]
            dg[j] = dg[j] + jnp.sum(raw * o, axis=1, keepdims=True)
            do = (raw * (gates[:, j : j + 1] * keep)).astype(BF)
            delta = jnp.sum(do.astype(F32) * o, axis=1, keepdims=True)
            s = dot_nt(q, k) * (HD**-0.5)
            p = jnp.where(ok, jnp.exp(s - lse[:, 2 * h + j : 2 * h + j + 1]), 0.0)
            ds = (p * (dot_nt(do, v) - delta)).astype(BF)
            dq = dot(ds, k) * (HD**-0.5)
            grads[:, lo : lo + HD] = unrotate(dq, cosf, sinf).astype(BF)
            dk = dk + dot_tn(ds, q)
            dv = dv + dot_tn(p.astype(BF), do)
        grads[:, at : at + HD] = unrotate(dk * (HD**-0.5), cosf, sinf).astype(BF)
        grads[:, at + width : at + width + HD] = dv.astype(BF)
    dgate[...] = jnp.zeros_like(dgate)
    dgate[:, 0:1] = dg[0]
    dgate[:, 1:2] = dg[1]


def chosen(hot0, hot1, a, b, e):
    return a * hot0[e] + b * hot1[e]


def one_hots(route):
    return [[jnp.where(route[:, j : j + 1] == e, 1.0, 0.0).astype(BF) for e in range(E_A)] for j in range(2)]


def gated(vals, gates, width):
    a = (vals[:, 0:width].astype(F32) * gates[:, 0:1]).astype(BF)
    b = (vals[:, width : 2 * width].astype(F32) * gates[:, 1:2]).astype(BF)
    return a, b


def att_out_body(width, sc, route, gates, om, ot, wm, wt, prev, out):
    acc = jnp.zeros(out.shape[1:], F32)
    hot0, hot1 = one_hots(route)
    am, bm = gated(om, gates, width)
    at, bt = gated(ot, gates, width)
    for e in range(E_A):
        acc += dot_nt(chosen(hot0, hot1, am, bm, e), wm[e])
        acc += dot_nt(chosen(hot0, hot1, at, bt, e), wt[e])
    out[0] = acc.astype(BF)


def att_in_back_body(width, sc, route, gm, gt, wm, wt, prev, out):
    acc = jnp.zeros(out.shape[1:], F32)
    hot0, hot1 = one_hots(route)
    am, bm = gm[:, 0:width], gm[:, width : 2 * width]
    at, bt = gt[:, 0:width], gt[:, width : 2 * width]
    for e in range(E_A):
        acc += dot_nt(chosen(hot0, hot1, am, bm, e), wm[e])
        acc += dot_nt(chosen(hot0, hot1, at, bt, e), wt[e])
    for i in range(2):
        lo = (2 + i) * width
        acc += dot_nt(gm[:, lo : lo + width], wm[E_A + i]) + dot_nt(gt[:, lo : lo + width], wt[E_A + i])
    out[0] = acc.astype(BF)


def att_weight_body(width, n, with_gates, extra, sc, *refs):
    xt, route, gates = refs[0], refs[1], refs[2]
    pieces = refs[3 : 3 + 2 * n]
    out = refs[3 + 2 * n]
    out2 = refs[4 + 2 * n] if extra else None
    vals = refs[-1]
    seq = route.shape[1]
    half = pl.program_id(0)
    e = pl.program_id(1)
    for side in range(2):

        @pl.when((half == side) & (e == 0))
        def _():
            for k in range(n):
                piece = pieces[2 * k + side]
                if with_gates:
                    a, b = gated(piece, gates[sc[k]], width)
                else:
                    a, b = piece[:, 0:width], piece[:, width : 2 * width]
                vals[k, :, 0:width] = a
                vals[k, :, width : 2 * width] = b
            if extra:
                for i in range(2):
                    lo = (2 + i) * width
                    acc = jnp.zeros((xt.shape[1], width), F32)
                    for k in range(n):
                        acc += dot(xt[sc[k]], pieces[2 * k + side][:, lo : lo + width])
                    out2[:, i, :] = acc

    acc = jnp.zeros((xt.shape[1], width), F32)
    for k in range(n):
        r = route[sc[k]]
        hot0 = jnp.where(r[:, 0:1] == e, 1.0, 0.0).astype(BF)
        hot1 = jnp.where(r[:, 1:2] == e, 1.0, 0.0).astype(BF)
        sel = vals[k, :, 0:width] * hot0 + vals[k, :, width : 2 * width] * hot1
        acc += dot(xt[sc[k]], sel)
    for i in range(E_A):

        @pl.when(e == i)
        def _():
            out[:, i, :] = acc


def row_chunks(rows):
    step = min(rows, 1024)
    return [(i, step) for i in range(0, rows, step)]


def group_proj_body(n, parts, base, sc, pos, xo, xt, wm, wt, *refs):
    outs, xs = refs[:parts], refs[parts]
    i = pl.program_id(0)
    steps = pl.num_programs(0)
    ts = outs[0].shape[1]
    dc = xo.shape[1]
    at = base + n + i
    tile, e, kind = sc[at], sc[at + steps], sc[at + 2 * steps]
    p0 = sc[base + tile]

    @pl.when(kind == 2)
    def _():
        a = jnp.zeros((ts, dc), F32)
        b = a
        for lo, m in row_chunks(xo.shape[0]):
            ids = p0 + lax.broadcasted_iota(jnp.int32, (ts, m), 0)
            hot = (pos[0:1, lo : lo + m] == ids) | (pos[1:2, lo : lo + m] == ids)
            hot = jnp.where(hot, 1.0, 0.0).astype(BF)
            a = a + dot(hot, xo[lo : lo + m, :])
            b = b + dot(hot, xt[lo : lo + m, :])
        xs[:, 0:dc] = a.astype(BF)
        xs[:, dc : 2 * dc] = b.astype(BF)

    rows = p0 + lax.broadcasted_iota(jnp.int32, (ts, 1), 0)
    for t in range(n):
        out, at = outs[t // (n // parts)], t % (n // parts)

        @pl.when((kind == 2) & (tile == t))
        def _():
            out[at] = (dot(xs[:, 0:dc], wm[0]) + dot(xs[:, dc : 2 * dc], wt[0])).astype(BF)

        @pl.when((kind == 1) & (tile == t))
        def _():
            r = dot(xs[:, 0:dc], wm[0]) + dot(xs[:, dc : 2 * dc], wt[0])
            out[at] = jnp.where(rows >= sc[base + n + 3 * steps + e], r, out[at].astype(F32)).astype(BF)


def middle_body(fl, sc, pos, rowv, *refs):
    gu, da = refs[0:4], refs[4:6]
    dgu, act, tok = refs[6:]
    ts = gu[0].shape[0]
    rows = pos.shape[1]
    half = pl.program_id(0)
    p0 = sc[half]
    inv = jnp.zeros((ts, 1), F32)
    gate = inv
    for lo, n in row_chunks(rows):
        ids = p0 + lax.broadcasted_iota(jnp.int32, (ts, n), 0)
        is0 = pos[0:1, lo : lo + n] == ids
        is1 = pos[1:2, lo : lo + n] == ids
        inv += jnp.sum(jnp.where(is0 | is1, rowv[0:1, lo : lo + n], 0.0), axis=1, keepdims=True)
        picked = jnp.where(is0, rowv[1:2, lo : lo + n], jnp.where(is1, rowv[2:3, lo : lo + n], 0.0))
        gate += jnp.sum(picked, axis=1, keepdims=True)

    def work(g0, g1, d):
        dpf = jnp.zeros((ts, 128), F32)
        dn = dpf
        step = 128
        for lo in range(0, fl, step):
            gt = (g0[:, lo : lo + step].astype(F32) + g1[:, lo : lo + step].astype(F32)) * inv
            up = (g0[:, fl + lo : fl + lo + step].astype(F32) + g1[:, fl + lo : fl + lo + step].astype(F32)) * inv
            raw = d[:, lo : lo + step].astype(F32)
            sg = 1.0 / (1.0 + jnp.exp(-gt))
            silu = gt * sg
            a = silu * up
            act[0, :, lo : lo + step] = (a * gate).astype(BF)
            da = raw * gate
            dgt = da * up * (sg + silu * (1.0 - sg))
            dup = da * silu
            dgu[0, :, lo : lo + step] = (dgt * inv).astype(BF)
            dgu[0, :, fl + lo : fl + lo + step] = (dup * inv).astype(BF)
            dpf += raw * a
            dn += dgt * gt + dup * up
        dpf = jnp.sum(dpf, axis=1, keepdims=True)
        dn = jnp.sum(dn, axis=1, keepdims=True)
        for lo, n in row_chunks(rows):
            ids = p0 + lax.broadcasted_iota(jnp.int32, (ts, n), 0)
            is0 = pos[0:1, lo : lo + n] == ids
            is1 = pos[1:2, lo : lo + n] == ids
            t0 = jnp.sum(jnp.where(is0, dpf, 0.0), axis=0, keepdims=True)
            t1 = jnp.sum(jnp.where(is1, dpf, 0.0), axis=0, keepdims=True)
            t2 = jnp.sum(jnp.where(is0 | is1, dn, 0.0), axis=0, keepdims=True)
            new = jnp.concatenate((t0, t1, t2, jnp.zeros((5, n), F32)), axis=0)
            tok[:, lo : lo + n] = new + jnp.where(half == 0, 0.0, tok[:, lo : lo + n])

    for h in range(2):

        @pl.when(half == h)
        def _():
            work(*gu[2 * h : 2 * h + 2], da[h])


def piece_of(arrays, place):
    i, h = place
    return arrays[i][...] if h is None else arrays[i][h]


def group_back_body(where, base, sc, posc, *refs):
    n = len(where)
    arrays, (w, prev, out, dh) = refs[:-4], refs[-4:]
    i = pl.program_id(0)
    steps = pl.num_programs(0)
    ts = dh.shape[0] // n
    at = base + n + i
    tile, e, kind = sc[at], sc[at + steps], sc[at + 2 * steps]
    p0 = sc[base + tile]
    rows = p0 + lax.broadcasted_iota(jnp.int32, (ts, 1), 0)
    for t in range(n):

        @pl.when((kind == 2) & (tile == t))
        def _():
            dh[t * ts : (t + 1) * ts, :] = dot_nt(piece_of(arrays, where[t]), w[0])

        @pl.when((kind == 1) & (tile == t))
        def _():
            r = dot_nt(piece_of(arrays, where[t]), w[0])
            old = dh[t * ts : (t + 1) * ts, :]
            dh[t * ts : (t + 1) * ts, :] = jnp.where(rows >= sc[base + n + 3 * steps + e], r, old)

    @pl.when(i == steps - 1)
    def _():
        for lo, m in row_chunks(out.shape[0]):
            acc = prev[lo : lo + m, :]
            for t in range(n):
                ids = sc[base + t] + lax.broadcasted_iota(jnp.int32, (m, ts), 1)
                hot = (posc[lo : lo + m, 0:1] == ids) | (posc[lo : lo + m, 1:2] == ids)
                acc = acc + dot(jnp.where(hot, 1.0, 0.0).astype(BF), dh[t * ts : (t + 1) * ts, :].astype(BF))
            out[lo : lo + m, :] = acc


def sort_t_body(sc, pos, x, out):
    p0 = sc[pl.program_id(0)]
    ts = out.shape[1]
    acc = jnp.zeros((ts, x.shape[1]), F32)
    for lo, m in row_chunks(x.shape[0]):
        ids = p0 + lax.broadcasted_iota(jnp.int32, (ts, m), 0)
        hot = (pos[0:1, lo : lo + m] == ids) | (pos[1:2, lo : lo + m] == ids)
        acc += dot(jnp.where(hot, 1.0, 0.0).astype(BF), x[lo : lo + m, :])
    out[...] = jnp.transpose(acc).astype(BF)


def group_weight_body(where, fl, sc, xs, *refs):
    n = len(where)
    arrays, (out, acc) = refs[:-2], refs[-2:]
    ts = xs.shape[1] // n
    e = pl.program_id(0)
    lo, hi = sc[n + e], sc[n + e + 1]
    acc[...] = jnp.zeros_like(acc)
    for i in range(n):
        p0 = sc[i]

        @pl.when((p0 < hi) & (p0 + ts > lo))
        def _():
            ids = p0 + lax.broadcasted_iota(jnp.int32, (1, ts), 1)
            ok = jnp.where((ids >= lo) & (ids < hi), 1.0, 0.0).astype(BF)
            acc[...] += dot(xs[:, i * ts : (i + 1) * ts] * ok, piece_of(arrays, where[i]))

    if len(out.shape) == 4:
        real = out.shape[3]
        out[:, 0, 0, :] = acc[:, 0:real]
        out[:, 0, 1, :] = acc[:, fl : fl + real]
    else:
        for i in range(E_F):

            @pl.when(e == i)
            def _():
                out[:, i, :] = acc[:, 0 : out.shape[2]]


def hold_body(sc, out):
    out[...] = jnp.zeros_like(out)


def add_body(sc, x, got, out):
    out[...] = x[...] + got[...]


def join_body(axis, n, sc, *refs):
    size = refs[0].shape[axis]
    for k in range(n):
        if axis:
            refs[n][:, k * size : (k + 1) * size] = refs[k][...]
        else:
            refs[n][k * size : (k + 1) * size, :] = refs[k][...]


def join_scaled_body(n, sc, gain, *refs):
    size = refs[0].shape[0]
    for k in range(n):
        v = refs[k][...]
        refs[n][k * size : (k + 1) * size, :] = v
        refs[n + 1][k * size : (k + 1) * size, :] = (v.astype(F32) * gain[...]).astype(BF)


def pairs_body(sc, a0, a1, b0, b1, a, b):
    a[...] = (a0[...].astype(F32) + a1[...].astype(F32)).astype(BF)
    b[...] = (b0[...].astype(F32) + b1[...].astype(F32)).astype(BF)


def total_body(n, sc, *refs):
    total = refs[0][...].astype(F32)
    for v in refs[1:n]:
        total = total + v[...].astype(F32)
    refs[n][...] = total
    refs[n + 1][...] = total.astype(BF)


def step_body(sc, *refs):
    for h in range(2):
        refs[4 + h][...] = (refs[2 * h][...].astype(F32) + refs[2 * h + 1][...].astype(F32)).astype(BF)


def middle_grad_body(n, sc, dy, y1, dlf, coef, rf, gf, *refs):
    i = pl.program_id(0)
    dy1, dh2 = refs[n:]
    router = dot_tn(dlf[...], rf[...])

    def work(part):
        total = part[...].astype(F32) + router
        dy1[...] = (dy[...].astype(F32) + total * gf[...] - y1[...].astype(F32) * coef[...]).astype(BF)

        @pl.when(i == 0)
        def _():
            dh2[...] = total

    for k in range(n):

        @pl.when(i == k)
        def _():
            work(refs[k])


def prep_gate_up_body(fl, sc, w, out):
    real = w.shape[3]
    for e in range(E_F):
        for j in range(2):
            out[e, :, j * fl : j * fl + real] = w[:, e, j, :].astype(BF)
            if real != fl:
                out[e, :, j * fl + real : (j + 1) * fl] = jnp.zeros((w.shape[0], fl - real), BF)


def prep_down_body(fl, sc, w, out):
    real = w.shape[2]
    out[:, :, 0:real] = jnp.swapaxes(w[...].astype(BF), 0, 1)
    if real != fl:
        out[:, :, real:fl] = jnp.zeros((E_F, w.shape[0], fl - real), BF)


def per_device(
    inputs,
    cotangent,
    doc_lengths,
    att_routes,
    ffn_routes,
    kv_weight,
    query_weight,
    output_weight,
    att_router,
    att_gain,
    gate_up_weight,
    down_weight,
    ffn_router,
    ffn_gain,
):
    n_ctx = lax.axis_size("ctx")
    n_z = lax.axis_size("fsdp")
    c = lax.axis_index("ctx")
    f = lax.axis_index("fsdp")
    n_chip = n_ctx // 2
    chip, core = c // 2, c % 2
    tok = inputs.shape[1]
    seq = tok * n_ctx
    dc = D // n_ctx
    rows = n_z * seq
    hc = HEADS // n_z // 2
    width = hc * HD
    half = seq // 2
    fl_real = FF // n_z
    fl = -(-fl_real // 128) * 128
    ts = 2 * rows // n_ctx // 2
    assert n_chip == n_z

    chain = []
    launch = functools.partial(call, chain)

    def swap(x, axis, k, n):
        return lax.ppermute(x, axis, [(i, i ^ k) for i in range(n)])

    def core_swap(x):
        return swap(x, "ctx", 1, n_ctx)

    def chip_swap(x, k):
        return swap(x, "ctx", 2 * k, n_ctx)

    def z_swap(x, k):
        return swap(x, "fsdp", k, n_z)

    chip_bits = [1 << i for i in range(n_chip.bit_length() - 1)]
    z_bits = [1 << i for i in range(n_z.bit_length() - 1)]

    def z_gather(x):
        return [x] + [z_swap(x, k) for k in range(1, n_z)]

    def z_send(pieces):
        return [pieces[0]] + [z_swap(pieces[k], k) for k in range(1, n_z)]

    def z_total(got, *others):
        got = [*got, *others]
        return launch(
            functools.partial(total_body, len(got)),
            jnp.zeros((1,), jnp.int32),
            (1,),
            [spec((seq, dc))] * len(got),
            [spec((seq, dc))] * 2,
            [jax.ShapeDtypeStruct((seq, dc), F32), jax.ShapeDtypeStruct((seq, dc), BF)],
            us=1.5,
        )(*got)

    def mark(*values):
        chain.extend(values)

    one = jnp.zeros((1,), jnp.int32)
    always = doc_lengths[0, 0] > 0

    def window(work, *args):
        outer = list(chain)

        def inside(tokens, args):
            chain[:] = tokens
            return work(*args)

        shapes = jax.eval_shape(inside, outer, args)
        nothing = lambda tokens, args: jax.tree.map(lambda v: jnp.zeros(v.shape, v.dtype), shapes)
        out = lax.cond(always, inside, nothing, outer, args)
        chain[:] = jax.tree.leaves(out)[:1]
        return out

    def hold(*vals):
        out = launch(
            hold_body, one, (1,), [], spec((8, 128)), jax.ShapeDtypeStruct((8, 128), F32), us=0.5
        )(carry=vals)
        return list(out[1:])

    def join(vals, axis):
        m, n = vals[0].shape
        shape = (m, len(vals) * n) if axis else (len(vals) * m, n)
        return launch(
            functools.partial(join_body, axis, len(vals)),
            one,
            (1,),
            [spec((m, n))] * len(vals),
            spec(shape),
            jax.ShapeDtypeStruct(shape, vals[0].dtype),
            us=1.5,
        )(*vals)

    def join_scaled(vals, gain):
        m, n = vals[0].shape
        shape = (len(vals) * m, n)
        return launch(
            functools.partial(join_scaled_body, len(vals)),
            one,
            (1,),
            [spec((1, n))] + [spec((m, n))] * len(vals),
            [spec(shape)] * 2,
            [jax.ShapeDtypeStruct(shape, BF)] * 2,
            us=2,
        )(gain, *vals)

    class Small:
        def __init__(self, x, hops):
            self.x = x
            self.todo = [
                (kind, b)
                for kind in hops
                for b in {"c": [1], "x": [2 * b for b in chip_bits], "z": z_bits, "g": z_bits}[kind]
            ]
            self.send()

        def send(self):
            kind, b = self.todo[0]
            axis, n = ("ctx", n_ctx) if kind in "cx" else ("fsdp", n_z)
            self.got = swap(self.x, axis, b, n)

        def step(self):
            if not self.todo:
                return
            kind, _ = self.todo.pop(0)
            if kind == "g":
                self.x = join([self.x, self.got], 1)
            else:
                m = self.x.shape
                self.x = launch(
                    add_body,
                    one,
                    (1,),
                    [spec(m)] * 2,
                    spec(m),
                    jax.ShapeDtypeStruct(m, F32),
                    us=0.5,
                )(self.x, self.got)
            if self.todo:
                self.send()

        def finish(self):
            while self.todo:
                self.step()
            return self.x

    orders = (chip_bits, chip_bits[::-1])

    def kept(order):
        ks = [0]
        for b in reversed(order[1:]):
            ks = ks + [k ^ b for k in ks]
        return ks

    late = [(k, h) for h in range(2) for k in kept(orders[h])]
    early = [(k ^ orders[h][0], h) for k, h in late]
    groups = (early, late, early + late)

    def send_first(tiles):
        return [chip_swap(tiles[h], orders[h][0]) for h in range(2)]

    def send_next(keep, got, step):
        n, m, cols = keep[0].shape

        def add(first):
            some = spec((1, m, cols), lambda i, sc: (i + first, 0, 0))
            part = spec((1, m, cols), lambda i, sc: (i, 0, 0))
            return launch(
                step_body,
                one,
                (n // 2,),
                [some] * 4,
                [part] * 2,
                [jax.ShapeDtypeStruct((n // 2, m, cols), BF)] * 2,
                us=n * m * cols * 4e-6,
            )(keep[0], got[0], keep[1], got[1])

        left = add(n // 2)
        sent = [chip_swap(left[h], orders[h][step]) for h in range(2)]
        return add(0), sent

    def finish_reduce(keep, got, step):
        while keep[0].shape[0] > 1:
            keep, got = send_next(keep, got, step)
            step += 1
        return [v[0] for h in range(2) for v in (keep[h], got[h])]

    def rel(x):
        return jnp.take(x, f ^ jnp.arange(n_z, dtype=jnp.int32), axis=0)

    x_loc = inputs[0].astype(F32)
    ends = jnp.cumsum(doc_lengths, axis=1)
    my_pos = c * tok + jnp.arange(tok, dtype=jnp.int32)
    my_ends = lax.dynamic_slice_in_dim(ends, f, 1, 0)
    my_keep = (my_pos < my_ends[0, DOCS - 1]).astype(F32)[:, None]
    inv1_loc = lax.rsqrt(jnp.mean(x_loc * x_loc, axis=1, keepdims=True) + norm_eps)
    n1_loc = x_loc * inv1_loc
    dy_loc = cotangent[0].astype(F32) * my_keep
    payload = jnp.stack((n1_loc.astype(BF), dy_loc.astype(BF), inputs[0]), axis=1)
    payload = payload.reshape(tok, 3, n_ctx, dc).transpose(2, 0, 1, 3).reshape(n_ctx, tok, 3 * dc)
    def split_halves(w):
        mine = lax.dynamic_slice_in_dim(w, core * width, width, 2)
        theirs = lax.dynamic_slice_in_dim(w, (1 - core) * width, width, 2)
        return mine, theirs, core_swap(theirs)

    def e_major(w):
        return jnp.transpose(w.astype(BF), (1, 0, 2))

    payload = lax.all_to_all(payload, "ctx", 0, 0, tiled=True).reshape(seq, 3 * dc)
    qk_weight = jnp.concatenate((e_major(query_weight), e_major(kv_weight)), axis=0)
    routes = jnp.concatenate((att_routes, ffn_routes), axis=2)[None]
    for b in [1] + [2 * v for v in chip_bits]:
        routes = jnp.concatenate((routes, swap(routes, "ctx", b, n_ctx)), axis=0)
    routes = jnp.take(routes, c ^ jnp.arange(n_ctx, dtype=jnp.int32), axis=0).reshape(seq, n_z, 4)
    small = jnp.concatenate((att_gain[None], ffn_gain[None]), axis=0).astype(BF)
    small_t = core_swap(small).astype(F32)
    small = small.astype(F32)
    wqk_m, wqk_t, wqk_x = split_halves(qk_weight)
    n1_own, dy_own, x_own = payload[:, :dc], payload[:, dc : 2 * dc], payload[:, 2 * dc :]

    routes = rel(jnp.transpose(routes, (1, 0, 2))).reshape(rows, 4)
    route_row = jnp.transpose(routes)
    att_route3 = routes[:, :2].reshape(n_z, seq, 2)
    experts = jnp.arange(E_F, dtype=jnp.int32)

    ga, gf, ga_t, gf_t = small[0:1], small[1:2], small_t[0:1], small_t[1:2]
    ra, rf = att_router.astype(BF), ffn_router.astype(BF)

    def row_logits(router, hidden):
        return lax.dot_general(router, hidden, (((0,), (1,)), ((), ())), preferred_element_type=F32)

    def gates_of(logits, route2):
        picked = jnp.sum(jnp.where(route2[:, None, :] == experts[None, :, None], logits[None], 0.0), axis=1)
        return jax.nn.softmax(picked, axis=0)

    la = Small(row_logits(ra, (n1_own.astype(F32) * ga).astype(BF)), "cxg")
    step = 32

    def first_window(n1_own, dy_own, gate_up_weight):
        n1 = z_gather(n1_own)
        dy_got = z_swap(dy_own, z_bits[0])
        wg = launch(
            functools.partial(prep_gate_up_body, fl),
            jnp.zeros((1,), jnp.int32),
            (dc // step,),
            [spec((step, E_F, 2, fl_real), lambda i, sc: (i, 0, 0, 0))],
            spec((E_F, step, 2 * fl), lambda i, sc: (0, i, 0)),
            jax.ShapeDtypeStruct((E_F, dc, 2 * fl), BF),
            us=26,
        )(gate_up_weight)
        n1, h1 = join_scaled(n1, ga)
        return n1, h1, join([dy_own, dy_got], 0), wg

    mark(routes)
    n1, h1, dy, wg = window(first_window, n1_own, dy_own, gate_up_weight)
    n1_t = core_swap(n1)
    wg_x = core_swap(wg)
    h1_x = (n1_t.astype(F32) * ga_t).astype(BF)
    def project(xo, xt, weights, n_extra, g):
        cols = (2 + n_extra) * width
        group = groups[g]
        n = len(group)
        at = lambda i, sc: (sc[i], 0)
        return launch(
            functools.partial(proj_body, n_extra, width, n),
            jnp.stack([2 * (chip ^ k) + h for k, h in group]),
            (n,),
            [spec((half, 4), at), spec((half, dc), at), spec((half, dc), at)] + [spec(w.shape) for w in weights],
            [spec((n // 2, half, cols))] * 2,
            [jax.ShapeDtypeStruct((n // 2, half, cols), BF)] * 2,
            [pltpu.VMEM((half, cols), BF)],
            us=8 if n_extra else 7,
        )(routes, xo, xt, *weights)

    def prep_down():
        return launch(
            functools.partial(prep_down_body, fl),
            jnp.zeros((1,), jnp.int32),
            (dc // step,),
            [spec((step, E_F, fl_real), lambda i, sc: (i, 0, 0))],
            spec((E_F, step, fl), lambda i, sc: (0, i, 0)),
            jax.ShapeDtypeStruct((E_F, dc, fl), BF),
                us=9.5,
        )(down_weight)

    tiles = project(h1, h1_x, (wqk_m, wqk_x), 2, 0)
    def start_of(k, other, h):
        return 2 * ts * (2 * (chip ^ k) + (core ^ other)) + h * ts

    def tile_scalars(table, offsets):
        ks, others, hs = (jnp.array([[t[i] for t in row] for row in table], jnp.int32) for i in range(3))
        p0 = start_of(ks, others, hs)
        n = p0.shape[1]
        first = jnp.sum((offsets[1:] <= p0[..., None]).astype(jnp.int32), axis=2)
        last = jnp.sum((offsets[1:] <= p0[..., None] + ts - 1).astype(jnp.int32), axis=2)
        count = last - first + 1
        lower = jnp.arange(n)[:, None] >= jnp.arange(n)[None, :]
        upto = jnp.sum(jnp.where(lower, count[:, None, :], 0), axis=2)
        v = jnp.arange(n + E_F - 1, dtype=jnp.int32)
        tile = jnp.minimum(jnp.sum((upto[:, None, :] <= v[:, None]).astype(jnp.int32), axis=2), n - 1)
        mine = tile[:, :, None] == jnp.arange(n)
        begin_v = jnp.sum(jnp.where(mine, (upto - count)[:, None, :], 0), axis=2)
        first_v = jnp.sum(jnp.where(mine, first[:, None, :], 0), axis=2)
        last_v = jnp.sum(jnp.where(mine, last[:, None, :], 0), axis=2)
        e = jnp.minimum(first_v + v - begin_v, last_v)
        kind = jnp.where(v < upto[:, -1:], jnp.where(v == begin_v, 2, 1), 0)
        ends = jnp.broadcast_to(offsets, (len(table), E_F + 1))
        return jnp.concatenate((p0, tile, e, kind, ends), axis=1).astype(jnp.int32)

    near = list(chip_bits)
    far = [k for k in range(1, n_chip) if k not in near]
    back_groups = ([0], near, far)
    back_table = [[(k, other, h) for other in range(2) for h in range(2)] for k in range(n_chip)]
    n_pieces = 4 * n_chip
    def places():
        hot = (route_row[2:4, None, :] == experts[None, :, None]).astype(F32)
        blocks = rows // 128
        hot_b = hot.reshape(2 * E_F, blocks, 128)
        lane = jnp.arange(128)
        tri = (lane[:, None] < lane[None, :]).astype(BF)
        before = jnp.einsum("anl,lm->anm", hot_b.astype(BF), tri, preferred_element_type=F32)
        totals = jnp.sum(hot_b, axis=2)
        lane_b = jnp.arange(blocks)
        tri_b = (lane_b[:, None] < lane_b[None, :]).astype(BF)
        before_b = jnp.dot(totals.astype(BF), tri_b, preferred_element_type=F32)
        rank = (before + before_b[:, :, None]).reshape(2, E_F, rows)
        counts = jnp.sum(totals, axis=1).reshape(2, E_F)
        per_expert = counts[0] + counts[1]
        off = jnp.sum(jnp.where(experts[:, None] > experts[None, :], per_expert[None, :], 0.0), axis=1)
        base = jnp.stack((off, off + counts[0]))
        pos_row = jnp.sum(hot * (base[:, :, None] + rank), axis=1).astype(jnp.int32)
        pos_col = jnp.transpose(pos_row)
        offsets = jnp.concatenate((off, jnp.sum(per_expert)[None])).astype(jnp.int32)
        proj_scalars = tile_scalars([[(k, 0, h) for k, h in group] for group in groups[:2]], offsets)
        all_scalars = tile_scalars([[(k, 0, h) for k, h in groups[2]]], offsets).reshape(-1)
        starts_all = start_of(*(jnp.array([t[i] for row in back_table for t in row], jnp.int32) for i in range(3)))
        weight_scalars = jnp.concatenate((starts_all, offsets))
        back_scalars = [
            tile_scalars([[t for k in ks for t in back_table[k]]], offsets).reshape(-1) for ks in back_groups
        ]
        return pos_row, pos_col, proj_scalars.reshape(-1), all_scalars, back_scalars, starts_all, weight_scalars

    n_tile = len(groups[0])
    proj_length = 4 * n_tile + 3 * (E_F - 1) + E_F + 1

    def group_proj(xo, xt, wm, wx, g):
        m = wm.shape[2]
        n = len(groups[g])
        steps = n + E_F - 1
        lo = g * proj_length if g < 2 else 0
        parts = 2 if g < 2 else 4
        by_expert = spec((1, dc, m), lambda i, sc: (sc[lo + n + steps + i], 0, 0))
        return launch(
            functools.partial(group_proj_body, n, parts, lo),
            proj_scalars if g < 2 else all_scalars,
            (steps,),
            [spec((2, rows)), spec((rows, dc)), spec((rows, dc)), by_expert, by_expert],
            [spec((n // parts, ts, m))] * parts,
            [jax.ShapeDtypeStruct((n // parts, ts, m), BF)] * parts,
            [pltpu.VMEM((ts, 2 * dc), BF)],
            us=17 if m > fl else 27,
        )(pos_row, xo, xt, wm, wx)

    def sort_t(x):
        return launch(
            sort_t_body,
            starts_all,
            (n_pieces,),
            [spec((2, rows)), spec((rows, dc))],
            spec((dc, ts), lambda i, sc: (0, i)),
            jax.ShapeDtypeStruct((dc, 2 * rows), BF),
            us=13,
        )(pos_row, x)

    def query_window(tiles, dy):
        sent = send_first(tiles)
        for b in z_bits[1:-1]:
            dy = join([dy, z_swap(dy, b)], 0)
        dy_got = z_swap(dy, z_bits[-1])
        keep = project(h1, h1_x, (wqk_m, wqk_x), 2, 1)
        wd = prep_down()
        return sent, keep, wd, dy, dy_got

    def sum_window(sent, keep, wd, dy, dy_got):
        if keep[0].shape[0] > 1:
            keep, sent = send_next(keep, sent, 1)
        dy = join([dy, dy_got], 0)
        wd_x, dy_x = core_swap(wd), core_swap(dy)
        return finish_reduce(keep, sent, 2), dy, dy_x, wd_x, places()

    la.step()
    sent, keep, wd, dy, dy_got = window(query_window, tiles, dy)
    la.step()
    qkv_parts, dy_all, dy_x, wd_x, at_places = window(sum_window, sent, keep, wd, dy, dy_got)
    pos_row, pos_col, proj_scalars, all_scalars, back_scalars, starts_all, weight_scalars = at_places
    la.step()

    s_abs = f ^ chip
    positions = jnp.arange(seq, dtype=jnp.int32)
    my_ends = lax.dynamic_index_in_dim(ends, s_abs, 0, keepdims=False)
    my_starts = my_ends - lax.dynamic_index_in_dim(doc_lengths, s_abs, 0, keepdims=False)
    doc_one = jnp.sum((positions[:, None] >= my_ends).astype(jnp.int32), axis=1)
    begin = jnp.sum(jnp.where(doc_one[:, None] == jnp.arange(DOCS, dtype=jnp.int32), my_starts, 0), axis=1)
    doc_col, doc_row = doc_one[:, None], doc_one[None, :]
    halves = jnp.arange(HD // 2, dtype=F32)
    angles = (positions - begin).astype(F32)[:, None] * (rope_base ** (-2.0 * halves / HD))[None, :]
    cos, sin = jnp.cos(angles), jnp.sin(angles)
    cosf = jnp.concatenate((cos, cos), axis=1)
    sinf = jnp.concatenate((-sin, sin), axis=1)

    qkv, ao, lse = launch(
        functools.partial(attend_body, hc),
        one,
        (1,),
        [spec((half, 4 * width))] * 4 + [spec((seq, 1)), spec((1, seq)), spec((seq, HD)), spec((seq, HD))],
        [spec((seq, 4 * width)), spec((seq, 2 * width)), spec((seq, 128))],
        [
            jax.ShapeDtypeStruct((seq, 4 * width), BF),
            jax.ShapeDtypeStruct((seq, 2 * width), BF),
            jax.ShapeDtypeStruct((seq, 128), F32),
        ],
            us=7,
    )(*qkv_parts, doc_col, doc_row, cosf, sinf)

    ao_m = [ao] + [chip_swap(ao, k) for k in range(1, n_chip)]
    ao_t = [core_swap(ao)]
    wo_m, wo_t, wo_x = split_halves(e_major(output_weight))
    la.step()
    da_all = group_proj(dy_all, dy_x, wd, wd_x, 2)
    da_tiles, da_keep = da_all[:2], da_all[2:]
    ao_m = [ao] + hold(*ao_m[1:])
    ao_t += [core_swap(v) for v in ao_m[1:]]
    pa = gates_of(la.finish(), route_row[0:2])
    pa3 = jnp.transpose(pa).reshape(n_z, seq, 2)

    def into_stream(body, k, streams, vals, weights, buf, us, cols, carry=()):
        sc = jnp.reshape(chip ^ k, (1,))
        by_stream = [spec((pl.squeezed, seq, 2), lambda i, sc: (sc[0], 0, 0))] * len(streams)
        n_in = len(streams) + 2 + len(weights)
        return launch(
            body,
            sc,
            (1,),
            by_stream
            + [spec((seq, cols))] * 2
            + [spec(w.shape) for w in weights]
            + [pl.BlockSpec(memory_space=pl.ANY)],
            spec((1, seq, dc), lambda i, sc: (sc[0], 0, 0)),
            jax.ShapeDtypeStruct((n_z, seq, dc), BF),
            aliases={n_in + 1: 0},
            us=us,
        )(*streams, *vals, *weights, buf, carry=carry)

    buf = jnp.zeros((n_z, seq, dc), BF)
    for k in range(n_chip):
        buf = into_stream(
            functools.partial(att_out_body, width),
            k,
            (att_route3, pa3),
            (ao_m[k], ao_t[k]),
            (wo_m, wo_t),
            buf,
            4.3,
            2 * width,
            da_tiles if k == n_chip - 1 else (),
        )
    buf, *da_tiles = buf
    y1_sent = z_send([buf[k] for k in range(n_z)])
    da_sent = send_first(da_tiles)
    y1, y1_own = z_total(y1_sent, x_own)

    y1_got = z_gather(y1_own)
    y1_f = y1_own.astype(F32)
    stat = jnp.concatenate(
        (
            row_logits(rf, (y1_f * gf).astype(BF)),
            jnp.sum(y1_f * y1_f, axis=1)[None],
            jnp.zeros((7, seq), F32),
        ),
        axis=0,
    )
    stat = Small(stat, "cxg")
    if da_keep[0].shape[0] > 1:
        da_keep, da_sent = send_next(da_keep, da_sent, 1)
    for _ in range(1 + len(chip_bits)):
        stat.step()
    y1_low, yg = join_scaled(y1_got, gf)
    yg_x = (core_swap(y1_low).astype(F32) * gf_t).astype(BF)

    gu_tiles = group_proj(yg, yg_x, wg, wg_x, 0)
    gu_sent = send_first(gu_tiles)
    da_parts = finish_reduce(da_keep, da_sent, 2)
    da_parts = launch(
        pairs_body,
        one,
        (1,),
        [spec((ts, fl))] * 4,
        [spec((ts, fl))] * 2,
        [jax.ShapeDtypeStruct((ts, fl), BF)] * 2,
        us=3,
    )(*da_parts)
    gu_keep = group_proj(yg, yg_x, wg, wg_x, 1)
    stat.step()
    yg_s = sort_t(yg)
    dy_s = sort_t(dy_all)
    if gu_keep[0].shape[0] > 1:
        gu_keep, gu_sent = send_next(gu_keep, gu_sent, 1)
    stat = stat.finish()
    inv2 = lax.rsqrt(stat[8:9] / D + norm_eps)
    lf = stat[0:E_F] * inv2
    pf = gates_of(lf, route_row[2:4])
    rowv = jnp.concatenate((inv2, pf, jnp.zeros((5, rows), F32)), axis=0)
    gu_parts = finish_reduce(gu_keep, gu_sent, 2)

    by_half = lambda n: spec((1, ts, n), lambda h, sc: (h, 0, 0))
    dgu, act, tok_sum = launch(
        functools.partial(middle_body, fl),
        jnp.stack([start_of(0, 0, h) for h in range(2)]),
        (2,),
        [spec((2, rows)), spec((8, rows))] + [spec((ts, 2 * fl))] * 4 + [spec((ts, fl))] * 2,
        [by_half(2 * fl), by_half(fl), spec((8, rows))],
        [
            jax.ShapeDtypeStruct((2, ts, 2 * fl), BF),
            jax.ShapeDtypeStruct((2, ts, fl), BF),
            jax.ShapeDtypeStruct((8, rows), F32),
        ],
            us=13,
    )(pos_row, rowv, *gu_parts, *da_parts)

    def router_back(dgate, gates, route2):
        dlog = gates * (dgate - jnp.sum(gates * dgate, axis=0, keepdims=True))
        return jnp.sum(jnp.where(route2[:, None, :] == experts[None, :, None], dlog[:, None, :], 0.0), axis=0)


    def gather_near(own):
        return {0: own} | {b: chip_swap(own, b) for b in near}

    def gather_far(got):
        result = {}
        for h in range(2):
            have = {k: got[k][h] for k in got}
            seen = orders[h][0]
            for b in orders[h][1:]:
                for k in [k for k in list(have) if k and not k & ~seen]:
                    have[k ^ b] = result[k ^ b, h] = chip_swap(have[k], b)
                seen |= b
        return result

    def whole(v):
        w = core_swap(v)
        return [(v, 0), (v, 1), (w, 0), (w, 1)]

    def apart(got, k):
        mine = [got[k, h] for h in range(2)]
        return [(v, None) for v in mine] + [(core_swap(v), None) for v in mine]

    def arrays_of(pieces):
        arrays, where = [], []
        for v, h in pieces:
            i = next((i for i, u in enumerate(arrays) if u is v), None)
            if i is None:
                i = len(arrays)
                arrays.append(v)
            where.append((i, h))
        return arrays, tuple(where)


    def group_back(g, pieces, w, acc, carry=()):
        m = w.shape[2]
        arrays, where = arrays_of([v for k in back_groups[g] for v in pieces[k]])
        n = len(where)
        steps = n + E_F - 1
        return launch(
            functools.partial(group_back_body, where, 0),
            back_scalars[g],
            (steps,),
            [spec((rows, 2))]
            + [spec(v.shape) for v in arrays]
            + [spec((1, dc, m), lambda i, sc: (sc[n + steps + i], 0, 0)), spec((rows, dc))],
            spec((rows, dc)),
            jax.ShapeDtypeStruct((rows, dc), F32),
            [pltpu.VMEM((n * ts, dc), F32)],
            aliases={3 + len(arrays): 0},
            us=3.4 * n if m > fl else 2.8 * n,
        )(pos_col, *arrays, w, acc, carry=carry)

    def group_weight(xs, pieces, out, out_spec):
        arrays, where = arrays_of([v for k in range(n_chip) for v in pieces[k]])
        m = arrays[0].shape[-1]
        return launch(
            functools.partial(group_weight_body, where, fl),
            weight_scalars,
            (E_F,),
            [spec((dc, 2 * rows))] + [spec(v.shape) for v in arrays],
            out_spec,
            out,
            [pltpu.VMEM((dc, m), F32)],
            us=30 if m > fl else 0.1,
        )(xs, *arrays)

    dgu_pieces = {0: whole(dgu)}
    act_x = core_swap(act)
    dgu_got = gather_near(dgu)

    tok_sum = Small(rel(tok_sum.reshape(8, n_z, seq).transpose(1, 0, 2)[:, :3]).reshape(n_z * 3, seq), "czx")
    tok_sum.step()
    dh2 = group_back(0, dgu_pieces, wg, jnp.zeros((rows, dc), F32))
    act_pieces = {0: [(act, 0), (act, 1), (act_x, 0), (act_x, 1)]}
    tok_sum.step()
    ffn = group_back(0, act_pieces, wd, jnp.zeros((rows, dc), F32))
    tok_sum.step()
    got = hold(*[dgu_got[b] for b in near])
    dgu_far = gather_far(dict(zip(near, got)))
    for b, v in zip(near, got):
        dgu_pieces[b] = whole(v)
    dh2, act = group_back(1, dgu_pieces, wg, dh2, carry=(act,))
    act_pieces[0] = [(act, 0), (act, 1), (act_x, 0), (act_x, 1)]
    tok_sum.step()
    dgu_far = dict(zip(dgu_far, hold(*dgu_far.values())))
    for k in far:
        dgu_pieces[k] = apart(dgu_far, k)
    act_got = gather_near(act)
    dh2 = group_back(2, dgu_pieces, wg, dh2)
    def first_back_window(dh2):
        sent = z_send([dh2[k * seq : (k + 1) * seq].astype(BF) for k in range(n_z)])
        gate_up_grad = group_weight(
            yg_s,
            dgu_pieces,
            jax.ShapeDtypeStruct((dc, E_F, 2, fl_real), F32),
            spec((dc, 1, 2, fl_real), lambda e, sc: (0, e, 0, 0)),
        )
        return z_total(sent)[1], gate_up_grad

    dh2, gate_up_grad = window(first_back_window, dh2)
    act_got = hold(*[act_got[b] for b in near])
    for b, v in zip(near, act_got):
        act_pieces[b] = whole(v)
    act_far = gather_far(dict(zip(near, act_got)))

    def second_back_window(dh2, ffn):
        got = z_gather(dh2)
        return group_back(1, act_pieces, wd, ffn), got

    ffn, dh2_got = window(second_back_window, dh2, ffn)
    tok_sum = rel(tok_sum.finish().reshape(n_z, 3, seq)).transpose(1, 0, 2).reshape(3, rows)
    dlf = router_back(tok_sum[0:2], pf, route_row[2:4])
    m2 = (tok_sum[2:3] + jnp.sum(dlf * lf, axis=0, keepdims=True)) / D
    dlf_inv = (dlf * inv2).astype(BF)
    by_row = lambda n: spec((seq, n), lambda i, sc: (i, 0))
    dy1_low, dh2_own = launch(
        functools.partial(middle_grad_body, n_z),
        jnp.zeros((1,), jnp.int32),
        (n_z,),
        [by_row(dc), by_row(dc), spec((E_F, seq), lambda i, sc: (0, i)), by_row(1), spec((E_F, dc)), spec((1, dc))]
        + [spec((seq, dc))] * n_z,
        [by_row(dc), spec((seq, dc))],
        [jax.ShapeDtypeStruct((rows, dc), BF), jax.ShapeDtypeStruct((seq, dc), F32)],
        us=4,
    )(dy_all, y1_low, dlf_inv, jnp.transpose(m2 * inv2 * inv2), jnp.transpose(rf), gf, *dh2_got)
    dy1_x = core_swap(dy1_low)

    tiles = project(dy1_low, dy1_x, (wo_m, wo_x), 0, 0)
    sent, keep = window(
        lambda tiles: (send_first(tiles), project(dy1_low, dy1_x, (wo_m, wo_x), 0, 1)), tiles
    )
    if keep[0].shape[0] > 1:
        keep, sent = send_next(keep, sent, 1)

    def att_weight(xt, with_gates, extra, mine, theirs, cols):
        pieces = [v for pair in zip(mine, theirs) for v in pair]
        sc = jnp.concatenate((chip ^ jnp.arange(n_chip, dtype=jnp.int32), core[None]))
        at = lambda i, e, sc: (0, 0, sc[n_chip] ^ i)
        outs = [E_A] + ([2] if extra else [])
        return launch(
            functools.partial(att_weight_body, width, n_chip, with_gates, extra),
            sc,
            (2, E_A),
            [spec(xt.shape), spec((n_z, seq, 2)), spec((n_z, seq, 2))] + [spec((seq, cols))] * len(pieces),
            [spec((dc, n, width), at) for n in outs],
            [jax.ShapeDtypeStruct((dc, n, 2 * width), F32) for n in outs],
            [pltpu.VMEM((n_chip, seq, 2 * width), BF)],
            us=20,
        )(xt, att_route3, pa3, *pieces)

    def stream_t(v):
        return jnp.transpose(v.reshape(n_z, seq, dc), (0, 2, 1))

    act_far = dict(zip(act_far, hold(*act_far.values())))
    for k in far:
        act_pieces[k] = apart(act_far, k)
    ffn = group_back(2, act_pieces, wd, ffn)
    dao_parts = finish_reduce(keep, sent, 2)

    pa_one = lax.dynamic_index_in_dim(pa3, chip, 0, keepdims=False)
    grads, dgate = launch(
        functools.partial(attend_back_body, hc),
        one,
        (1,),
        [spec((half, 2 * width))] * 4
        + [spec((seq, 4 * width)), spec((seq, 2 * width)), spec((seq, 128)), spec((seq, 2))]
        + [spec((seq, 1)), spec((1, seq)), spec((seq, HD)), spec((seq, HD))],
        [spec((seq, 4 * width)), spec((seq, 128))],
        [jax.ShapeDtypeStruct((seq, 4 * width), BF), jax.ShapeDtypeStruct((seq, 128), F32)],
            us=7,
    )(*dao_parts, qkv, ao, lse, pa_one, doc_col, doc_row, cosf, sinf)
    dpa = jnp.zeros((n_z, 2, seq), F32)
    dpa = lax.dynamic_update_slice(dpa, jnp.transpose(dgate[:, :2])[None], (s_abs, 0, 0))
    dpa = Small(dpa.reshape(n_z * 2, seq), "czx")
    def grads_window(grads, ffn):
        got = [chip_swap(grads, k) for k in range(1, n_chip)]
        own = core_swap(grads)
        ffn_sent = z_swap(ffn[rows // 2 :], z_bits[-1])
        down_grad = group_weight(
            dy_s,
            act_pieces,
            jax.ShapeDtypeStruct((dc, E_F, fl_real), F32),
            spec((dc, E_F, fl_real)),
        )
        return got, own, ffn_sent, down_grad

    ffn = ffn.astype(BF)
    g_m, own_t, ffn_sent, down_grad = window(grads_window, grads, ffn)
    g_m, g_t = [grads, *g_m], [own_t]
    dpa.step()
    g_t += [core_swap(v) for v in g_m[1:]]

    def to_rows(v):
        n = v.shape[1] // dc
        v = lax.all_to_all(v.reshape(n_ctx, tok, n * dc), "ctx", 0, 0, tiled=True)
        v = v.reshape(n_ctx, tok, n, dc).transpose(2, 1, 0, 3)
        return v.reshape(n, tok, D)

    buf = jnp.zeros((n_z, seq, dc), BF)
    for k in range(n_chip):
        buf = into_stream(
            functools.partial(att_in_back_body, width),
            k,
            (att_route3,),
            (g_m[k], g_t[k]),
            (wqk_m, wqk_t),
            buf,
            5,
            4 * width,
        )
        dpa.step()
        if k == 0:
            for b in z_bits[-2::-1]:
                n = ffn_sent.shape[0] // 2
                both = [spec((n, dc), lambda i, sc: (i, 0))] * 2
                ffn, _ = launch(
                    functools.partial(total_body, 2),
                    one,
                    (2,),
                    both,
                    both,
                    [jax.ShapeDtypeStruct((2 * n, dc), F32), jax.ShapeDtypeStruct((2 * n, dc), BF)],
                    us=2,
                )(ffn, ffn_sent)[::-1]
                ffn_sent = z_swap(ffn[n:], b)
    dpa = lax.dynamic_index_in_dim(dpa.finish().reshape(n_z, 2, seq), f, 0, keepdims=False)
    ffn = z_total([ffn[:seq], ffn_sent], y1)[1]

    def last_window(buf):
        sent = z_send([buf[k] for k in range(n_z)])
        query_grad, kv_grad = att_weight(stream_t(h1), False, True, g_m, g_t, 4 * width)
        return z_total(sent)[0], query_grad, kv_grad

    dh1, query_grad, kv_grad = window(last_window, buf)
    dla = router_back(dpa, pa[:, :seq], route_row[0:2, :seq]).astype(BF)
    dh1 = dh1 + lax.dot_general(dla, ra, (((0,), (1,)), ((), ())), preferred_element_type=F32)
    back_col = jnp.concatenate(((dh1 * ga).astype(BF), dy1_low[:seq]), axis=1)

    back = to_rows(jnp.concatenate((back_col, ffn), axis=1))
    outputs, back = back[2:], back[:2].astype(F32)
    input_grad = back[1] + inv1_loc * (back[0] - n1_loc * jnp.mean(back[0] * n1_loc, axis=1, keepdims=True))
    input_grad = input_grad.astype(BF)[None]

    mark(back_col)
    (output_grad,) = att_weight(stream_t(dy1_low), True, False, ao_m, ao_t, 2 * width)

    own = slice(0, seq)
    tail = jnp.concatenate(
        (
            jnp.dot(dla, h1[own], preferred_element_type=F32),
            jnp.dot(dlf_inv[:, own], yg[own], preferred_element_type=F32),
            jnp.sum(dh1 * n1_own.astype(F32), axis=0, keepdims=True),
            jnp.sum(dh2_own * y1_f, axis=0, keepdims=True),
            jnp.zeros((6, dc), F32),
        ),
        axis=0,
    )
    tail = Small(tail, "z").finish()
    att_router_grad = jnp.transpose(tail[0:E_A])
    ffn_router_grad = jnp.transpose(tail[E_A : E_A + E_F])
    att_gain_grad = tail[E_A + E_F]
    ffn_gain_grad = tail[E_A + E_F + 1]

    return (
        outputs,
        input_grad,
        kv_grad,
        query_grad,
        output_grad,
        att_router_grad,
        att_gain_grad,
        gate_up_grad,
        down_grad,
        ffn_router_grad,
        ffn_gain_grad,
    )


def solution(mesh):
    in_specs = (
        P("fsdp", "ctx", None),
        P("fsdp", "ctx", None),
        P(),
        P("ctx", None, None),
        P("ctx", None, None),
        P("ctx", None, "fsdp"),
        P("ctx", None, "fsdp"),
        P("ctx", None, "fsdp"),
        P("ctx", None),
        P("ctx"),
        P("ctx", None, None, "fsdp"),
        P("ctx", None, "fsdp"),
        P("ctx", None),
        P("ctx"),
    )
    out_specs = (
        P("fsdp", "ctx", None),
        P("fsdp", "ctx", None),
        P("ctx", None, "fsdp"),
        P("ctx", None, "fsdp"),
        P("ctx", None, "fsdp"),
        P("ctx", None),
        P("ctx"),
        P("ctx", None, None, "fsdp"),
        P("ctx", None, "fsdp"),
        P("ctx", None),
        P("ctx"),
    )
    return jax.shard_map(
        per_device, mesh=mesh, in_specs=in_specs, out_specs=out_specs, check_vma=False
    )
```
